32 devices in a mesh: dp: 4 (over y, x), seq: 8 (over z, core).
Axes of the slice: x: 2, y: 2, z: 4, core: 2. Of those that a mesh axis runs over, the one named last changes fastest.
Arguments:
- tokens: bfloat16 [4, 2048, 2048], P('dp', 'seq'), may hold values from -6 to 6
- doc_reset: int32 [4, 2048], P('dp', 'seq'), may hold values from 0 to 1, as said below
- cotangent: bfloat16 [4, 2048, 2048], P('dp', 'seq'), may hold values from -6 to 6
- norm_gain: bfloat16 [2048], P(('dp', 'seq')), may hold values from 0.5 to 1.5
- input_proj: bfloat16 [2048, 2560], P(('dp', 'seq')), may hold values from -0.125 to 0.125
- branch_proj: bfloat16 [2048, 2560], P(('dp', 'seq')), may hold values from -0.125 to 0.125
- conv_kernel: bfloat16 [4, 2560], P(None, ('dp', 'seq')), may hold values from -3 to 3
- conv_bias: bfloat16 [2560], P(('dp', 'seq')), may hold values from -3 to 3
- gate_weight: bfloat16 [2, 2560, 256], P(None, ('dp', 'seq')), may hold values from -0.375 to 0.375
- gate_bias: bfloat16 [2, 2560], P(None, ('dp', 'seq')), may hold values from -4 to 4
- decay_param: bfloat16 [2560], P(('dp', 'seq')), may hold values from 4 to 10
- output_proj: bfloat16 [2560, 2048], P(None, ('dp', 'seq')), may hold values from -0.25 to 0.25
- ffn_gain: bfloat16 [2048], P(('dp', 'seq')), may hold values from 0.5 to 1.5
- ffn_gate: bfloat16 [2048, 6144], P(('dp', 'seq')), may hold values from -0.125 to 0.125
- ffn_up: bfloat16 [2048, 6144], P(('dp', 'seq')), may hold values from -0.125 to 0.125
- ffn_down: bfloat16 [6144, 2048], P(('dp', 'seq')), may hold values from -0.109375 to 0.109375
Outputs:
- layer_out: float32 [4, 2048, 2048], P('dp', 'seq')
- input_grad: float32 [4, 2048, 2048], P('dp', 'seq')
- gain_grad: float32 [2048], P(('dp', 'seq'))
- input_proj_grad: float32 [2048, 2560], P(('dp', 'seq'))
- branch_proj_grad: float32 [2048, 2560], P(('dp', 'seq'))
- kernel_grad: float32 [4, 2560], P(None, ('dp', 'seq'))
- conv_bias_grad: float32 [2560], P(('dp', 'seq'))
- gate_weight_grad: float32 [2, 2560, 256], P(None, ('dp', 'seq'))
- gate_bias_grad: float32 [2, 2560], P(None, ('dp', 'seq'))
- decay_grad: float32 [2560], P(('dp', 'seq'))
- output_proj_grad: float32 [2560, 2048], P(None, ('dp', 'seq'))
- ffn_gain_grad: float32 [2048], P(('dp', 'seq'))
- ffn_gate_grad: float32 [2048, 6144], P(('dp', 'seq'))
- ffn_up_grad: float32 [2048, 6144], P(('dp', 'seq'))
- ffn_down_grad: float32 [6144, 2048], P(('dp', 'seq'))
The draws below stay inside these ranges and needn't reach their ends.
Inputs may be any that keep to these rules, and one draw needn't show every extreme that they name: `doc_reset`: every sequence's first position is 1.
All inputs are finite; a program needn't handle non-finite values.
Results may differ from the reference program's by a relative error of at most 0.0095.
Values may be sent and summed in bfloat16 or wider, within the bound.
No kernel may reach another device: no remote copies, remote signals or barrier semaphores. Data moves between devices by JAX's collectives and lax.ppermute only.
A program may use at most 448 MiB of HBM per device.

```python
import math
import jax
import jax.numpy as jnp
from jax import lax

D = 2048
BLOCKS = 10
BW = 256
FF = 6144
CONV = 4
REC = 2560
SEQS = 1
LENGTH = 2048
STRETCH = 256
BATCH = 4


def draw_doc_reset(key, part):
    key = jax.random.fold_in(key, 11)
    key_scatter, key_pick = jax.random.split(key)
    scattered = (jax.random.randint(key_scatter, (BATCH, LENGTH), 0, LENGTH) < 8).astype(jnp.int32)
    picked = jax.random.randint(key_pick, (BATCH // SEQS,), 0, SEQS)
    row_ids = jnp.arange(BATCH)
    chosen = picked[row_ids // SEQS] == row_ids % SEQS
    places = jnp.arange(LENGTH)
    edges = (places < STRETCH) | (places >= LENGTH - STRETCH)
    cleared = jnp.where(chosen[:, None] & jnp.logical_not(edges)[None, :], 0, scattered)
    first_place = (places == 0).astype(jnp.int32)
    return jnp.maximum(cleared, first_place[None, :]).astype(jnp.int32)


def draw_decay_param(key, part):
    key = jax.random.fold_in(key, 23)
    values = jax.random.uniform(key, (REC,), jnp.float32, 4.0, 10.0)
    return values.astype(jnp.bfloat16)


def spiked(entries, own_key, source, target, blocks, factor):
    owner, partner = [(jnp.arange(entries.shape[position]) // (entries.shape[position] // blocks)).reshape([-1 if axis == position else 1 for axis in range(entries.ndim)]) for position in (source, target)]
    chosen = jax.random.permutation(own_key, blocks)[partner]
    strong = (owner == chosen) | (owner == (partner + blocks // 2) % blocks)
    return jnp.where(strong, factor * entries, entries)


def level_of(rng, dims, cuts, low, top_value):
    factor_of = 1.0
    for axis_at, shards_of in cuts:
        heights = jax.random.uniform(jax.random.fold_in(jax.random.fold_in(rng, 6), axis_at), (shards_of,), jnp.float32, low / len(cuts), top_value / len(cuts))
        factor_of = factor_of * jnp.repeat(jnp.exp(heights), dims[axis_at] // shards_of).reshape((-1,) + (1,) * (len(dims) - 1 - axis_at))
    return factor_of


def scatter_about(own_key, shape, width, limit, pieces=(), held_as=jnp.bfloat16):
    array = jax.random.normal(own_key, shape, jnp.float32) * width
    if len(pieces) > 0:
        array = level_of(own_key, shape, pieces, -0.22, 0.18) * array
    return jnp.clip(array, min=-limit, max=limit).astype(held_as)


def gaussian_with(stream_key, dims, deviation, most, cuts, heavy, dtype=jnp.bfloat16):
    entries = deviation * jax.random.normal(stream_key, dims, jnp.float32)
    if cuts:
        entries = entries * level_of(stream_key, dims, cuts, -0.22, 0.18)
    return jnp.clip(spiked(entries, jax.random.fold_in(stream_key, 3), *heavy), -most, most).astype(dtype)


def setup_inputs(seed: int = 0) -> dict:
    splits = jax.random.split(jax.random.key(seed), 17)
    tokens = scatter_about(splits[0], (BATCH, LENGTH, D), 1.0, 6.0, ((0, 4), (1, 8)))
    doc_reset = draw_doc_reset(jax.random.fold_in(splits[16], 71), 0)
    cotangent = gaussian_with(splits[2], (BATCH, LENGTH, D), 1.0, 6.0, ((0, 4), (1, 8)), (1, 2, 8, 2.0))
    norm_gain = jnp.clip(1.0 + 0.1 * jax.random.normal(splits[3], (D,), jnp.float32), 0.5, 1.5).astype(jnp.bfloat16)
    input_proj = scatter_about(splits[4], (D, REC), D ** -0.5, 0.125, ((0, 32),))
    branch_proj = scatter_about(splits[5], (D, REC), D ** -0.5, 0.125, ((0, 32),))
    conv_kernel = scatter_about(splits[6], (CONV, REC), 0.5, 3.0, ((1, 32),))
    conv_bias = scatter_about(splits[7], (REC,), 0.5, 3.0, ((0, 32),))
    gate_weight = scatter_about(splits[8], (2, REC, BW), BW ** -0.5, 0.375, ((1, 32),))
    gate_bias = scatter_about(splits[9], (2, REC), 1.0, 4.0, ((1, 32),))
    decay_param = draw_decay_param(jax.random.fold_in(splits[16], 71), 0)
    output_proj = scatter_about(splits[11], (REC, D), (REC // 4) ** -0.5, 0.25, ((1, 32),))
    ffn_gain = jnp.clip(1.0 + 0.1 * jax.random.normal(splits[12], (D,), jnp.float32), 0.5, 1.5).astype(jnp.bfloat16)
    ffn_gate = scatter_about(splits[13], (D, FF), D ** -0.5, 0.125, ((0, 32),))
    ffn_up = scatter_about(splits[14], (D, FF), D ** -0.5, 0.125, ((0, 32),))
    ffn_down = scatter_about(splits[15], (FF, D), (FF // 2) ** -0.5, 0.109375, ((0, 32),))
    return dict(tokens=tokens, doc_reset=doc_reset, cotangent=cotangent, norm_gain=norm_gain, input_proj=input_proj, branch_proj=branch_proj, conv_kernel=conv_kernel, conv_bias=conv_bias, gate_weight=gate_weight, gate_bias=gate_bias, decay_param=decay_param, output_proj=output_proj, ffn_gain=ffn_gain, ffn_gate=ffn_gate, ffn_up=ffn_up, ffn_down=ffn_down)


EPSILON = 1e-06
POWER = 8.0
HIGHEST = lax.Precision.HIGHEST

@jax.custom_vjp
def low(v):
    return lax.optimization_barrier(v.astype(jnp.bfloat16)).astype(jnp.float32)

@jax.custom_vjp
def low_back(v):
    return v

def low_keep(v):
    return (low(v), None)

def low_pass(kept, grad):
    return (grad,)

def back_keep(v):
    return (v, None)

def back_low(kept, grad):
    return (low(grad),)
low.defvjp(low_keep, low_pass)
low_back.defvjp(back_keep, back_low)

def rglru_terms(rate_pre, open_pre, conved, lam_vals, keeping):
    rate_val = jax.nn.sigmoid(rate_pre)
    open_val = jax.nn.sigmoid(open_pre)
    log_decay = -POWER * rate_val * jax.nn.softplus(-lam_vals)
    decay_val = jnp.exp(log_decay)
    scaling = keeping * jnp.sqrt(-jnp.expm1(2.0 * log_decay)) + (1.0 - keeping)
    return (decay_val * keeping, scaling * open_val * conved)

def layer_forward(tokens_in, gain_vals, input_proj, branch_proj, conv_kernel, conv_bias, gate_weight, gate_bias, lam_vals, output_proj, ffn_gain, ffn_gate, ffn_up, ffn_down, keeping):
    groups = tokens_in.shape[0]
    length = tokens_in.shape[1]
    mean_square = lax.optimization_barrier(jnp.mean(tokens_in * tokens_in, axis=-1, keepdims=True))
    normed = low(tokens_in * lax.rsqrt(mean_square + EPSILON) * gain_vals)
    inner_val = low(low_back(jnp.einsum('gld,dr->glr', normed, input_proj, precision=HIGHEST)))
    branch = low_back(jnp.einsum('gld,dr->glr', normed, branch_proj, precision=HIGHEST))
    activated = jax.nn.gelu(branch)
    padded = jnp.pad(inner_val, ((0, 0), (CONV - 1, 0), (0, 0)))
    conved = conv_bias + jnp.zeros_like(inner_val)
    for offset in range(CONV):
        conved = conved + conv_kernel[offset] * padded[:, CONV - 1 - offset:CONV - 1 - offset + length]
    rounded = low(conved).reshape(groups, length, BLOCKS, BW)
    mixing = jnp.einsum('glhj,khjm->kglhm', rounded, gate_weight.reshape(2, BLOCKS, BW, BW), precision=HIGHEST)
    mixing = mixing.reshape(2, groups, length, REC) + gate_bias[:, None, None, :]
    gate_rate = low_back(mixing[0])
    gate_open = low_back(mixing[1])
    decay_val, driven = rglru_terms(gate_rate, gate_open, conved, lam_vals, keeping)

    def advance(running_state, step_pair):
        next_state = step_pair[0] * running_state + step_pair[1]
        return (next_state, next_state)
    initial = jnp.zeros((groups, REC), jnp.float32)
    final_state, states = lax.scan(advance, initial, (jnp.swapaxes(decay_val, 0, 1), jnp.swapaxes(driven, 0, 1)))
    hidden = jnp.swapaxes(states, 0, 1)
    mixed_out = low(hidden * activated)
    rec_out = low_back(jnp.einsum('glr,rd->gld', mixed_out, output_proj, precision=HIGHEST))
    middle = tokens_in + rec_out
    mid_square = lax.optimization_barrier(jnp.mean(middle * middle, axis=-1, keepdims=True))
    ffn_normed = low(middle * lax.rsqrt(mid_square + EPSILON) * ffn_gain)
    ffn_pre = low_back(jnp.einsum('gld,df->glf', ffn_normed, ffn_gate, precision=HIGHEST))
    ffn_lin = low_back(jnp.einsum('gld,df->glf', ffn_normed, ffn_up, precision=HIGHEST))
    ffn_hidden = low(jax.nn.gelu(ffn_pre) * ffn_lin)
    return middle + jnp.einsum('glf,fd->gld', ffn_hidden, ffn_down, precision=HIGHEST)

def reference(tokens, doc_reset, cotangent, norm_gain, input_proj, branch_proj, conv_kernel, conv_bias, gate_weight, gate_bias, decay_param, output_proj, ffn_gain, ffn_gate, ffn_up, ffn_down):
    group_size = math.gcd(BATCH, max(1, 4096 // LENGTH))
    group_count = BATCH // group_size
    weights = tuple((array_in.astype(jnp.float32) for array_in in (norm_gain, input_proj, branch_proj, conv_kernel, conv_bias, gate_weight, gate_bias, decay_param, output_proj, ffn_gain, ffn_gate, ffn_up, ffn_down)))
    keeping = (1 - doc_reset).astype(jnp.float32)[..., None]
    stacked = (tokens.astype(jnp.float32).reshape(group_count, group_size, LENGTH, D), keeping.reshape(group_count, group_size, LENGTH, 1), cotangent.astype(jnp.float32).reshape(group_count, group_size, LENGTH, D))

    def visit(totals, group_items):
        tokens_in, keep_in, cot_in = group_items
        result, pullback = jax.vjp(lambda first_arg, *weight_list: layer_forward(first_arg, *weight_list, keep_in), tokens_in, *weights)
        gradients = pullback(cot_in)
        totals = tuple((left_sum + right_term for left_sum, right_term in zip(totals, gradients[1:])))
        return (totals, (result, gradients[0]))
    zero_totals = tuple((jnp.zeros_like(array_in) for array_in in weights))
    totals, (outputs, input_grads) = lax.scan(visit, zero_totals, stacked)
    return (outputs.reshape(BATCH, LENGTH, D), input_grads.reshape(BATCH, LENGTH, D), totals[0], totals[1], totals[2], totals[3], totals[4], totals[5], totals[6], totals[7], totals[8], totals[9], totals[10], totals[11], totals[12])
```

```python
import functools

import jax
import jax.numpy as jnp
from jax import lax
from jax.experimental import pallas as pl
from jax.experimental.pallas import tpu as pltpu
from jax.sharding import Mesh
from jax.sharding import PartitionSpec as P

EPSILON = 1e-06
POWER = 8.0
BF = jnp.bfloat16
F32 = jnp.float32
GROUP = ("dp", "core")
EVERY = ("dp", "z", "core")
GELU_A = 0.7978845608028654
GELU_B = 0.044715
HALO = 16
VMEM_BYTES = 48 * 1024 * 1024


def gelu_pair(x):
    x2 = x * x
    th = jnp.tanh(GELU_A * (x + GELU_B * x2 * x))
    half = 0.5 * (1.0 + th)
    slope = half + 0.5 * x * (1.0 - th * th) * (GELU_A * (1.0 + 3.0 * GELU_B * x2))
    return x * half, slope


def gelu_only(x):
    return 0.5 * x * (1.0 + jnp.tanh(GELU_A * (x + GELU_B * x * x * x)))


def dot(a, b):
    return lax.dot_general(a, b, (((1,), (0,)), ((), ())), preferred_element_type=F32)


def dot_rows(a, b):
    return lax.dot_general(a, b, (((0,), (0,)), ((), ())), preferred_element_type=F32)


def dot_cols(a, b):
    return lax.dot_general(a, b, (((1,), (1,)), ((), ())), preferred_element_type=F32)


def minus_expm1(x):
    series = -x * (1.0 + x * (1 / 2) * (1.0 + x * (1 / 3) * (1.0 + x * (1 / 4) * (1.0 + x * (1 / 5) * (1.0 + x * (1 / 6))))))
    return jnp.where(x > -0.125, series, 1.0 - jnp.exp(x))


def conv_and_gates(inner_ref, prev, vec, gwf_ref, gws_ref, ext, block, own):
    rows = inner_ref.shape[0]
    ext[0:HALO, :] = prev.astype(F32)
    ext[HALO : HALO + rows, :] = inner_ref[...].astype(F32)
    conved = vec[4:5, :] + vec[0:1, :] * ext[HALO : HALO + rows, :]
    for tap in range(1, 4):
        conved = conved + vec[tap : tap + 1, :] * ext[HALO - tap : HALO - tap + rows, :]
    rounded = conved.astype(BF)
    gf = dot(rounded[:, :block], gwf_ref[...])
    gs = dot(rounded[:, block:], gws_ref[...])
    part = own - block
    rate_pre = jnp.concatenate([gf[:, :block], gs[:, :part]], axis=1) + vec[5:6, :own]
    open_pre = jnp.concatenate([gf[:, block:], gs[:, part:]], axis=1) + vec[6:7, :own]
    return conved, rounded, rate_pre, open_pre


def scan_groups(a_ref, b_ref, out_h, out_c, h, c, rows, width):
    place = lax.broadcasted_iota(jnp.int32, (8, width), 0)

    def one(g, carry):
        h, c = carry
        at = pl.ds(pl.multiple_of(g * 8, 8), 8)
        a, b = a_ref[at, :], b_ref[at, :]
        for shift in (1, 2, 4):
            keep = place >= shift
            pa = jnp.where(keep, pltpu.roll(a, shift, 0), 1.0)
            pb = jnp.where(keep, pltpu.roll(b, shift, 0), 0.0)
            b = a * pb + b
            a = a * pa
        b = b + a * h
        a = a * c
        out_h[at, :] = b
        out_c[at, :] = a
        return b[7:8, :], a[7:8, :]

    return lax.fori_loop(0, rows // 8, one, (h, c), unroll=4)


def forward_kernel(
    inner_ref, prev_ref, halo_ref, keep_ref, vec_ref, gwf_ref, gws_ref,
    decay_ref, local_ref, cum_ref, last_ref, ext, b_ref, carry, *, block, own,
):
    c = pl.program_id(2)
    rows = inner_ref.shape[0]
    prev = jnp.where(c == 0, halo_ref[...].astype(F32), prev_ref[...].astype(F32))
    vec = vec_ref[...]
    conved, _, rate_pre, open_pre = conv_and_gates(inner_ref, prev, vec, gwf_ref, gws_ref, ext, block, own)
    keep = keep_ref[...]
    rate = jax.nn.sigmoid(rate_pre)
    opening = jax.nn.sigmoid(open_pre)
    log_decay = vec[7:8, :own] * rate
    scale = keep * jnp.sqrt(minus_expm1(2.0 * log_decay)) + (1.0 - keep)
    decay_ref[...] = jnp.exp(log_decay) * keep
    b_ref[...] = scale * opening * conved[:, :own]

    @pl.when(c == 0)
    def _():
        carry[0:1, :] = jnp.zeros((1, own), F32)
        carry[1:2, :] = jnp.ones((1, own), F32)

    h, p = scan_groups(decay_ref, b_ref, local_ref, cum_ref, carry[0:1, :], carry[1:2, :], rows, own)
    carry[0:1, :] = h
    carry[1:2, :] = p
    last_ref[...] = carry[...]


def reverse_kernel(decay_ref, grad_ref, branch_ref, adj_ref, prod_ref, first_ref, carry, *, own):
    c = pl.program_id(2)
    rows = decay_ref.shape[0]
    place = lax.broadcasted_iota(jnp.int32, (8, own), 0)

    @pl.when(c == 0)
    def _():
        carry[0:1, :] = jnp.zeros((1, own), F32)
        carry[1:2, :] = jnp.ones((1, own), F32)

    def one(i, state):
        s, p = state
        at = pl.ds(pl.multiple_of((rows // 8 - 1 - i) * 8, 8), 8)
        a = decay_ref[at, :]
        hg = grad_ref[at, :] * gelu_only(branch_ref[at, :])
        b = a * hg
        for shift in (1, 2, 4):
            keep = place < 8 - shift
            na = jnp.where(keep, pltpu.roll(a, 8 - shift, 0), 1.0)
            nb = jnp.where(keep, pltpu.roll(b, 8 - shift, 0), 0.0)
            b = a * nb + b
            a = a * na
        b = b + a * s
        a = a * p
        last = place == 7
        adj_ref[at, :] = hg + jnp.where(last, s, pltpu.roll(b, 7, 0))
        prod_ref[at, :] = jnp.where(last, p, pltpu.roll(a, 7, 0))
        return b[0:1, :], a[0:1, :]

    s, p = lax.fori_loop(0, rows // 8, one, (carry[0:1, :], carry[1:2, :]), unroll=4)
    carry[0:1, :] = s
    carry[1:2, :] = p
    first_ref[...] = carry[...]


def backward_kernel(
    inner_ref, prev_ref, halo_ref, keep_ref, vec_ref, gwf_ref, gws_ref, hidden_ref, before_ref, start_ref,
    adj_ref, prod_ref, suffix_ref,
    igrad_ref, tail_ref, head_ref, dgf_ref, dgs_ref, sums_ref, ext, hext, cext, *, block, own,
):
    c = pl.program_id(2)
    peers = pl.num_programs(2)
    first = (pl.program_id(0) == 0) & (pl.program_id(1) == 0) & (c == 0)
    at_start = c == peers - 1
    rows = inner_ref.shape[0]
    part = own - block
    window = vec_ref.shape[1]

    @pl.when(first)
    def _():
        dgf_ref[...] = jnp.zeros_like(dgf_ref)
        dgs_ref[...] = jnp.zeros_like(dgs_ref)
        sums_ref[...] = jnp.zeros_like(sums_ref)

    @pl.when(c == 0)
    def _():
        cext[rows : rows + 8, :] = jnp.zeros((8, window), F32)

    @pl.when(c > 0)
    def _():
        cext[rows : rows + 8, :] = cext[0:8, :]

    prev = jnp.where(at_start, halo_ref[...].astype(F32), prev_ref[...].astype(F32))
    vec = vec_ref[...]
    conved, rounded, rate_pre, open_pre = conv_and_gates(inner_ref, prev, vec, gwf_ref, gws_ref, ext, block, own)
    keep = keep_ref[...]
    conv = conved[:, :own]
    rate = jax.nn.sigmoid(rate_pre)
    opening = jax.nn.sigmoid(open_pre)
    factor = vec[7:8, :own]
    log_decay = factor * rate
    e = jnp.exp(log_decay)
    root = jnp.sqrt(minus_expm1(2.0 * log_decay))
    scale = keep * root + (1.0 - keep)

    adj = adj_ref[...] + prod_ref[...] * suffix_ref[0:1, :]
    hext[0:8, :] = jnp.where(at_start, jnp.broadcast_to(start_ref[0:1, :], (8, own)), before_ref[...])
    hext[8 : 8 + rows, :] = hidden_ref[...]
    before = hext[7 : 7 + rows, :]
    d_log = keep * (adj * before * e - adj * opening * conv * (e * e) / root)
    direct = adj * scale * opening
    g_rate = (d_log * factor * rate * (1.0 - rate)).astype(BF)
    g_open = (adj * scale * conv * opening * (1.0 - opening)).astype(BF)
    gf = jnp.concatenate([g_rate[:, :block], g_open[:, :block]], axis=1)
    gs = jnp.concatenate([g_rate[:, block:], g_open[:, block:]], axis=1)
    cgrad = jnp.concatenate([dot_cols(gf, gwf_ref[...]), dot_cols(gs, gws_ref[...])], axis=1)
    cgrad = cgrad + jnp.concatenate([direct, jnp.zeros((rows, window - own), F32)], axis=1)
    cext[0:rows, :] = cgrad
    dgf_ref[...] += dot_rows(rounded[:, :block], gf)
    dgs_ref[...] += dot_rows(rounded[:, block:], gs)

    igrad = vec[0:1, :] * cgrad
    for tap in range(1, 4):
        igrad = igrad + vec[tap : tap + 1, :] * cext[tap : tap + rows, :]
    igrad_ref[...] = igrad.astype(BF)

    @pl.when(c == 0)
    def _():
        tail_ref[...] = igrad[rows - HALO :, :]

    head_ref[...] = cgrad[0:8, :]

    def total(x):
        return jnp.sum(x, axis=0, keepdims=True)

    for tap in range(4):
        sums_ref[tap : tap + 1, :] += total(ext[HALO - tap : HALO - tap + rows, :] * cgrad)
    sums_ref[4:5, :] += total(cgrad)
    sums_ref[5:6, :own] += total(g_rate.astype(F32))
    sums_ref[6:7, :own] += total(g_open.astype(F32))
    sums_ref[7:8, :own] += total(d_log * rate)


class Blocks:
    def __init__(self, peers, seqs, back):
        self.peers, self.seqs, self.back = peers, seqs, back

    def core(self, c):
        return self.peers - 1 - c if self.back else c

    def rows(self, count, width):
        return pl.BlockSpec((count, width), lambda d, s, c: ((d * self.peers + self.core(c)) * self.seqs + s, 0))

    def before(self, count, width, length):
        each = length // count

        def index(d, s, c):
            c = jnp.maximum(self.core(c) - 1, 0)
            return (((d * self.peers + c) * self.seqs + s) * each + each - 1, 0)

        return pl.BlockSpec((count, width), index)

    def sequence(self, count, width):
        return pl.BlockSpec((count, width), lambda d, s, c: (d * self.seqs + s, 0))

    def whole(self, *shape):
        return pl.BlockSpec(shape, lambda d, s, c: (0,) * len(shape))


def body(
    tokens, doc_reset, cotangent, norm_gain, input_proj, branch_proj, conv_kernel, conv_bias, gate_weight, gate_bias,
    decay_param, output_proj, ffn_gain, ffn_gate, ffn_up, ffn_down,
):
    seqs, span, width = tokens.shape
    rows = seqs * span
    n_dp, n_z, n_core = (lax.axis_size(a) for a in EVERY)
    group = n_dp * n_core
    devices = group * n_z
    zi = lax.axis_index("z")
    me = lax.axis_index("dp") * n_core + lax.axis_index("core")
    rec = input_proj.shape[1]
    ff = ffn_gate.shape[1]
    block = gate_weight.shape[2]
    taps = conv_kernel.shape[0]
    drow = input_proj.shape[0]
    frow = ffn_down.shape[0]
    ff_own = ff // group
    blocks = rec // block
    shared = blocks - group
    sharers = group // shared
    part = block // sharers
    lanes = 128 * (-(-part // 128))
    own = block + lanes
    window = 2 * block
    total_rows = group * rows
    lines = n_dp * seqs

    def d_to_z(x):
        lead = x.shape[:-1]
        y = x.reshape(*lead, n_dp, n_z, n_core * drow)
        return jnp.swapaxes(y, -3, -2).reshape(*lead, width)

    def d_from_z(x):
        lead = x.shape[:-1]
        y = x.reshape(*lead, n_z, n_dp, n_core * drow)
        return jnp.swapaxes(y, -3, -2).reshape(*lead, width)

    def own_columns(w):
        lead = w.shape[0]
        full = w[:, : group * block].reshape(lead, group, block)
        rest = w[:, group * block :].reshape(lead, group, part)
        return jnp.concatenate([full, rest, jnp.zeros((lead, group, lanes - part), w.dtype)], axis=2)

    def window_columns(w):
        lead = w.shape[0]
        full = w[:, : group * block].reshape(lead, group, block)
        rest = w[:, group * block :].reshape(lead, shared, block)
        turned = jnp.stack([jnp.roll(rest, -part * q, axis=2) for q in range(sharers)], axis=2)
        return jnp.concatenate([full, turned.reshape(lead, group, block)], axis=2)

    def exchange(x):
        return lax.all_to_all(x, GROUP, split_axis=0, concat_axis=0, tiled=True)

    def to_members(x):
        y = jnp.swapaxes(x, 0, 1)
        return exchange(y.reshape(group * x.shape[0], x.shape[2]))

    def over_z(x):
        return lax.all_gather(x, "z", axis=0, tiled=True)

    w_in = over_z(to_members(jnp.concatenate([window_columns(input_proj), own_columns(branch_proj)], axis=2)))
    w_out = over_z(to_members(own_columns(output_proj.T)))

    def ff_columns(w):
        y = w.reshape(drow, n_dp, n_z, n_core, frow)
        return jnp.transpose(y, (0, 1, 3, 2, 4)).reshape(drow, group, ff_own)

    w_ff = over_z(to_members(jnp.concatenate([ff_columns(ffn_gate), ff_columns(ffn_up)], axis=2)))
    w_down = over_z(ffn_down)

    rrow = rec // devices
    small = jnp.concatenate(
        [
            gate_weight.reshape(-1), norm_gain, ffn_gain, conv_kernel.reshape(-1), conv_bias, gate_bias.reshape(-1),
            decay_param,
        ]
    )
    small_len = small.shape[0]
    small = jnp.pad(small, (0, -small_len % (16 * 256))).reshape(-1, 256)
    small = lax.all_gather(small, EVERY, axis=0, tiled=False).reshape(devices, -1)
    gates_len = 2 * rrow * block
    gates_all = small[:, :gates_len].reshape(devices, 2, rrow, block)
    gates_all = jnp.swapaxes(gates_all, 0, 1).reshape(2, rec, block)
    rest = small[:, gates_len:small_len].astype(F32)
    gain = rest[:, :drow].reshape(width)
    fgain = rest[:, drow : 2 * drow].reshape(width)
    chan = rest[:, 2 * drow :].reshape(devices, taps + 4, rrow)
    chan = jnp.swapaxes(chan, 0, 1).reshape(taps + 4, rec)
    lam = chan[taps + 3 :]
    chan = jnp.concatenate([chan[: taps + 3], -POWER * jax.nn.softplus(-lam)], axis=0)

    quarter = me % sharers
    shared_at = (group + me // sharers) * block

    def my_window(x, axis):
        full = lax.dynamic_slice_in_dim(x, me * block, block, axis)
        other = lax.dynamic_slice_in_dim(x, shared_at, block, axis)
        turned = lax.dynamic_slice_in_dim(jnp.concatenate([other, other], axis), quarter * part, block, axis)
        return full, turned

    vec = jnp.concatenate(my_window(chan, 1), axis=1)
    gw_full, gw_shared = my_window(gates_all, 1)
    gw_shared = lax.dynamic_slice_in_dim(gw_shared, quarter * part, part, 2)
    gw_shared = jnp.pad(gw_shared, ((0, 0), (0, 0), (0, lanes - part)))
    gwf = jnp.concatenate([gw_full[0], gw_full[1]], axis=1)
    gws = jnp.concatenate([gw_shared[0], gw_shared[1]], axis=1)

    tok = d_to_z(tokens.reshape(rows, width)).astype(F32)
    cot = cotangent.reshape(rows, width)
    gain_z = d_to_z(gain)
    fgain_z = d_to_z(fgain)
    inv = lax.rsqrt(jnp.mean(tok * tok, axis=1, keepdims=True) + EPSILON)
    normed_own = (tok * inv * gain_z).astype(BF)

    def over_group(x):
        return lax.all_gather(x, GROUP, axis=0, tiled=True)

    def sum_group(x):
        return lax.psum_scatter(x.astype(BF), GROUP, scatter_dimension=0, tiled=True).astype(F32)

    normed = over_group(normed_own)
    keep = over_group((1 - doc_reset).astype(BF).reshape(rows)).astype(F32).reshape(total_rows, 1)
    cot_all = over_group(cot)

    both = dot(normed, w_in)
    inner = both[:, :window].astype(BF)
    branch = both[:, window:]
    ends = inner.reshape(n_dp, n_core, seqs, span, window)[:, n_core - 1, :, span - HALO :].reshape(lines * HALO, window)
    halo = lax.ppermute(ends, "z", [(i, i + 1) for i in range(n_z - 1)])

    grid = (n_dp, seqs, n_core)
    at = Blocks(n_core, seqs, False)
    params = pltpu.CompilerParams(vmem_limit_bytes=VMEM_BYTES)
    seq_in = [
        lambda b: b.rows(span, window), lambda b: b.before(HALO, window, span), lambda b: b.sequence(HALO, window),
        lambda b: b.rows(span, 1), lambda b: b.whole(8, window), lambda b: b.whole(block, window),
        lambda b: b.whole(block, 2 * lanes),
    ]
    row_f32 = jax.ShapeDtypeStruct((total_rows, own), F32)
    decay, local, cum, last = pl.pallas_call(
        functools.partial(forward_kernel, block=block, own=own),
        grid=grid,
        in_specs=[f(at) for f in seq_in],
        out_specs=[at.rows(span, own)] * 3 + [at.sequence(8, own)],
        out_shape=[row_f32] * 3 + [jax.ShapeDtypeStruct((lines * 8, own), F32)],
        scratch_shapes=[
            pltpu.VMEM((span + HALO, window), F32), pltpu.VMEM((span, own), F32), pltpu.VMEM((8, own), F32),
        ],
        compiler_params=params,
    )(inner, inner, halo, keep, vec, gwf, gws)

    def carried(x, order, reached):
        every = lax.all_gather(x.reshape(lines, 8, own)[:, :2], "z", axis=0, tiled=False)
        state = jnp.zeros((lines, own), F32)
        for k in order:
            state = jnp.where(reached(k), every[k, :, 1] * state + every[k, :, 0], state)
        return state

    start = carried(last, range(n_z), lambda k: k < zi)

    def by_line(x):
        return x.reshape(n_dp, 1, seqs, 1, own)

    def spread(x):
        return x.reshape(n_dp, n_core, seqs, span, own)

    hidden = (spread(local) + spread(cum) * by_line(start)).reshape(total_rows, own)
    mixed_out = (hidden * gelu_only(branch)).astype(BF)
    mid = tok + sum_group(dot_cols(mixed_out, w_out))

    finv = lax.rsqrt(jnp.mean(mid * mid, axis=1, keepdims=True) + EPSILON)
    fnormed = over_group((mid * finv * fgain_z).astype(BF))
    pre_lin = dot(fnormed, w_ff)
    act, slope = gelu_pair(pre_lin[:, :ff_own])
    lin = pre_lin[:, ff_own:]
    fhidden = (act * lin).astype(BF)
    hid_grad = dot_cols(cot_all, w_down)
    fgrad = jnp.concatenate([(hid_grad * lin * slope).astype(BF), (hid_grad * act).astype(BF)], axis=1)
    fnormed_grad = sum_group(dot_cols(fgrad, w_ff))
    layer_out = d_from_z(mid) + sum_group(dot(fhidden, w_down))

    fg = fgain_z * fnormed_grad
    ffn_gain_part = jnp.sum(fnormed_grad * mid * finv, axis=0)
    mid_grad = (
        d_to_z(cot).astype(F32) + finv * fg - mid * (finv * finv * finv) * jnp.mean(mid * fg, axis=1, keepdims=True)
    )
    mid_low = over_group(mid_grad.astype(BF))

    def sum_z(x):
        return lax.psum_scatter(x.astype(BF), "z", scatter_dimension=0, tiled=True)

    down_out = sum_z(dot_rows(fhidden, cot_all)).astype(F32)
    ff_part = exchange(sum_z(dot_rows(fnormed, fgrad))).reshape(group, drow, 2, ff_own)

    def ff_natural(x):
        y = x.reshape(n_dp, n_core, drow, n_z, frow)
        return jnp.transpose(y, (2, 0, 3, 1, 4)).reshape(drow, ff).astype(F32)

    mixed_grad = dot(mid_low, w_out)
    act_r, slope_r = gelu_pair(branch)
    branch_grad = (mixed_grad * hidden * slope_r).astype(BF)
    back = Blocks(n_core, seqs, True)
    adj, prod, front = pl.pallas_call(
        functools.partial(reverse_kernel, own=own),
        grid=grid,
        in_specs=[back.rows(span, own)] * 3,
        out_specs=[back.rows(span, own)] * 2 + [back.sequence(8, own)],
        out_shape=[row_f32] * 2 + [jax.ShapeDtypeStruct((lines * 8, own), F32)],
        scratch_shapes=[pltpu.VMEM((8, own), F32)],
        compiler_params=params,
    )(decay, mixed_grad, branch)
    suffix = carried(front, reversed(range(n_z)), lambda k: k > zi)

    def eight(x):
        return jnp.broadcast_to(x[:, None, :], (lines, 8, own)).reshape(lines * 8, own)

    igrad, tail, head, dgf, dgs, sums = pl.pallas_call(
        functools.partial(backward_kernel, block=block, own=own),
        grid=grid,
        in_specs=[f(back) for f in seq_in]
        + [
            back.rows(span, own), back.before(8, own, span), back.sequence(8, own), back.rows(span, own),
            back.rows(span, own), back.sequence(8, own),
        ],
        out_specs=[
            back.rows(span, window), back.sequence(HALO, window), back.sequence(8, window), back.whole(block, window),
            back.whole(block, 2 * lanes), back.whole(8, window),
        ],
        out_shape=[
            jax.ShapeDtypeStruct((total_rows, window), BF), jax.ShapeDtypeStruct((lines * HALO, window), F32),
            jax.ShapeDtypeStruct((lines * 8, window), F32), jax.ShapeDtypeStruct((block, window), F32),
            jax.ShapeDtypeStruct((block, 2 * lanes), F32), jax.ShapeDtypeStruct((8, window), F32),
        ],
        scratch_shapes=[
            pltpu.VMEM((span + HALO, window), F32), pltpu.VMEM((span + 8, own), F32), pltpu.VMEM((span + 8, window), F32),
        ],
        compiler_params=params,
    )(inner, inner, halo, keep, vec, gwf, gws, hidden, hidden, eight(start), adj, prod, eight(suffix))

    after = lax.ppermute(head.astype(BF), "z", [(i + 1, i) for i in range(n_z - 1)]).astype(F32).reshape(lines, 8, window)
    fix = jnp.zeros((lines, HALO, window), F32)
    for tap in range(1, taps):
        fix = fix.at[:, HALO - tap :, :].add(vec[tap] * after[:, :tap])
    tail = (tail.reshape(lines, HALO, window) + fix).astype(BF).reshape(n_dp, 1, seqs, HALO, window)
    igrad = lax.dynamic_update_slice(
        igrad.reshape(n_dp, n_core, seqs, span, window), tail, (0, n_core - 1, 0, span - HALO, 0)
    ).reshape(total_rows, window)
    rgrad = jnp.concatenate([igrad, branch_grad], axis=1)
    normed_grad = sum_group(dot_cols(rgrad, w_in))

    g = gain_z * normed_grad
    gain_part = jnp.sum(normed_grad * tok * inv, axis=0)
    input_grad = mid_grad + inv * g - tok * (inv * inv * inv) * jnp.mean(tok * g, axis=1, keepdims=True)
    input_grad = d_from_z(input_grad)

    out_part = exchange(sum_z(dot_rows(mid_low, mixed_out))).reshape(group, drow, own)
    in_part = exchange(sum_z(dot_rows(normed, rgrad))).reshape(group, drow, window + own)

    def own_natural(x):
        full = jnp.swapaxes(x[:, :, :block], 0, 1).reshape(drow, group * block)
        rest = jnp.swapaxes(x[:, :, block : block + part], 0, 1).reshape(drow, group * part)
        return jnp.concatenate([full, rest], axis=1).astype(F32)

    full = jnp.swapaxes(in_part[:, :, :block], 0, 1).reshape(drow, group * block).astype(F32)
    turned = in_part[:, :, block:window].astype(F32).reshape(shared, sharers, drow, block)
    other = sum(jnp.roll(turned[:, q], part * q, axis=2) for q in range(sharers))
    input_proj_grad = jnp.concatenate([full, jnp.swapaxes(other, 0, 1).reshape(drow, shared * block)], axis=1)
    branch_proj_grad = own_natural(in_part[:, :, window:])
    output_proj_grad = own_natural(out_part).T

    def place_window(x, axis_len):
        lead = x.shape[:-1]
        other = x[..., block:]
        turned = lax.dynamic_slice_in_dim(
            jnp.concatenate([other, other], -1), lax.rem(block - quarter * part, block), block, x.ndim - 1
        )
        y = jnp.zeros((*lead, axis_len), x.dtype)
        y = lax.dynamic_update_slice_in_dim(y, x[..., :block], me * block, x.ndim - 1)
        return lax.dynamic_update_slice_in_dim(y, turned, shared_at, x.ndim - 1)

    lane = jnp.arange(window)
    mine = lane < block + part
    sums = jnp.where(jnp.concatenate([jnp.ones((5, window), bool), jnp.broadcast_to(mine, (3, window))], axis=0), sums, 0.0)
    sums = place_window(sums, rec)
    sums = jnp.concatenate([sums[:7], sums[7:8] * (POWER * jax.nn.sigmoid(-lam))], axis=0)
    vectors = jnp.concatenate(
        [
            d_from_z(gain_part).reshape(devices, drow), d_from_z(ffn_gain_part).reshape(devices, drow),
            jnp.swapaxes(sums.reshape(8, devices, rrow), 0, 1).reshape(devices, 8 * rrow),
        ],
        axis=1,
    )
    vec_len = vectors.shape[1]
    vectors = lax.all_to_all(vectors, EVERY, split_axis=0, concat_axis=0, tiled=True)
    vectors = jnp.sum(vectors.reshape(devices, vec_len), axis=0)
    gain_out = vectors[:drow]
    fgain_out = vectors[drow : 2 * drow]
    chan_out = vectors[2 * drow :].reshape(8, rrow)

    dg_full = jnp.stack([dgf[:, :block], dgf[:, block:]])
    dg_shared = jnp.stack([dgs[:, :part], dgs[:, lanes : lanes + part]])
    dg_shared = lax.dynamic_slice_in_dim(
        jnp.concatenate([dg_shared, dg_shared], 1), lax.rem(block - quarter * part, block), block, 1
    )
    gates = jnp.zeros((2, rec, block), BF)
    gates = lax.dynamic_update_slice(gates, dg_full.astype(BF), (0, me * block, 0))
    gates = lax.dynamic_update_slice(gates, dg_shared.astype(BF), (0, shared_at, quarter * part))
    gates = jnp.swapaxes(gates.reshape(2, devices, rrow, block), 0, 1).reshape(devices * 2 * rrow, block)
    gates = lax.all_to_all(gates, EVERY, split_axis=0, concat_axis=0, tiled=True)
    gates_out = jnp.sum(gates.reshape(devices, 2, rrow, block).astype(F32), axis=0)

    return (
        layer_out.reshape(seqs, span, width),
        input_grad.reshape(seqs, span, width),
        gain_out,
        input_proj_grad,
        branch_proj_grad,
        chan_out[:taps],
        chan_out[taps],
        gates_out,
        chan_out[taps + 1 : taps + 3],
        chan_out[taps + 3],
        output_proj_grad,
        fgain_out,
        ff_natural(ff_part[:, :, 0]),
        ff_natural(ff_part[:, :, 1]),
        down_out,
    )


def solution(mesh):
    n_dp, n_seq = mesh.shape["dp"], mesh.shape["seq"]
    split = Mesh(mesh.devices.reshape(n_dp, n_seq // 2, 2), EVERY)
    seq = ("z", "core")
    line = P("dp", seq, None)
    first = P(EVERY)
    rows = P(EVERY, None)
    cols = P(None, EVERY)
    mids = P(None, EVERY, None)
    return jax.shard_map(
        body,
        mesh=split,
        in_specs=(
            line, P("dp", seq), line, first, rows, rows, cols, first, mids, cols, first, cols, first, rows, rows, rows,
        ),
        out_specs=(
            line, line, first, rows, rows, cols, first, mids, cols, first, cols, first, rows, rows, rows,
        ),
        check_vma=False,
    )
```

```python
import functools

import jax
import jax.numpy as jnp
from jax import lax
from jax.experimental import pallas as pl
from jax.experimental.pallas import tpu as pltpu
from jax.sharding import Mesh
from jax.sharding import PartitionSpec as P

EPSILON = 1e-06
POWER = 8.0
BF = jnp.bfloat16
F32 = jnp.float32
GROUP = ("dp", "core")
EVERY = ("dp", "z", "core")
GELU_A = 0.7978845608028654
GELU_B = 0.044715
HALO = 16
VMEM_BYTES = 48 * 1024 * 1024


def after(x, *others):
    return lax.optimization_barrier((x, *others))[0]


def gelu_pair(x):
    x2 = x * x
    th = jnp.tanh(GELU_A * (x + GELU_B * x2 * x))
    half = 0.5 * (1.0 + th)
    slope = half + 0.5 * x * (1.0 - th * th) * (GELU_A * (1.0 + 3.0 * GELU_B * x2))
    return x * half, slope


def gelu_only(x):
    return 0.5 * x * (1.0 + jnp.tanh(GELU_A * (x + GELU_B * x * x * x)))


def dot(a, b):
    return lax.dot_general(a, b, (((1,), (0,)), ((), ())), preferred_element_type=F32)


def dot_rows(a, b):
    return lax.dot_general(a, b, (((0,), (0,)), ((), ())), preferred_element_type=F32)


def dot_cols(a, b):
    return lax.dot_general(a, b, (((1,), (1,)), ((), ())), preferred_element_type=F32)


def minus_expm1(x):
    series = -x * (1.0 + x * (1 / 2) * (1.0 + x * (1 / 3) * (1.0 + x * (1 / 4) * (1.0 + x * (1 / 5) * (1.0 + x * (1 / 6))))))
    return jnp.where(x > -0.125, series, 1.0 - jnp.exp(x))


def conv_and_gates(inner_ref, prev, vec, gwf_ref, gws_ref, ext, block, own):
    rows = inner_ref.shape[0]
    ext[0:HALO, :] = prev.astype(F32)
    ext[HALO : HALO + rows, :] = inner_ref[...].astype(F32)
    conved = vec[4:5, :] + vec[0:1, :] * ext[HALO : HALO + rows, :]
    for tap in range(1, 4):
        conved = conved + vec[tap : tap + 1, :] * ext[HALO - tap : HALO - tap + rows, :]
    rounded = conved.astype(BF)
    gf = dot(rounded[:, :block], gwf_ref[...])
    gs = dot(rounded[:, block:], gws_ref[...])
    part = own - block
    rate_pre = jnp.concatenate([gf[:, :block], gs[:, :part]], axis=1) + vec[5:6, :own]
    open_pre = jnp.concatenate([gf[:, block:], gs[:, part:]], axis=1) + vec[6:7, :own]
    return conved, rounded, rate_pre, open_pre


def scan_groups(a_ref, b_ref, out_h, out_c, h, c, rows, width):
    place = lax.broadcasted_iota(jnp.int32, (8, width), 0)

    def one(g, carry):
        h, c = carry
        at = pl.ds(pl.multiple_of(g * 8, 8), 8)
        a, b = a_ref[at, :], b_ref[at, :]
        for shift in (1, 2, 4):
            keep = place >= shift
            pa = jnp.where(keep, pltpu.roll(a, shift, 0), 1.0)
            pb = jnp.where(keep, pltpu.roll(b, shift, 0), 0.0)
            b = a * pb + b
            a = a * pa
        b = b + a * h
        a = a * c
        out_h[at, :] = b
        out_c[at, :] = a
        return b[7:8, :], a[7:8, :]

    return lax.fori_loop(0, rows // 8, one, (h, c), unroll=4)


def forward_kernel(
    core_ref, inner_ref, prev_ref, halo_ref, keep_ref, vec_ref, gwf_ref, gws_ref,
    decay_ref, local_ref, cum_ref, last_ref, ext, b_ref, carry, *, block, own,
):
    c = pl.program_id(2)
    rows = inner_ref.shape[0]
    prev = jnp.where(c == 0, halo_ref[...].astype(F32), prev_ref[...].astype(F32))
    vec = vec_ref[...]
    conved, _, rate_pre, open_pre = conv_and_gates(inner_ref, prev, vec, gwf_ref, gws_ref, ext, block, own)
    keep = keep_ref[...]
    rate = jax.nn.sigmoid(rate_pre)
    opening = jax.nn.sigmoid(open_pre)
    log_decay = vec[7:8, :own] * rate
    scale = keep * jnp.sqrt(minus_expm1(2.0 * log_decay)) + (1.0 - keep)
    decay_ref[...] = jnp.exp(log_decay) * keep
    b_ref[...] = scale * opening * conved[:, :own]

    @pl.when(c == 0)
    def _():
        carry[0:1, :] = jnp.zeros((1, own), F32)
        carry[1:2, :] = jnp.ones((1, own), F32)

    h, p = scan_groups(decay_ref, b_ref, local_ref, cum_ref, carry[0:1, :], carry[1:2, :], rows, own)
    carry[0:1, :] = h
    carry[1:2, :] = p
    last_ref[...] = carry[...]


def reverse_kernel(core_ref, decay_ref, grad_ref, branch_ref, adj_ref, prod_ref, first_ref, carry, *, own):
    c = pl.program_id(2)
    rows = decay_ref.shape[0]
    place = lax.broadcasted_iota(jnp.int32, (8, own), 0)

    @pl.when(c == 0)
    def _():
        carry[0:1, :] = jnp.zeros((1, own), F32)
        carry[1:2, :] = jnp.ones((1, own), F32)

    def one(i, state):
        s, p = state
        at = pl.ds(pl.multiple_of((rows // 8 - 1 - i) * 8, 8), 8)
        a = decay_ref[at, :]
        hg = grad_ref[at, :] * gelu_only(branch_ref[at, :])
        b = a * hg
        for shift in (1, 2, 4):
            keep = place < 8 - shift
            na = jnp.where(keep, pltpu.roll(a, 8 - shift, 0), 1.0)
            nb = jnp.where(keep, pltpu.roll(b, 8 - shift, 0), 0.0)
            b = a * nb + b
            a = a * na
        b = b + a * s
        a = a * p
        last = place == 7
        adj_ref[at, :] = hg + jnp.where(last, s, pltpu.roll(b, 7, 0))
        prod_ref[at, :] = jnp.where(last, p, pltpu.roll(a, 7, 0))
        return b[0:1, :], a[0:1, :]

    s, p = lax.fori_loop(0, rows // 8, one, (carry[0:1, :], carry[1:2, :]), unroll=4)
    carry[0:1, :] = s
    carry[1:2, :] = p
    first_ref[...] = carry[...]


def backward_kernel(
    core_ref, inner_ref, prev_ref, halo_ref, keep_ref, vec_ref, gwf_ref, gws_ref, hidden_ref, before_ref, start_ref,
    adj_ref, prod_ref, suffix_ref,
    igrad_ref, tail_ref, head_ref, dgf_ref, dgs_ref, sums_ref, ext, hext, cext, *, block, own,
):
    c = pl.program_id(2)
    peers = pl.num_programs(2)
    first = (pl.program_id(0) == 0) & (pl.program_id(1) == 0) & (c == 0)
    at_start = c == peers - 1
    rows = inner_ref.shape[0]
    part = own - block
    window = vec_ref.shape[1]

    @pl.when(first)
    def _():
        dgf_ref[...] = jnp.zeros_like(dgf_ref)
        dgs_ref[...] = jnp.zeros_like(dgs_ref)
        sums_ref[...] = jnp.zeros_like(sums_ref)

    @pl.when(c == 0)
    def _():
        cext[rows : rows + 8, :] = jnp.zeros((8, window), F32)

    @pl.when(c > 0)
    def _():
        cext[rows : rows + 8, :] = cext[0:8, :]

    prev = jnp.where(at_start, halo_ref[...].astype(F32), prev_ref[...].astype(F32))
    vec = vec_ref[...]
    conved, rounded, rate_pre, open_pre = conv_and_gates(inner_ref, prev, vec, gwf_ref, gws_ref, ext, block, own)
    keep = keep_ref[...]
    conv = conved[:, :own]
    rate = jax.nn.sigmoid(rate_pre)
    opening = jax.nn.sigmoid(open_pre)
    factor = vec[7:8, :own]
    log_decay = factor * rate
    e = jnp.exp(log_decay)
    root = jnp.sqrt(minus_expm1(2.0 * log_decay))
    scale = keep * root + (1.0 - keep)

    adj = adj_ref[...] + prod_ref[...] * suffix_ref[0:1, :]
    hext[0:8, :] = jnp.where(at_start, jnp.broadcast_to(start_ref[0:1, :], (8, own)), before_ref[...])
    hext[8 : 8 + rows, :] = hidden_ref[...]
    before = hext[7 : 7 + rows, :]
    d_log = keep * (adj * before * e - adj * opening * conv * (e * e) / root)
    direct = adj * scale * opening
    g_rate = (d_log * factor * rate * (1.0 - rate)).astype(BF)
    g_open = (adj * scale * conv * opening * (1.0 - opening)).astype(BF)
    gf = jnp.concatenate([g_rate[:, :block], g_open[:, :block]], axis=1)
    gs = jnp.concatenate([g_rate[:, block:], g_open[:, block:]], axis=1)
    cgrad = jnp.concatenate([dot_cols(gf, gwf_ref[...]), dot_cols(gs, gws_ref[...])], axis=1)
    cgrad = cgrad + jnp.concatenate([direct, jnp.zeros((rows, window - own), F32)], axis=1)
    cext[0:rows, :] = cgrad
    dgf_ref[...] += dot_rows(rounded[:, :block], gf)
    dgs_ref[...] += dot_rows(rounded[:, block:], gs)

    igrad = vec[0:1, :] * cgrad
    for tap in range(1, 4):
        igrad = igrad + vec[tap : tap + 1, :] * cext[tap : tap + rows, :]
    igrad_ref[...] = igrad.astype(BF)

    @pl.when(c == 0)
    def _():
        tail_ref[...] = igrad[rows - HALO :, :]

    head_ref[...] = cgrad[0:8, :]

    def total(x):
        return jnp.sum(x, axis=0, keepdims=True)

    for tap in range(4):
        sums_ref[tap : tap + 1, :] += total(ext[HALO - tap : HALO - tap + rows, :] * cgrad)
    sums_ref[4:5, :] += total(cgrad)
    sums_ref[5:6, :own] += total(g_rate.astype(F32))
    sums_ref[6:7, :own] += total(g_open.astype(F32))
    sums_ref[7:8, :own] += total(d_log * rate)


def lane_blocks(n_dp, n_z):
    return [(d * n_z + z, z * n_dp + d) for d in range(n_dp) for z in range(n_z)]


def to_z(x, n_dp, n_z):
    w = x.shape[1] // (n_dp * n_z)
    pairs = sorted(lane_blocks(n_dp, n_z), key=lambda p: p[1])
    return jnp.concatenate([x[:, a * w : (a + 1) * w] for a, _ in pairs], axis=1)


def from_z(x, n_dp, n_z):
    w = x.shape[1] // (n_dp * n_z)
    return jnp.concatenate([x[:, b * w : (b + 1) * w] for _, b in lane_blocks(n_dp, n_z)], axis=1)


def total(pieces, i, steps):
    q, ax, a, bx, b = pieces
    low = i < steps // 2
    pick = lambda u, v: jnp.where(low, u[...].astype(F32), v[...].astype(F32))
    return q[...] + pick(ax, bx) + pick(a, b)


def inverse(x):
    return lax.rsqrt(jnp.mean(x * x, axis=1, keepdims=True) + EPSILON)


def norm_kernel(gain_ref, *refs, cuts):
    out_ref = refs[-1]
    for k, ref in enumerate(refs[:-1]):

        @pl.when(pl.program_id(0) == k)
        def _(ref=ref):
            x = ref[...].astype(F32)
            out_ref[...] = to_z(x * inverse(x) * gain_ref[...], *cuts).astype(BF)


def mid_kernel(q, ax, a, bx, b, tok_ref, gain_ref, mid_ref, normed_ref, *, cuts):
    i = pl.program_id(0)
    x = tok_ref[...].astype(F32) + from_z(total((q, ax, a, bx, b), i, pl.num_programs(0)), *cuts)
    mid_ref[...] = x
    normed_ref[...] = to_z(x * inverse(x) * gain_ref[...], *cuts).astype(BF)


def norm_back(grad, x, gain):
    inv = inverse(x)
    g = grad * gain
    return inv * g - x * (inv * inv * inv) * jnp.mean(x * g, axis=1, keepdims=True), grad * x * inv


def add_rows(ref, x):
    first = pl.program_id(0) == 0
    terms = jnp.sum(x.reshape(-1, 8, x.shape[1]), axis=0)

    @pl.when(first)
    def _():
        ref[...] = terms

    @pl.when(jnp.logical_not(first))
    def _():
        ref[...] += terms


def mid_back_kernel(q, ax, a, bx, b, mid_ref, cot_ref, gain_ref, grad_ref, low_ref, part_ref, *, cuts):
    i = pl.program_id(0)
    g = from_z(total((q, ax, a, bx, b), i, pl.num_programs(0)), *cuts)
    back, part = norm_back(g, mid_ref[...], gain_ref[...])
    grad = cot_ref[...].astype(F32) + back
    grad_ref[...] = grad
    low_ref[...] = to_z(grad, *cuts).astype(BF)
    add_rows(part_ref, part)


def tok_back_kernel(q, ax, a, bx, b, tok_ref, mid_grad_ref, gain_ref, grad_ref, part_ref, *, cuts):
    i = pl.program_id(0)
    g = from_z(total((q, ax, a, bx, b), i, pl.num_programs(0)), *cuts)
    back, part = norm_back(g, tok_ref[...].astype(F32), gain_ref[...])
    grad_ref[...] = mid_grad_ref[...] + back
    add_rows(part_ref, part)


def out_kernel(q, ax, a, bx, b, mid_ref, out_ref):
    out_ref[...] = mid_ref[...] + total((q, ax, a, bx, b), pl.program_id(0), pl.num_programs(0))


class OwnRows:
    def __init__(self, rows, width, steps=4):
        self.rows, self.width, self.steps = rows, width, steps

    def call(self, kernel, pieces, arrays, gain, outs):
        n, step = self.steps, self.rows // self.steps
        tile = pl.BlockSpec((step, self.width), lambda i: (i, 0))
        low = pl.BlockSpec((step, self.width), lambda i: (jnp.minimum(i, n // 2 - 1), 0))
        high = pl.BlockSpec((step, self.width), lambda i: (jnp.maximum(i - n // 2, 0), 0))
        line = pl.BlockSpec((1, self.width), lambda i: (0, 0))
        part = pl.BlockSpec((8, self.width), lambda i: (0, 0))
        shape = jax.ShapeDtypeStruct
        gains = [] if gain is None else [gain.reshape(1, self.width)]
        return pl.pallas_call(
            kernel,
            grid=(n,),
            in_specs=([tile, low, low, high, high] if pieces else []) + [tile] * len(arrays) + [line] * len(gains),
            out_specs=[part if t is None else tile for t in outs],
            out_shape=[
                shape((8, self.width), F32) if t is None else shape((self.rows, self.width), t) for t in outs
            ],
            compiler_params=pltpu.CompilerParams(vmem_limit_bytes=VMEM_BYTES),
        )(*pieces, *arrays, *gains)


def ff_pack_kernel(gate_ref, up_ref, out_ref, *, cuts):
    n_dp, n_z, n_core = cuts
    w = gate_ref.shape[1] // (n_dp * n_z * n_core)
    for d in range(n_dp):
        for c in range(n_core):
            for j, ref in enumerate((gate_ref, up_ref)):
                cols = [((d * n_z + z) * n_core + c) * w for z in range(n_z)]
                x = jnp.concatenate([ref[:, o : o + w].astype(F32) for o in cols], axis=1)
                out_ref[d * n_core + c, :, j * n_z * w : (j + 1) * n_z * w] = x.astype(BF)


def ff_unpack_kernel(x_ref, gate_ref, up_ref, *, cuts):
    n_dp, n_z, n_core = cuts
    w = gate_ref.shape[1] // (n_dp * n_z * n_core)
    for j, ref in enumerate((gate_ref, up_ref)):
        for d in range(n_dp):
            cols = []
            for z in range(n_z):
                for c in range(n_core):
                    o = (j * n_z + z) * w
                    cols.append(x_ref[d * n_core + c, :, o : o + w].astype(F32))
            span = n_z * n_core * w
            ref[:, d * span : (d + 1) * span] = jnp.concatenate(cols, axis=1)


class Blocks:
    def __init__(self, peers, lines, seqs, back):
        self.peers, self.lines, self.seqs, self.back = peers, lines, seqs, back

    def core(self, c):
        return self.peers - 1 - c if self.back else c

    def block(self, d, s, c, core):
        return (jnp.bitwise_xor(c, core[0]) * self.lines + d) * self.seqs + s

    def rows(self, count, width):
        return pl.BlockSpec((count, width), lambda d, s, c, core: (self.block(d, s, self.core(c), core), 0))

    def before(self, count, width, length):
        each = length // count

        def index(d, s, c, core):
            return (self.block(d, s, jnp.maximum(self.core(c) - 1, 0), core) * each + each - 1, 0)

        return pl.BlockSpec((count, width), index)

    def sequence(self, count, width):
        return pl.BlockSpec((count, width), lambda d, s, c, core: (d * self.seqs + s, 0))

    def whole(self, *shape):
        return pl.BlockSpec(shape, lambda d, s, c, core: (0,) * len(shape))

    def call(self, kernel, in_specs, out_specs, out_shape, scratch, *args):
        return pl.pallas_call(
            kernel,
            grid_spec=pltpu.PrefetchScalarGridSpec(
                num_scalar_prefetch=1,
                grid=(self.lines, self.seqs, self.peers),
                in_specs=in_specs,
                out_specs=out_specs,
                scratch_shapes=scratch,
            ),
            out_shape=out_shape,
            compiler_params=pltpu.CompilerParams(vmem_limit_bytes=VMEM_BYTES),
        )(*args)


class Plane:
    def __init__(self, n_dp, n_core):
        self.n_dp, self.n_core = n_dp, n_core
        self.core = lax.axis_index("core")
        self.dp = lax.axis_index("dp")

    def near(self, x, k):
        return lax.ppermute(x, "dp", [(i, i ^ k) for i in range(self.n_dp)])

    def twin(self, x):
        return lax.ppermute(x, "core", [(0, 1), (1, 0)])

    def pieces(self, x):
        half = x.shape[0] // 2
        x1, x2 = self.near(x, 1), self.near(x, 2)
        x3 = jnp.concatenate([self.near(x2[:half], 1), self.near(x1[half:], 2)], axis=0)
        mine = [x, x1, x2, x3]
        return mine + [self.twin(m) for m in mine]

    def gather(self, x):
        return jnp.concatenate(self.pieces(x), axis=0)

    def terms(self, product, rows):
        n = self.n_dp
        order = (3, 1, 2, 0)
        other = {k: self.twin(product((n + k) * rows, (n + k + 1) * rows).astype(BF)) for k in order}
        q = {k: product(k * rows, (k + 1) * rows) + other[k].astype(F32) for k in order}
        return [q[k] for k in range(n)]

    def add_up(self, q):
        half = q[0].shape[0] // 2
        low = lambda x: x.astype(BF)
        a3, b3 = self.near(low(q[3][:half]), 1), self.near(low(q[3][half:]), 2)
        a1, b2 = self.near(low(q[1][:half]), 1), self.near(low(q[2][half:]), 2)
        a = self.near(low(q[2][:half] + a3.astype(F32)), 2)
        b = self.near(low(q[1][half:] + b3.astype(F32)), 1)
        return q[0], a1, a, b2, b

    def scatter(self, product, rows):
        return self.add_up(self.terms(product, rows))

    def in_order(self, x):
        x = jnp.where(self.core == 1, x[::-1], x)
        for bit in (1, 2):
            y = x.reshape(2, self.n_dp // (2 * bit), 2, bit, *x.shape[2:])
            x = jnp.where((self.dp & bit) != 0, y[:, :, ::-1], y).reshape(x.shape)
        return jnp.swapaxes(x, 0, 1)


def body(
    tokens, doc_reset, cotangent, norm_gain, input_proj, branch_proj, conv_kernel, conv_bias, gate_weight, gate_bias,
    decay_param, output_proj, ffn_gain, ffn_gate, ffn_up, ffn_down,
):
    seqs, span, width = tokens.shape
    rows = seqs * span
    n_dp, n_z, n_core = (lax.axis_size(a) for a in EVERY)
    group = n_dp * n_core
    devices = group * n_z
    zi = lax.axis_index("z")
    me = lax.axis_index("dp") * n_core + lax.axis_index("core")
    rec = input_proj.shape[1]
    ff = ffn_gate.shape[1]
    block = gate_weight.shape[2]
    taps = conv_kernel.shape[0]
    drow = input_proj.shape[0]
    frow = ffn_down.shape[0]
    ff_own = ff // group
    blocks = rec // block
    shared = blocks - group
    sharers = group // shared
    part = block // sharers
    lanes = 128 * (-(-part // 128))
    own = block + lanes
    window = 2 * block
    total_rows = group * rows
    lines = n_dp * seqs

    plane = Plane(n_dp, n_core)
    core = plane.core
    core_id = core.astype(jnp.int32).reshape(1)

    def own_columns(w):
        lead = w.shape[0]
        full = w[:, : group * block].reshape(lead, group, block)
        rest = w[:, group * block :].reshape(lead, group, part)
        return jnp.concatenate([full, rest, jnp.zeros((lead, group, lanes - part), w.dtype)], axis=2)

    def window_columns(w):
        lead = w.shape[0]
        full = w[:, : group * block].reshape(lead, group, block)
        rest = w[:, group * block :].reshape(lead, shared, block)
        turned = jnp.stack([jnp.roll(rest, -part * q, axis=2) for q in range(sharers)], axis=2)
        return jnp.concatenate([full, turned.reshape(lead, group, block)], axis=2)

    def exchange(x):
        return lax.all_to_all(x, GROUP, split_axis=0, concat_axis=0, tiled=True)

    def to_members(x):
        y = jnp.swapaxes(x, 0, 1)
        return exchange(y.reshape(group * x.shape[0], x.shape[2]))

    def sum_z(x):
        return lax.psum_scatter(x, "z", scatter_dimension=0, tiled=True)

    def over_z(x):
        return lax.all_gather(x, "z", axis=0, tiled=True)

    cuts = (n_dp, n_z)
    cot = cotangent.reshape(rows, width)
    tok = tokens.reshape(rows, width)
    tok_pieces = plane.pieces(tok)
    sent_in = to_members(window_columns(input_proj))
    w_in = over_z(sent_in)
    both = jnp.concatenate([own_columns(branch_proj), own_columns(output_proj.T)], axis=2)
    rrow = rec // devices
    small = jnp.concatenate(
        [
            gate_weight.reshape(-1), norm_gain, ffn_gain, conv_kernel.reshape(-1), conv_bias, gate_bias.reshape(-1),
            decay_param,
        ]
    )
    small_len = small.shape[0]
    marks = (1 - doc_reset).astype(BF).reshape(-1, 256)
    small = jnp.pad(small, (0, -small_len % 256)).reshape(-1, 256)
    marks_at = small.shape[0]
    small = jnp.concatenate([small, marks])
    small = jnp.pad(small, ((0, -small.shape[0] % 32), (0, 0)))
    packed = small.shape[0]
    small = over_z(after(small, sent_in))
    sent_both = to_members(after(both, small, tok_pieces[1], tok_pieces[2]))
    w_both = over_z(sent_both)
    w_branch, w_out = w_both[:, :own], w_both[:, own:]
    small = plane.gather(small).reshape(n_core, n_dp, n_z, packed, 256)
    keep = lax.dynamic_index_in_dim(small, zi, 2, False)[:, :, marks_at : marks_at + rows // 256]
    keep = keep.astype(F32).reshape(total_rows, 1)
    small = jnp.swapaxes(plane.in_order(small), 1, 2).reshape(devices, packed * 256)
    gates_len = 2 * rrow * block
    gates_all = small[:, :gates_len].reshape(devices, 2, rrow, block)
    gates_all = jnp.swapaxes(gates_all, 0, 1).reshape(2, rec, block)
    rest = small[:, gates_len:small_len].astype(F32)
    gain = rest[:, :drow].reshape(width)
    fgain = rest[:, drow : 2 * drow].reshape(width)
    ff_packed = pl.pallas_call(
        functools.partial(ff_pack_kernel, cuts=(n_dp, n_z, n_core)),
        out_shape=jax.ShapeDtypeStruct((group, drow, 2 * ff_own), BF),
        compiler_params=pltpu.CompilerParams(vmem_limit_bytes=VMEM_BYTES),
    )(ffn_gate, ffn_up)
    sent_ff = exchange(after(ff_packed.reshape(group * drow, 2 * ff_own), tok_pieces[3], gain))
    w_ff = over_z(sent_ff)
    w_down = over_z(after(ffn_down, sent_ff))

    chan = rest[:, 2 * drow :].reshape(devices, taps + 4, rrow)
    chan = jnp.swapaxes(chan, 0, 1).reshape(taps + 4, rec)
    lam = chan[taps + 3 :]
    chan = jnp.concatenate([chan[: taps + 3], -POWER * jax.nn.softplus(-lam)], axis=0)

    quarter = me % sharers
    shared_at = (group + me // sharers) * block

    def my_window(x, axis):
        full = lax.dynamic_slice_in_dim(x, me * block, block, axis)
        other = lax.dynamic_slice_in_dim(x, shared_at, block, axis)
        turned = lax.dynamic_slice_in_dim(jnp.concatenate([other, other], axis), quarter * part, block, axis)
        return full, turned

    vec = jnp.concatenate(my_window(chan, 1), axis=1)
    gw_full, gw_shared = my_window(gates_all, 1)
    gw_shared = lax.dynamic_slice_in_dim(gw_shared, quarter * part, part, 2)
    gw_shared = jnp.pad(gw_shared, ((0, 0), (0, 0), (0, lanes - part)))
    gwf = jnp.concatenate([gw_full[0], gw_full[1]], axis=1)
    gws = jnp.concatenate([gw_shared[0], gw_shared[1]], axis=1)

    mine = OwnRows(rows, width)
    normed = pl.pallas_call(
        functools.partial(norm_kernel, cuts=cuts),
        grid=(group,),
        in_specs=[pl.BlockSpec((1, width), lambda i: (0, 0))] + [pl.BlockSpec((rows, width), lambda i: (0, 0))] * group,
        out_specs=pl.BlockSpec((rows, width), lambda i: (i, 0)),
        out_shape=jax.ShapeDtypeStruct((total_rows, width), BF),
        compiler_params=pltpu.CompilerParams(vmem_limit_bytes=VMEM_BYTES),
    )(gain.reshape(1, width), *tok_pieces)
    cot_all = plane.gather(after(cot, sent_ff))

    inner = dot(normed, w_in).astype(BF)
    branch = dot(normed, w_branch)
    ends = inner.reshape(n_core, n_dp, seqs, span, window)[:, :, :, span - HALO :]
    ends = jnp.where(core == 1, ends[0], ends[1]).reshape(lines * HALO, window)
    halo = lax.ppermute(ends, "z", [(i, i + 1) for i in range(n_z - 1)])

    at = Blocks(n_core, n_dp, seqs, False)
    seq_in = [
        lambda b: b.rows(span, window), lambda b: b.before(HALO, window, span), lambda b: b.sequence(HALO, window),
        lambda b: b.rows(span, 1), lambda b: b.whole(8, window), lambda b: b.whole(block, window),
        lambda b: b.whole(block, 2 * lanes),
    ]
    row_f32 = jax.ShapeDtypeStruct((total_rows, own), F32)
    decay, local, cum, last = at.call(
        functools.partial(forward_kernel, block=block, own=own),
        [f(at) for f in seq_in],
        [at.rows(span, own)] * 3 + [at.sequence(8, own)],
        [row_f32] * 3 + [jax.ShapeDtypeStruct((lines * 8, own), F32)],
        [pltpu.VMEM((span + HALO, window), F32), pltpu.VMEM((span, own), F32), pltpu.VMEM((8, own), F32)],
        core_id, inner, inner, halo, keep, vec, gwf, gws,
    )

    def carried(x, way, beside):
        x = x.reshape(lines, 8, own)[:, :2]
        state = jnp.zeros((lines, own), F32)
        for k in range(n_z - 1, 0, -1):
            hops = [(i, i + way * k) for i in range(n_z) if 0 <= i + way * k < n_z]
            come = after(lax.ppermute(x, "z", hops), *beside)
            state = come[:, 1] * state + come[:, 0]
        return state

    start = carried(last, 1, [branch])

    def by_line(x):
        return x.reshape(1, n_dp, seqs, 1, own)

    def spread(x):
        return x.reshape(n_core, n_dp, seqs, span, own)

    hidden = (spread(local) + spread(cum) * by_line(start)).reshape(total_rows, own)
    mixed_out = (hidden * gelu_only(branch)).astype(BF)
    terms = plane.scatter(lambda lo, hi: dot_cols(mixed_out[lo:hi], w_out), rows)
    mid, fnormed = mine.call(functools.partial(mid_kernel, cuts=cuts), terms, [tok], fgain, [F32, BF])

    fnormed = plane.gather(fnormed)
    pre_lin = dot(fnormed, w_ff)
    act, slope = gelu_pair(pre_lin[:, :ff_own])
    lin = pre_lin[:, ff_own:]
    fhidden = (act * lin).astype(BF)
    down_terms = dot_rows(fhidden, cot_all).astype(BF)
    hid_grad = dot_cols(after(cot_all, down_terms), w_down)
    fgrad = jnp.concatenate([(hid_grad * lin * slope).astype(BF), (hid_grad * act).astype(BF)], axis=1)
    down_sum = sum_z(down_terms)
    down_out = down_sum.astype(F32)
    ff_terms = dot_rows(fnormed, fgrad).astype(BF)
    terms = plane.scatter(lambda lo, hi: dot_cols(fgrad[lo:hi], w_ff), rows)
    ff_sum = sum_z(after(ff_terms, down_sum))
    ff_part = exchange(ff_sum).reshape(group, drow, 2 * ff_own)
    terms = (after(terms[0], down_sum, ff_terms), *terms[1:])
    mid_grad, mid_low, ffn_gain_part = mine.call(
        functools.partial(mid_back_kernel, cuts=cuts), terms, [mid, cot], fgain, [F32, BF, None]
    )
    mid_low = plane.gather(mid_low)
    later = after(fhidden, mid_grad)
    out_terms = plane.terms(lambda lo, hi: dot(later[lo:hi], w_down), rows)
    mid_low = after(mid_low, *out_terms)
    out_terms[3] = after(out_terms[3], mid_low)
    layer_out = mine.call(out_kernel, plane.add_up(out_terms), [mid], None, [F32])[0]

    gate_out, up_out = pl.pallas_call(
        functools.partial(ff_unpack_kernel, cuts=(n_dp, n_z, n_core)),
        out_shape=[jax.ShapeDtypeStruct((drow, ff), F32)] * 2,
        compiler_params=pltpu.CompilerParams(vmem_limit_bytes=VMEM_BYTES),
    )(ff_part)

    mixed_grad = dot(mid_low, w_out)
    act_r, slope_r = gelu_pair(branch)
    branch_grad = (mixed_grad * hidden * slope_r).astype(BF)
    back = Blocks(n_core, n_dp, seqs, True)
    adj, prod, front = back.call(
        functools.partial(reverse_kernel, own=own),
        [back.rows(span, own)] * 3,
        [back.rows(span, own)] * 2 + [back.sequence(8, own)],
        [row_f32] * 2 + [jax.ShapeDtypeStruct((lines * 8, own), F32)],
        [pltpu.VMEM((8, own), F32)],
        core_id, after(decay, ff_sum), mixed_grad, branch,
    )
    both = jnp.concatenate([dot_rows(normed, branch_grad).astype(BF), dot_rows(mid_low, mixed_out).astype(BF)], axis=1)
    suffix = carried(front, -1, [both])

    def eight(x):
        return jnp.broadcast_to(x[:, None, :], (lines, 8, own)).reshape(lines * 8, own)

    igrad, tail, head, dgf, dgs, sums = back.call(
        functools.partial(backward_kernel, block=block, own=own),
        [f(back) for f in seq_in]
        + [
            back.rows(span, own), back.before(8, own, span), back.sequence(8, own), back.rows(span, own),
            back.rows(span, own), back.sequence(8, own),
        ],
        [
            back.rows(span, window), back.sequence(HALO, window), back.sequence(8, window), back.whole(block, window),
            back.whole(block, 2 * lanes), back.whole(8, window),
        ],
        [
            jax.ShapeDtypeStruct((total_rows, window), BF), jax.ShapeDtypeStruct((lines * HALO, window), F32),
            jax.ShapeDtypeStruct((lines * 8, window), F32), jax.ShapeDtypeStruct((block, window), F32),
            jax.ShapeDtypeStruct((block, 2 * lanes), F32), jax.ShapeDtypeStruct((8, window), F32),
        ],
        [
            pltpu.VMEM((span + HALO, window), F32), pltpu.VMEM((span + 8, own), F32), pltpu.VMEM((span + 8, window), F32),
        ],
        core_id, inner, inner, halo, keep, vec, gwf, gws, hidden, hidden, eight(start), adj, prod, eight(suffix),
    )

    coming = lax.ppermute(head.astype(BF), "z", [(i + 1, i) for i in range(n_z - 1)]).astype(F32).reshape(lines, 8, window)
    fix = jnp.zeros((lines, HALO, window), F32)
    for tap in range(1, taps):
        fix = fix.at[:, HALO - tap :, :].add(vec[tap] * coming[:, :tap])
    tail = (tail.reshape(lines, HALO, window) + fix).astype(BF).reshape(1, n_dp, seqs, HALO, window)
    igrad = lax.dynamic_update_slice(
        igrad.reshape(n_core, n_dp, seqs, span, window), tail, (1 - core, 0, 0, span - HALO, 0)
    ).reshape(total_rows, window)
    both_sum = sum_z(after(both, ff_sum))
    igrad = after(igrad, layer_out, both_sum)
    in_terms = dot_rows(normed, igrad).astype(BF)
    igrad = after(igrad, in_terms)
    terms = plane.scatter(
        lambda lo, hi: dot_cols(igrad[lo:hi], w_in) + dot_cols(branch_grad[lo:hi], w_branch), rows
    )
    both_part = exchange(both_sum).reshape(group, drow, 2 * own)

    def own_natural(x):
        full = jnp.swapaxes(x[:, :, :block], 0, 1).reshape(drow, group * block)
        rest = jnp.swapaxes(x[:, :, block : block + part], 0, 1).reshape(drow, group * part)
        return jnp.concatenate([full, rest], axis=1).astype(F32)

    branch_proj_grad = own_natural(both_part[:, :, :own])
    output_proj_grad = own_natural(both_part[:, :, own:]).T

    def place_window(x, axis_len):
        lead = x.shape[:-1]
        other = x[..., block:]
        turned = lax.dynamic_slice_in_dim(
            jnp.concatenate([other, other], -1), lax.rem(block - quarter * part, block), block, x.ndim - 1
        )
        y = jnp.zeros((*lead, axis_len), x.dtype)
        y = lax.dynamic_update_slice_in_dim(y, x[..., :block], me * block, x.ndim - 1)
        return lax.dynamic_update_slice_in_dim(y, turned, shared_at, x.ndim - 1)

    dg_full = jnp.stack([dgf[:, :block], dgf[:, block:]])
    dg_shared = jnp.stack([dgs[:, :part], dgs[:, lanes : lanes + part]])
    dg_shared = lax.dynamic_slice_in_dim(
        jnp.concatenate([dg_shared, dg_shared], 1), lax.rem(block - quarter * part, block), block, 1
    )
    lot = n_core * rrow
    lots = (block + 2 * lot - 2) // lot

    def by_z(x, row):
        y = jnp.swapaxes(x, 0, 1).reshape(block, -1).astype(BF)
        q = row // lot
        y = lax.dynamic_update_slice(jnp.zeros((n_z * lot, y.shape[1]), BF), y, (row - q * lot, 0))
        y = y.reshape(n_z, lot, -1)
        return lax.dynamic_slice_in_dim(jnp.concatenate([y, y]), lax.rem(n_z - lax.rem(q, n_z), n_z), n_z, 0)

    def to_lines(x, row):
        q = row // lot
        q = q + lax.rem(zi + n_z - lax.rem(q, n_z), n_z)
        y = jnp.zeros((n_dp, *x.shape), x.dtype)
        return lax.dynamic_update_slice(y, x[None], (jnp.minimum(q // n_z, n_dp - 1), 0, 0))

    assert lots <= n_z
    gates = jnp.concatenate([by_z(dg_full, me * block), by_z(dg_shared, shared_at)], axis=2)
    gates = sum_z(after(gates.reshape(n_z * lot, 2 * (block + part)), both_sum))
    in_part = exchange(sum_z(after(in_terms, gates))).reshape(group, drow, window)
    gates = jnp.concatenate(
        [to_lines(gates[:, : 2 * block], me * block), to_lines(gates[:, 2 * block :], shared_at)], axis=2
    )
    gates = exchange(gates.reshape(group * rrow, 2 * (block + part))).reshape(group, rrow, 2 * (block + part)).astype(F32)
    terms = (after(terms[0], gates, both_part, gate_out, up_out), *terms[1:])
    input_grad, gain_part = mine.call(
        functools.partial(tok_back_kernel, cuts=cuts), terms, [tok, mid_grad], gain, [F32, None]
    )

    lane = jnp.arange(window)
    mine = lane < block + part
    sums = jnp.where(jnp.concatenate([jnp.ones((5, window), bool), jnp.broadcast_to(mine, (3, window))], axis=0), sums, 0.0)
    sums = place_window(sums, rec)
    sums = jnp.concatenate([sums[:7], sums[7:8] * (POWER * jax.nn.sigmoid(-lam))], axis=0)
    vectors = jnp.concatenate(
        [
            jnp.sum(gain_part, axis=0).reshape(devices, drow), jnp.sum(ffn_gain_part, axis=0).reshape(devices, drow),
            jnp.swapaxes(sums.reshape(8, devices, rrow), 0, 1).reshape(devices, 8 * rrow),
        ],
        axis=1,
    )
    vec_len = vectors.shape[1]
    vectors = lax.all_to_all(vectors, EVERY, split_axis=0, concat_axis=0, tiled=True)
    vectors = jnp.sum(vectors.reshape(devices, vec_len), axis=0)
    gain_out = vectors[:drow]
    fgain_out = vectors[drow : 2 * drow]
    chan_out = vectors[2 * drow :].reshape(8, rrow)

    gates_out = jnp.sum(gates[:, :, : 2 * block], axis=0).reshape(rrow, 2, block)
    rest = jnp.sum(gates[:, :, 2 * block :].reshape(shared, sharers, rrow, 2, part), axis=0)
    rest = jnp.transpose(rest, (1, 2, 0, 3)).reshape(rrow, 2, block)
    gates_out = jnp.swapaxes(gates_out + rest, 0, 1)

    full = jnp.swapaxes(in_part[:, :, :block], 0, 1).reshape(drow, group * block).astype(F32)
    turned = in_part[:, :, block:window].astype(F32).reshape(shared, sharers, drow, block)
    other = sum(jnp.roll(turned[:, q], part * q, axis=2) for q in range(sharers))
    input_proj_grad = jnp.concatenate([full, jnp.swapaxes(other, 0, 1).reshape(drow, shared * block)], axis=1)

    return (
        layer_out.reshape(seqs, span, width),
        input_grad.reshape(seqs, span, width),
        gain_out,
        input_proj_grad,
        branch_proj_grad,
        chan_out[:taps],
        chan_out[taps],
        gates_out,
        chan_out[taps + 1 : taps + 3],
        chan_out[taps + 3],
        output_proj_grad,
        fgain_out,
        gate_out,
        up_out,
        down_out,
    )


def solution(mesh):
    n_dp, n_seq = mesh.shape["dp"], mesh.shape["seq"]
    split = Mesh(mesh.devices.reshape(n_dp, n_seq // 2, 2), EVERY)
    seq = ("z", "core")
    line = P("dp", seq, None)
    first = P(EVERY)
    rows = P(EVERY, None)
    cols = P(None, EVERY)
    mids = P(None, EVERY, None)
    return jax.shard_map(
        body,
        mesh=split,
        in_specs=(
            line, P("dp", seq), line, first, rows, rows, cols, first, mids, cols, first, cols, first, rows, rows, rows,
        ),
        out_specs=(
            line, line, first, rows, rows, cols, first, mids, cols, first, cols, first, rows, rows, rows,
        ),
        check_vma=False,
    )
```

```python
import functools

import jax
import jax.numpy as jnp
from jax import lax
from jax.experimental import pallas as pl
from jax.experimental.pallas import tpu as pltpu
from jax.sharding import Mesh
from jax.sharding import PartitionSpec as P

EPSILON = 1e-06
POWER = 8.0
BF = jnp.bfloat16
F32 = jnp.float32
GROUP = ("dp", "core")
EVERY = ("dp", "z", "core")
GELU_A = 0.7978845608028654
GELU_B = 0.044715
HALO = 16
VMEM_BYTES = 48 * 1024 * 1024


def after(x, *others):
    return lax.optimization_barrier((x, *others))[0]


def gelu_pair(x):
    x2 = x * x
    th = jnp.tanh(GELU_A * (x + GELU_B * x2 * x))
    half = 0.5 * (1.0 + th)
    slope = half + 0.5 * x * (1.0 - th * th) * (GELU_A * (1.0 + 3.0 * GELU_B * x2))
    return x * half, slope


def gelu_only(x):
    return 0.5 * x * (1.0 + jnp.tanh(GELU_A * (x + GELU_B * x * x * x)))


def dot(a, b):
    return lax.dot_general(a, b, (((1,), (0,)), ((), ())), preferred_element_type=F32)


def dot_rows(a, b):
    return lax.dot_general(a, b, (((0,), (0,)), ((), ())), preferred_element_type=F32)


def dot_cols(a, b):
    return lax.dot_general(a, b, (((1,), (1,)), ((), ())), preferred_element_type=F32)


def minus_expm1(x):
    series = -x * (1.0 + x * (1 / 2) * (1.0 + x * (1 / 3) * (1.0 + x * (1 / 4) * (1.0 + x * (1 / 5) * (1.0 + x * (1 / 6))))))
    return jnp.where(x > -0.125, series, 1.0 - jnp.exp(x))


def conv_and_gates(inner_ref, prev, vec, gwf_ref, gws_ref, ext, block, own):
    rows = inner_ref.shape[0]
    ext[0:HALO, :] = prev.astype(F32)
    ext[HALO : HALO + rows, :] = inner_ref[...].astype(F32)
    conved = vec[4:5, :] + vec[0:1, :] * ext[HALO : HALO + rows, :]
    for tap in range(1, 4):
        conved = conved + vec[tap : tap + 1, :] * ext[HALO - tap : HALO - tap + rows, :]
    rounded = conved.astype(BF)
    gf = dot(rounded[:, :block], gwf_ref[...])
    gs = dot(rounded[:, block:], gws_ref[...])
    part = own - block
    rate_pre = jnp.concatenate([gf[:, :block], gs[:, :part]], axis=1) + vec[5:6, :own]
    open_pre = jnp.concatenate([gf[:, block:], gs[:, part:]], axis=1) + vec[6:7, :own]
    return conved, rounded, rate_pre, open_pre


def scan_groups(a_ref, b_ref, out_h, out_c, h, c, rows, width):
    place = lax.broadcasted_iota(jnp.int32, (8, width), 0)

    def one(g, carry):
        h, c = carry
        at = pl.ds(pl.multiple_of(g * 8, 8), 8)
        a, b = a_ref[at, :], b_ref[at, :]
        for shift in (1, 2, 4):
            keep = place >= shift
            pa = jnp.where(keep, pltpu.roll(a, shift, 0), 1.0)
            pb = jnp.where(keep, pltpu.roll(b, shift, 0), 0.0)
            b = a * pb + b
            a = a * pa
        b = b + a * h
        a = a * c
        out_h[at, :] = b
        out_c[at, :] = a
        return b[7:8, :], a[7:8, :]

    return lax.fori_loop(0, rows // 8, one, (h, c), unroll=4)


def forward_kernel(
    core_ref, inner_ref, prev_ref, halo_ref, keep_ref, vec_ref, gwf_ref, gws_ref,
    decay_ref, local_ref, cum_ref, last_ref, ext, b_ref, carry, *, block, own,
):
    c = pl.program_id(2)
    rows = inner_ref.shape[0]
    prev = jnp.where(c == 0, halo_ref[...].astype(F32), prev_ref[...].astype(F32))
    vec = vec_ref[...]
    conved, _, rate_pre, open_pre = conv_and_gates(inner_ref, prev, vec, gwf_ref, gws_ref, ext, block, own)
    keep = keep_ref[...]
    rate = jax.nn.sigmoid(rate_pre)
    opening = jax.nn.sigmoid(open_pre)
    log_decay = vec[7:8, :own] * rate
    scale = keep * jnp.sqrt(minus_expm1(2.0 * log_decay)) + (1.0 - keep)
    decay_ref[...] = jnp.exp(log_decay) * keep
    b_ref[...] = scale * opening * conved[:, :own]

    @pl.when(c == 0)
    def _():
        carry[0:1, :] = jnp.zeros((1, own), F32)
        carry[1:2, :] = jnp.ones((1, own), F32)

    h, p = scan_groups(decay_ref, b_ref, local_ref, cum_ref, carry[0:1, :], carry[1:2, :], rows, own)
    carry[0:1, :] = h
    carry[1:2, :] = p
    last_ref[...] = carry[...]


def reverse_kernel(core_ref, decay_ref, grad_ref, branch_ref, adj_ref, prod_ref, first_ref, carry, *, own):
    c = pl.program_id(2)
    rows = decay_ref.shape[0]
    place = lax.broadcasted_iota(jnp.int32, (8, own), 0)

    @pl.when(c == 0)
    def _():
        carry[0:1, :] = jnp.zeros((1, own), F32)
        carry[1:2, :] = jnp.ones((1, own), F32)

    def one(i, state):
        s, p = state
        at = pl.ds(pl.multiple_of((rows // 8 - 1 - i) * 8, 8), 8)
        a = decay_ref[at, :]
        hg = grad_ref[at, :] * gelu_only(branch_ref[at, :])
        b = a * hg
        for shift in (1, 2, 4):
            keep = place < 8 - shift
            na = jnp.where(keep, pltpu.roll(a, 8 - shift, 0), 1.0)
            nb = jnp.where(keep, pltpu.roll(b, 8 - shift, 0), 0.0)
            b = a * nb + b
            a = a * na
        b = b + a * s
        a = a * p
        last = place == 7
        adj_ref[at, :] = hg + jnp.where(last, s, pltpu.roll(b, 7, 0))
        prod_ref[at, :] = jnp.where(last, p, pltpu.roll(a, 7, 0))
        return b[0:1, :], a[0:1, :]

    s, p = lax.fori_loop(0, rows // 8, one, (carry[0:1, :], carry[1:2, :]), unroll=4)
    carry[0:1, :] = s
    carry[1:2, :] = p
    first_ref[...] = carry[...]


def backward_kernel(
    core_ref, inner_ref, prev_ref, halo_ref, keep_ref, vec_ref, gwf_ref, gws_ref, hidden_ref, before_ref, start_ref,
    adj_ref, prod_ref, suffix_ref,
    igrad_ref, tail_ref, head_ref, dgf_ref, dgs_ref, sums_ref, ext, hext, cext, *, block, own,
):
    c = pl.program_id(2)
    peers = pl.num_programs(2)
    first = (pl.program_id(0) == 0) & (pl.program_id(1) == 0) & (c == 0)
    at_start = c == peers - 1
    rows = inner_ref.shape[0]
    part = own - block
    window = vec_ref.shape[1]

    @pl.when(first)
    def _():
        dgf_ref[...] = jnp.zeros_like(dgf_ref)
        dgs_ref[...] = jnp.zeros_like(dgs_ref)
        sums_ref[...] = jnp.zeros_like(sums_ref)

    @pl.when(c == 0)
    def _():
        cext[rows : rows + 8, :] = jnp.zeros((8, window), F32)

    @pl.when(c > 0)
    def _():
        cext[rows : rows + 8, :] = cext[0:8, :]

    prev = jnp.where(at_start, halo_ref[...].astype(F32), prev_ref[...].astype(F32))
    vec = vec_ref[...]
    conved, rounded, rate_pre, open_pre = conv_and_gates(inner_ref, prev, vec, gwf_ref, gws_ref, ext, block, own)
    keep = keep_ref[...]
    conv = conved[:, :own]
    rate = jax.nn.sigmoid(rate_pre)
    opening = jax.nn.sigmoid(open_pre)
    factor = vec[7:8, :own]
    log_decay = factor * rate
    e = jnp.exp(log_decay)
    root = jnp.sqrt(minus_expm1(2.0 * log_decay))
    scale = keep * root + (1.0 - keep)

    adj = adj_ref[...] + prod_ref[...] * suffix_ref[0:1, :]
    hext[0:8, :] = jnp.where(at_start, jnp.broadcast_to(start_ref[0:1, :], (8, own)), before_ref[...])
    hext[8 : 8 + rows, :] = hidden_ref[...]
    before = hext[7 : 7 + rows, :]
    d_log = keep * (adj * before * e - adj * opening * conv * (e * e) / root)
    direct = adj * scale * opening
    g_rate = (d_log * factor * rate * (1.0 - rate)).astype(BF)
    g_open = (adj * scale * conv * opening * (1.0 - opening)).astype(BF)
    gf = jnp.concatenate([g_rate[:, :block], g_open[:, :block]], axis=1)
    gs = jnp.concatenate([g_rate[:, block:], g_open[:, block:]], axis=1)
    cgrad = jnp.concatenate([dot_cols(gf, gwf_ref[...]), dot_cols(gs, gws_ref[...])], axis=1)
    cgrad = cgrad + jnp.concatenate([direct, jnp.zeros((rows, window - own), F32)], axis=1)
    cext[0:rows, :] = cgrad
    dgf_ref[...] += dot_rows(rounded[:, :block], gf)
    dgs_ref[...] += dot_rows(rounded[:, block:], gs)

    igrad = vec[0:1, :] * cgrad
    for tap in range(1, 4):
        igrad = igrad + vec[tap : tap + 1, :] * cext[tap : tap + rows, :]
    igrad_ref[...] = igrad.astype(BF)

    @pl.when(c == 0)
    def _():
        tail_ref[...] = igrad[rows - HALO :, :]

    head_ref[...] = cgrad[0:8, :]

    def total(x):
        return jnp.sum(x, axis=0, keepdims=True)

    for tap in range(4):
        sums_ref[tap : tap + 1, :] += total(ext[HALO - tap : HALO - tap + rows, :] * cgrad)
    sums_ref[4:5, :] += total(cgrad)
    sums_ref[5:6, :own] += total(g_rate.astype(F32))
    sums_ref[6:7, :own] += total(g_open.astype(F32))
    sums_ref[7:8, :own] += total(d_log * rate)


def lane_blocks(n_dp, n_z):
    return [(d * n_z + z, z * n_dp + d) for d in range(n_dp) for z in range(n_z)]


def to_z(x, n_dp, n_z):
    w = x.shape[1] // (n_dp * n_z)
    pairs = sorted(lane_blocks(n_dp, n_z), key=lambda p: p[1])
    return jnp.concatenate([x[:, a * w : (a + 1) * w] for a, _ in pairs], axis=1)


def from_z(x, n_dp, n_z):
    w = x.shape[1] // (n_dp * n_z)
    return jnp.concatenate([x[:, b * w : (b + 1) * w] for _, b in lane_blocks(n_dp, n_z)], axis=1)


def total(pieces, i, steps):
    q, ax, a, bx, b = pieces
    low = i < steps // 2
    pick = lambda u, v: jnp.where(low, u[...].astype(F32), v[...].astype(F32))
    return q[...] + pick(ax, bx) + pick(a, b)


def inverse(x):
    return lax.rsqrt(jnp.mean(x * x, axis=1, keepdims=True) + EPSILON)


def norm_kernel(gain_ref, *refs, cuts):
    out_ref = refs[-1]
    for k, ref in enumerate(refs[:-1]):

        @pl.when(pl.program_id(0) == k)
        def _(ref=ref):
            x = ref[...].astype(F32)
            out_ref[...] = to_z(x * inverse(x) * gain_ref[...], *cuts).astype(BF)


def mid_kernel(q, ax, a, bx, b, tok_ref, gain_ref, mid_ref, normed_ref, *, cuts):
    i = pl.program_id(0)
    x = tok_ref[...].astype(F32) + from_z(total((q, ax, a, bx, b), i, pl.num_programs(0)), *cuts)
    mid_ref[...] = x
    normed_ref[...] = to_z(x * inverse(x) * gain_ref[...], *cuts).astype(BF)


def norm_back(grad, x, gain):
    inv = inverse(x)
    g = grad * gain
    return inv * g - x * (inv * inv * inv) * jnp.mean(x * g, axis=1, keepdims=True), grad * x * inv


def add_rows(ref, x):
    first = pl.program_id(0) == 0
    terms = jnp.sum(x.reshape(-1, 8, x.shape[1]), axis=0)

    @pl.when(first)
    def _():
        ref[...] = terms

    @pl.when(jnp.logical_not(first))
    def _():
        ref[...] += terms


def mid_back_kernel(q, ax, a, bx, b, mid_ref, cot_ref, gain_ref, grad_ref, low_ref, part_ref, *, cuts):
    i = pl.program_id(0)
    g = from_z(total((q, ax, a, bx, b), i, pl.num_programs(0)), *cuts)
    back, part = norm_back(g, mid_ref[...], gain_ref[...])
    grad = cot_ref[...].astype(F32) + back
    grad_ref[...] = grad
    low_ref[...] = to_z(grad, *cuts).astype(BF)
    add_rows(part_ref, part)


def tok_back_kernel(q, ax, a, bx, b, tok_ref, mid_grad_ref, gain_ref, grad_ref, part_ref, *, cuts):
    i = pl.program_id(0)
    g = from_z(total((q, ax, a, bx, b), i, pl.num_programs(0)), *cuts)
    back, part = norm_back(g, tok_ref[...].astype(F32), gain_ref[...])
    grad_ref[...] = mid_grad_ref[...] + back
    add_rows(part_ref, part)


def out_kernel(q, ax, a, bx, b, mid_ref, out_ref):
    out_ref[...] = mid_ref[...] + total((q, ax, a, bx, b), pl.program_id(0), pl.num_programs(0))


class OwnRows:
    def __init__(self, rows, width, steps=4):
        self.rows, self.width, self.steps = rows, width, steps

    def call(self, kernel, pieces, arrays, gain, outs):
        n, step = self.steps, self.rows // self.steps
        tile = pl.BlockSpec((step, self.width), lambda i: (i, 0))
        low = pl.BlockSpec((step, self.width), lambda i: (jnp.minimum(i, n // 2 - 1), 0))
        high = pl.BlockSpec((step, self.width), lambda i: (jnp.maximum(i - n // 2, 0), 0))
        line = pl.BlockSpec((1, self.width), lambda i: (0, 0))
        part = pl.BlockSpec((8, self.width), lambda i: (0, 0))
        shape = jax.ShapeDtypeStruct
        gains = [] if gain is None else [gain.reshape(1, self.width)]
        return pl.pallas_call(
            kernel,
            grid=(n,),
            in_specs=([tile, low, low, high, high] if pieces else []) + [tile] * len(arrays) + [line] * len(gains),
            out_specs=[part if t is None else tile for t in outs],
            out_shape=[
                shape((8, self.width), F32) if t is None else shape((self.rows, self.width), t) for t in outs
            ],
            compiler_params=pltpu.CompilerParams(vmem_limit_bytes=VMEM_BYTES),
        )(*pieces, *arrays, *gains)


def ff_pack_kernel(gate_ref, up_ref, out_ref, *, cuts):
    n_dp, n_z, n_core = cuts
    w = gate_ref.shape[1] // (n_dp * n_z * n_core)
    for d in range(n_dp):
        for c in range(n_core):
            for j, ref in enumerate((gate_ref, up_ref)):
                cols = [((d * n_z + z) * n_core + c) * w for z in range(n_z)]
                x = jnp.concatenate([ref[:, o : o + w].astype(F32) for o in cols], axis=1)
                out_ref[d * n_core + c, :, j * n_z * w : (j + 1) * n_z * w] = x.astype(BF)


def ff_unpack_kernel(x_ref, gate_ref, up_ref, *, cuts):
    n_dp, n_z, n_core = cuts
    w = gate_ref.shape[1] // (n_dp * n_z * n_core)
    for j, ref in enumerate((gate_ref, up_ref)):
        for d in range(n_dp):
            cols = []
            for z in range(n_z):
                for c in range(n_core):
                    o = (j * n_z + z) * w
                    cols.append(x_ref[d * n_core + c, :, o : o + w].astype(F32))
            span = n_z * n_core * w
            ref[:, d * span : (d + 1) * span] = jnp.concatenate(cols, axis=1)


class Blocks:
    def __init__(self, peers, lines, seqs, back):
        self.peers, self.lines, self.seqs, self.back = peers, lines, seqs, back

    def core(self, c):
        return self.peers - 1 - c if self.back else c

    def block(self, d, s, c, core):
        return (jnp.bitwise_xor(c, core[0]) * self.lines + d) * self.seqs + s

    def rows(self, count, width):
        return pl.BlockSpec((count, width), lambda d, s, c, core: (self.block(d, s, self.core(c), core), 0))

    def before(self, count, width, length):
        each = length // count

        def index(d, s, c, core):
            return (self.block(d, s, jnp.maximum(self.core(c) - 1, 0), core) * each + each - 1, 0)

        return pl.BlockSpec((count, width), index)

    def sequence(self, count, width):
        return pl.BlockSpec((count, width), lambda d, s, c, core: (d * self.seqs + s, 0))

    def whole(self, *shape):
        return pl.BlockSpec(shape, lambda d, s, c, core: (0,) * len(shape))

    def call(self, kernel, in_specs, out_specs, out_shape, scratch, *args):
        return pl.pallas_call(
            kernel,
            grid_spec=pltpu.PrefetchScalarGridSpec(
                num_scalar_prefetch=1,
                grid=(self.lines, self.seqs, self.peers),
                in_specs=in_specs,
                out_specs=out_specs,
                scratch_shapes=scratch,
            ),
            out_shape=out_shape,
            compiler_params=pltpu.CompilerParams(vmem_limit_bytes=VMEM_BYTES),
        )(*args)


class Plane:
    def __init__(self, n_dp, n_core):
        self.n_dp, self.n_core = n_dp, n_core
        self.core = lax.axis_index("core")
        self.dp = lax.axis_index("dp")

    def near(self, x, k):
        return lax.ppermute(x, "dp", [(i, i ^ k) for i in range(self.n_dp)])

    def twin(self, x):
        return lax.ppermute(x, "core", [(0, 1), (1, 0)])

    def pieces(self, x, late=()):
        half = x.shape[0] // 2
        x1, x2 = self.near(x, 1), self.near(x, 2)
        if late:
            x1, x2 = lax.optimization_barrier((x1, x2, *late))[:2]
        x3 = jnp.concatenate([self.near(x2[:half], 1), self.near(x1[half:], 2)], axis=0)
        mine = [x, x1, x2, x3]
        return mine + [self.twin(m) for m in mine]

    def gather(self, x, late=()):
        return jnp.concatenate(self.pieces(x, late), axis=0)

    def terms(self, product, rows):
        n = self.n_dp
        halves = ((n // 2, n), (0, n // 2))
        other = [self.twin(product((n + lo) * rows, (n + hi) * rows).astype(BF)) for lo, hi in halves]
        far, near = (product(lo * rows, hi * rows) + x.astype(F32) for (lo, hi), x in zip(halves, other))
        far = far.astype(BF)
        return [x[k * rows : (k + 1) * rows] for x in (near, far) for k in range(n // 2)]

    def send_first(self, q):
        half = q[0].shape[0] // 2
        low = lambda x: x.astype(BF)
        a3, b3 = self.near(q[3][:half], 1), self.near(q[3][half:], 2)
        a1, b2 = self.near(low(q[1][:half]), 1), self.near(q[2][half:], 2)
        return a3, b3, a1, b2

    def add_up(self, q, first=None, late=()):
        half = q[0].shape[0] // 2
        low = lambda x: x.astype(BF)
        a3, b3, a1, b2 = first or self.send_first(q)
        q2, q1 = (after(q[2], *late), after(q[1], *late)) if late else (q[2], q[1])
        self.second = (low(q2[:half].astype(F32) + a3.astype(F32)), low(q1[half:] + b3.astype(F32)))
        a, b = self.near(self.second[0], 2), self.near(self.second[1], 1)
        return q[0], a1, a, b2, b

    def scatter(self, product, rows):
        return self.add_up(self.terms(product, rows))

    def in_order(self, x):
        x = jnp.where(self.core == 1, x[::-1], x)
        for bit in (1, 2):
            y = x.reshape(2, self.n_dp // (2 * bit), 2, bit, *x.shape[2:])
            x = jnp.where((self.dp & bit) != 0, y[:, :, ::-1], y).reshape(x.shape)
        return jnp.swapaxes(x, 0, 1)


def body(
    tokens, doc_reset, cotangent, norm_gain, input_proj, branch_proj, conv_kernel, conv_bias, gate_weight, gate_bias,
    decay_param, output_proj, ffn_gain, ffn_gate, ffn_up, ffn_down,
):
    seqs, span, width = tokens.shape
    rows = seqs * span
    n_dp, n_z, n_core = (lax.axis_size(a) for a in EVERY)
    group = n_dp * n_core
    devices = group * n_z
    zi = lax.axis_index("z")
    me = lax.axis_index("dp") * n_core + lax.axis_index("core")
    rec = input_proj.shape[1]
    ff = ffn_gate.shape[1]
    block = gate_weight.shape[2]
    taps = conv_kernel.shape[0]
    drow = input_proj.shape[0]
    frow = ffn_down.shape[0]
    ff_own = ff // group
    blocks = rec // block
    shared = blocks - group
    sharers = group // shared
    part = block // sharers
    lanes = 128 * (-(-part // 128))
    own = block + lanes
    window = 2 * block
    total_rows = group * rows
    lines = n_dp * seqs

    plane = Plane(n_dp, n_core)
    core = plane.core
    core_id = core.astype(jnp.int32).reshape(1)

    def own_columns(w):
        lead = w.shape[0]
        full = w[:, : group * block].reshape(lead, group, block)
        rest = w[:, group * block :].reshape(lead, group, part)
        return jnp.concatenate([full, rest, jnp.zeros((lead, group, lanes - part), w.dtype)], axis=2)

    def window_columns(w):
        lead = w.shape[0]
        full = w[:, : group * block].reshape(lead, group, block)
        rest = w[:, group * block :].reshape(lead, shared, block)
        turned = jnp.stack([jnp.roll(rest, -part * q, axis=2) for q in range(sharers)], axis=2)
        return jnp.concatenate([full, turned.reshape(lead, group, block)], axis=2)

    def exchange(x):
        return lax.all_to_all(x, GROUP, split_axis=0, concat_axis=0, tiled=True)

    def to_members(x):
        y = jnp.swapaxes(x, 0, 1)
        return exchange(y.reshape(group * x.shape[0], x.shape[2]))

    def sum_z(x):
        return lax.psum_scatter(x, "z", scatter_dimension=0, tiled=True)

    def over_z(x):
        return lax.all_gather(x, "z", axis=0, tiled=True)

    cuts = (n_dp, n_z)
    cot = cotangent.reshape(rows, width)
    tok = tokens.reshape(rows, width)
    tok_pieces = plane.pieces(tok)
    rrow = rec // devices
    small = jnp.concatenate(
        [
            gate_weight.reshape(-1), norm_gain, ffn_gain, conv_kernel.reshape(-1), conv_bias, gate_bias.reshape(-1),
            decay_param,
        ]
    )
    small_len = small.shape[0]
    marks = (1 - doc_reset).astype(BF).reshape(-1, 256)
    small = jnp.pad(small, (0, -small_len % 256)).reshape(-1, 256)
    marks_at = small.shape[0]
    small = jnp.concatenate([small, marks])
    small = jnp.pad(small, ((0, -small.shape[0] % 32), (0, 0)))
    packed = small.shape[0]
    small = over_z(small)
    source, small, *near = lax.optimization_barrier((input_proj, small, *tok_pieces[1:3]))
    sent_in = to_members(window_columns(source))

    def pair(a, b):
        cut = block + part
        return jnp.concatenate([a[..., :block], b[..., :block], a[..., block:cut], b[..., block:cut]], axis=-1)

    def unpair(x, k):
        at = 2 * block + k * part
        return jnp.concatenate([x[..., k * block : (k + 1) * block], x[..., at : at + part]], axis=-1)

    both = pair(own_columns(branch_proj), own_columns(output_proj.T))
    sent_both = to_members(after(both, sent_in))
    ff_packed = pl.pallas_call(
        functools.partial(ff_pack_kernel, cuts=(n_dp, n_z, n_core)),
        out_shape=jax.ShapeDtypeStruct((group, drow, 2 * ff_own), BF),
        compiler_params=pltpu.CompilerParams(vmem_limit_bytes=VMEM_BYTES),
    )(ffn_gate, ffn_up)
    w_in = over_z(sent_in)
    w_both = over_z(sent_both)
    w_branch, w_out = (jnp.pad(unpair(w_both, k), ((0, 0), (0, lanes - part))) for k in range(2))
    small = plane.gather(small).reshape(n_core, n_dp, n_z, packed, 256)
    keep = lax.dynamic_index_in_dim(small, zi, 2, False)[:, :, marks_at : marks_at + rows // 256]
    keep = keep.astype(F32).reshape(total_rows, 1)
    ff_packed, small = lax.optimization_barrier((ff_packed, small))
    sent_ff = exchange(ff_packed.reshape(group * drow, 2 * ff_own))
    gates_len = 2 * rrow * block
    rest = small[:, :, :, gates_len // 256 : marks_at]
    rest = jnp.swapaxes(plane.in_order(rest), 1, 2).reshape(devices, -1)[:, : small_len - gates_len].astype(F32)
    gain = rest[:, :drow].reshape(width)
    fgain = rest[:, drow : 2 * drow].reshape(width)
    chan = rest[:, 2 * drow :].reshape(devices, taps + 4, rrow)
    chan = jnp.swapaxes(chan, 0, 1).reshape(taps + 4, rec)
    lam = chan[taps + 3 :]
    chan = jnp.concatenate([chan[: taps + 3], -POWER * jax.nn.softplus(-lam)], axis=0)

    quarter = me % sharers
    shared_at = (group + me // sharers) * block

    def my_window(x, axis):
        full = lax.dynamic_slice_in_dim(x, me * block, block, axis)
        other = lax.dynamic_slice_in_dim(x, shared_at, block, axis)
        turned = lax.dynamic_slice_in_dim(jnp.concatenate([other, other], axis), quarter * part, block, axis)
        return full, turned

    vec = jnp.concatenate(my_window(chan, 1), axis=1)
    mine = OwnRows(rows, width)
    normed = pl.pallas_call(
        functools.partial(norm_kernel, cuts=cuts),
        grid=(group,),
        in_specs=[pl.BlockSpec((1, width), lambda i: (0, 0))] + [pl.BlockSpec((rows, width), lambda i: (0, 0))] * group,
        out_specs=pl.BlockSpec((rows, width), lambda i: (i, 0)),
        out_shape=jax.ShapeDtypeStruct((total_rows, width), BF),
        compiler_params=pltpu.CompilerParams(vmem_limit_bytes=VMEM_BYTES),
    )(gain.reshape(1, width), *tok_pieces)

    normed, small, sent_ff = lax.optimization_barrier((normed, small, sent_ff))
    gates_all = small[:, :, :, : gates_len // 256].reshape(n_core, n_dp, n_z, 2, rrow * block // 256, 256)
    gates_all = jnp.transpose(plane.in_order(gates_all), (3, 0, 2, 1, 4, 5)).reshape(2, rec, block)
    gw_full, gw_shared = my_window(gates_all, 1)
    gw_shared = lax.dynamic_slice_in_dim(gw_shared, quarter * part, part, 2)
    gw_shared = jnp.pad(gw_shared, ((0, 0), (0, 0), (0, lanes - part)))
    gwf = jnp.concatenate([gw_full[0], gw_full[1]], axis=1)
    gws = jnp.concatenate([gw_shared[0], gw_shared[1]], axis=1)

    w_ff = over_z(sent_ff)
    w_down = over_z(after(ffn_down, sent_ff))
    inner = dot(normed, w_in).astype(BF)
    cot_here, inner = lax.optimization_barrier((cot, inner))
    cot_pieces = plane.pieces(cot_here)
    branch = dot(normed, w_branch)
    ends = inner.reshape(n_core, n_dp, seqs, span, window)[:, :, :, span - HALO :]
    ends = jnp.where(core == 1, ends[0], ends[1]).reshape(lines * HALO, window)
    halo = lax.ppermute(ends, "z", [(i, i + 1) for i in range(n_z - 1)])

    at = Blocks(n_core, n_dp, seqs, False)
    seq_in = [
        lambda b: b.rows(span, window), lambda b: b.before(HALO, window, span), lambda b: b.sequence(HALO, window),
        lambda b: b.rows(span, 1), lambda b: b.whole(8, window), lambda b: b.whole(block, window),
        lambda b: b.whole(block, 2 * lanes),
    ]
    row_f32 = jax.ShapeDtypeStruct((total_rows, own), F32)
    decay, local, cum, last = at.call(
        functools.partial(forward_kernel, block=block, own=own),
        [f(at) for f in seq_in],
        [at.rows(span, own)] * 3 + [at.sequence(8, own)],
        [row_f32] * 3 + [jax.ShapeDtypeStruct((lines * 8, own), F32)],
        [pltpu.VMEM((span + HALO, window), F32), pltpu.VMEM((span, own), F32), pltpu.VMEM((8, own), F32)],
        core_id, inner, inner, halo, keep, vec, gwf, gws,
    )

    def carried(x, way, beside):
        x = x.reshape(lines, 8, own)[:, :2]
        state = jnp.zeros((lines, own), F32)
        for k in range(n_z - 1, 0, -1):
            hops = [(i, i + way * k) for i in range(n_z) if 0 <= i + way * k < n_z]
            come = after(lax.ppermute(x, "z", hops), *beside)
            state = come[:, 1] * state + come[:, 0]
        return state

    start = carried(last, 1, [branch])

    def by_line(x):
        return x.reshape(1, n_dp, seqs, 1, own)

    def spread(x):
        return x.reshape(n_core, n_dp, seqs, span, own)

    hidden = (spread(local) + spread(cum) * by_line(start)).reshape(total_rows, own)
    mixed_out = (hidden * gelu_only(branch)).astype(BF)
    mixed_out, *cot_pieces = lax.optimization_barrier((mixed_out, *cot_pieces))
    terms = plane.scatter(lambda lo, hi: dot_cols(mixed_out[lo:hi], w_out), rows)
    mid, fnormed = mine.call(functools.partial(mid_kernel, cuts=cuts), terms, [tok], fgain, [F32, BF])

    cot_pieces[0] = after(cot_pieces[0], fnormed)
    cot_all = jnp.concatenate(cot_pieces, axis=0)
    fnormed = plane.gather(fnormed, [cot_all])
    pre_lin = dot(fnormed, w_ff)
    act, slope = gelu_pair(pre_lin[:, :ff_own])
    lin = pre_lin[:, ff_own:]
    fhidden = (act * lin).astype(BF)
    down_terms = dot_rows(fhidden, cot_all).astype(BF)
    hid_grad = dot_cols(after(cot_all, down_terms), w_down)
    fgrad = jnp.concatenate([(hid_grad * lin * slope).astype(BF), (hid_grad * act).astype(BF)], axis=1)
    down_sum = sum_z(down_terms)
    down_out = down_sum.astype(F32)
    terms = plane.terms(lambda lo, hi: dot_cols(fgrad[lo:hi], w_ff), rows)
    ff_terms = dot_rows(fnormed, after(fgrad, down_sum, *terms)).astype(BF)
    terms = plane.add_up(terms)
    ff_sum = sum_z(after(ff_terms, down_sum))
    terms = (after(terms[0], down_sum, ff_terms), *terms[1:])
    mid_grad, mid_low, ffn_gain_part = mine.call(
        functools.partial(mid_back_kernel, cuts=cuts), terms, [mid, cot], fgain, [F32, BF, None]
    )
    later = after(fhidden, mid_grad)
    out_terms = plane.terms(lambda lo, hi: dot(later[lo:hi], w_down), rows)
    ffn_gain_part = jnp.sum(ffn_gain_part, axis=0)
    mid_low = plane.gather(mid_low, [*out_terms, ffn_gain_part, down_out])
    out_terms[3] = after(out_terms[3], mid_low)

    mixed_grad = dot(mid_low, w_out)
    act_r, slope_r = gelu_pair(branch)
    branch_grad = (mixed_grad * hidden * slope_r).astype(BF)
    back = Blocks(n_core, n_dp, seqs, True)
    out_first = plane.send_first(out_terms)
    adj, prod, front = back.call(
        functools.partial(reverse_kernel, own=own),
        [back.rows(span, own)] * 3,
        [back.rows(span, own)] * 2 + [back.sequence(8, own)],
        [row_f32] * 2 + [jax.ShapeDtypeStruct((lines * 8, own), F32)],
        [pltpu.VMEM((8, own), F32)],
        core_id, decay, mixed_grad, branch,
    )
    branch_late, mixed_late, *out_first = lax.optimization_barrier((branch_grad, mixed_out, *out_first, adj))[:6]
    out_terms = plane.add_up(out_terms, out_first)
    both = pair(dot_rows(normed, branch_late).astype(BF), dot_rows(mid_low, mixed_late).astype(BF))
    suffix, ff_sum, *out_terms = lax.optimization_barrier((carried(front, -1, [both]), ff_sum, *out_terms))

    def eight(x):
        return jnp.broadcast_to(x[:, None, :], (lines, 8, own)).reshape(lines * 8, own)

    igrad, tail, head, dgf, dgs, sums = back.call(
        functools.partial(backward_kernel, block=block, own=own),
        [f(back) for f in seq_in]
        + [
            back.rows(span, own), back.before(8, own, span), back.sequence(8, own), back.rows(span, own),
            back.rows(span, own), back.sequence(8, own),
        ],
        [
            back.rows(span, window), back.sequence(HALO, window), back.sequence(8, window), back.whole(block, window),
            back.whole(block, 2 * lanes), back.whole(8, window),
        ],
        [
            jax.ShapeDtypeStruct((total_rows, window), BF), jax.ShapeDtypeStruct((lines * HALO, window), F32),
            jax.ShapeDtypeStruct((lines * 8, window), F32), jax.ShapeDtypeStruct((block, window), F32),
            jax.ShapeDtypeStruct((block, 2 * lanes), F32), jax.ShapeDtypeStruct((8, window), F32),
        ],
        [
            pltpu.VMEM((span + HALO, window), F32), pltpu.VMEM((span + 8, own), F32), pltpu.VMEM((span + 8, window), F32),
        ],
        core_id, inner, inner, halo, keep, vec, gwf, gws, hidden, hidden, eight(start), adj, prod, eight(suffix),
    )

    coming = lax.ppermute(head.astype(BF), "z", [(i + 1, i) for i in range(n_z - 1)]).astype(F32).reshape(lines, 8, window)
    fix = jnp.zeros((lines, HALO, window), F32)
    for tap in range(1, taps):
        fix = fix.at[:, HALO - tap :, :].add(vec[tap] * coming[:, :tap])
    tail = (tail.reshape(lines, HALO, window) + fix).astype(BF).reshape(1, n_dp, seqs, HALO, window)
    igrad = lax.dynamic_update_slice(
        igrad.reshape(n_core, n_dp, seqs, span, window), tail, (1 - core, 0, 0, span - HALO, 0)
    ).reshape(total_rows, window)
    ff_part = exchange(ff_sum)
    both_sum = sum_z(after(both, ff_sum))
    in_terms = dot_rows(normed, igrad).astype(BF)
    both_part = exchange(both_sum)
    igrad, in_terms, ff_part = lax.optimization_barrier((igrad, in_terms, ff_part))
    layer_out = mine.call(out_kernel, out_terms, [mid], None, [F32])[0]
    gate_out, up_out = pl.pallas_call(
        functools.partial(ff_unpack_kernel, cuts=(n_dp, n_z, n_core)),
        out_shape=[jax.ShapeDtypeStruct((drow, ff), F32)] * 2,
        compiler_params=pltpu.CompilerParams(vmem_limit_bytes=VMEM_BYTES),
    )(ff_part.reshape(group, drow, 2 * ff_own))
    terms = plane.terms(
        lambda lo, hi: dot_cols(igrad[lo:hi], w_in) + dot_cols(branch_grad[lo:hi], w_branch), rows
    )
    terms = plane.add_up(terms)
    second = plane.second
    first_terms, layer_out, gate_out, up_out, both_part = lax.optimization_barrier(
        (terms[0], layer_out, gate_out, up_out, both_part)
    )
    terms = (first_terms, *terms[1:])
    both_part = both_part.reshape(group, drow, 2 * (block + part))

    def own_natural(x):
        full = jnp.swapaxes(x[:, :, :block], 0, 1).reshape(drow, group * block)
        rest = jnp.swapaxes(x[:, :, block : block + part], 0, 1).reshape(drow, group * part)
        return jnp.concatenate([full, rest], axis=1).astype(F32)

    branch_proj_grad = own_natural(unpair(both_part, 0))
    output_proj_grad = own_natural(unpair(both_part, 1)).T

    def place_window(x, axis_len):
        lead = x.shape[:-1]
        other = x[..., block:]
        turned = lax.dynamic_slice_in_dim(
            jnp.concatenate([other, other], -1), lax.rem(block - quarter * part, block), block, x.ndim - 1
        )
        y = jnp.zeros((*lead, axis_len), x.dtype)
        y = lax.dynamic_update_slice_in_dim(y, x[..., :block], me * block, x.ndim - 1)
        return lax.dynamic_update_slice_in_dim(y, turned, shared_at, x.ndim - 1)

    dg_full = jnp.stack([dgf[:, :block], dgf[:, block:]])
    dg_shared = jnp.stack([dgs[:, :part], dgs[:, lanes : lanes + part]])
    dg_shared = lax.dynamic_slice_in_dim(
        jnp.concatenate([dg_shared, dg_shared], 1), lax.rem(block - quarter * part, block), block, 1
    )
    lot = n_core * rrow
    lots = (block + 2 * lot - 2) // lot

    def by_z(x, row):
        y = jnp.swapaxes(x, 0, 1).reshape(block, -1).astype(BF)
        q = row // lot
        y = lax.dynamic_update_slice(jnp.zeros((n_z * lot, y.shape[1]), BF), y, (row - q * lot, 0))
        y = y.reshape(n_z, lot, -1)
        return lax.dynamic_slice_in_dim(jnp.concatenate([y, y]), lax.rem(n_z - lax.rem(q, n_z), n_z), n_z, 0)

    def to_lines(x, row):
        q = row // lot
        q = q + lax.rem(zi + n_z - lax.rem(q, n_z), n_z)
        y = jnp.zeros((n_dp, *x.shape), x.dtype)
        return lax.dynamic_update_slice(y, x[None], (jnp.minimum(q // n_z, n_dp - 1), 0, 0))

    assert lots <= n_z
    gates = jnp.concatenate([by_z(dg_full, me * block), by_z(dg_shared, shared_at)], axis=2)
    gates = gates.reshape(n_z, lot * 2 * (block + part) // window, window)
    joined = jnp.concatenate([in_terms.reshape(n_z, group * drow, window), gates], axis=1)
    joined = sum_z(after(joined.reshape(-1, window), both_sum))
    joined, first_terms = lax.optimization_barrier((joined, terms[0], *second))[:2]
    terms = (first_terms, *terms[1:])
    in_part = joined[: group * drow].reshape(group, drow, window)
    gates = joined[group * drow :].reshape(lot, 2 * (block + part))
    gates = jnp.concatenate(
        [to_lines(gates[:, : 2 * block], me * block), to_lines(gates[:, 2 * block :], shared_at)], axis=2
    )
    gates = gates.reshape(group, rrow * 2 * (block + part) // window, window)
    joined = exchange(jnp.concatenate([in_part, gates], axis=1).reshape(-1, window))
    input_grad, gain_part = mine.call(
        functools.partial(tok_back_kernel, cuts=cuts), terms, [tok, mid_grad], gain, [F32, None]
    )

    lane = jnp.arange(window)
    mine = lane < block + part
    sums = jnp.where(jnp.concatenate([jnp.ones((5, window), bool), jnp.broadcast_to(mine, (3, window))], axis=0), sums, 0.0)
    sums = place_window(sums, rec)
    sums = jnp.concatenate([sums[:7], sums[7:8] * (POWER * jax.nn.sigmoid(-lam))], axis=0)
    vectors = jnp.concatenate(
        [
            jnp.sum(gain_part, axis=0).reshape(devices, drow), ffn_gain_part.reshape(devices, drow),
            jnp.swapaxes(sums.reshape(8, devices, rrow), 0, 1).reshape(devices, 8 * rrow),
        ],
        axis=1,
    )
    vec_len = vectors.shape[1]
    vectors, joined = lax.optimization_barrier((vectors, joined))
    vectors = lax.all_to_all(vectors, EVERY, split_axis=0, concat_axis=0, tiled=True)
    joined = joined.reshape(group, -1, window)
    in_part = joined[:, :drow]
    gates = joined[:, drow:].reshape(group, rrow, 2 * (block + part)).astype(F32)
    vectors = jnp.sum(vectors.reshape(devices, vec_len), axis=0)
    gain_out = vectors[:drow]
    fgain_out = vectors[drow : 2 * drow]
    chan_out = vectors[2 * drow :].reshape(8, rrow)

    gates_out = jnp.sum(gates[:, :, : 2 * block], axis=0).reshape(rrow, 2, block)
    rest = jnp.sum(gates[:, :, 2 * block :].reshape(shared, sharers, rrow, 2, part), axis=0)
    rest = jnp.transpose(rest, (1, 2, 0, 3)).reshape(rrow, 2, block)
    gates_out = jnp.swapaxes(gates_out + rest, 0, 1)

    full = jnp.swapaxes(in_part[:, :, :block], 0, 1).reshape(drow, group * block).astype(F32)
    turned = in_part[:, :, block:window].astype(F32).reshape(shared, sharers, drow, block)
    other = sum(jnp.roll(turned[:, q], part * q, axis=2) for q in range(sharers))
    input_proj_grad = jnp.concatenate([full, jnp.swapaxes(other, 0, 1).reshape(drow, shared * block)], axis=1)

    return (
        layer_out.reshape(seqs, span, width),
        input_grad.reshape(seqs, span, width),
        gain_out,
        input_proj_grad,
        branch_proj_grad,
        chan_out[:taps],
        chan_out[taps],
        gates_out,
        chan_out[taps + 1 : taps + 3],
        chan_out[taps + 3],
        output_proj_grad,
        fgain_out,
        gate_out,
        up_out,
        down_out,
    )


def solution(mesh):
    n_dp, n_seq = mesh.shape["dp"], mesh.shape["seq"]
    split = Mesh(mesh.devices.reshape(n_dp, n_seq // 2, 2), EVERY)
    seq = ("z", "core")
    line = P("dp", seq, None)
    first = P(EVERY)
    rows = P(EVERY, None)
    cols = P(None, EVERY)
    mids = P(None, EVERY, None)
    return jax.shard_map(
        body,
        mesh=split,
        in_specs=(
            line, P("dp", seq), line, first, rows, rows, cols, first, mids, cols, first, cols, first, rows, rows, rows,
        ),
        out_specs=(
            line, line, first, rows, rows, cols, first, mids, cols, first, cols, first, rows, rows, rows,
        ),
        check_vma=False,
    )
```

```python
import functools

import jax
import jax.numpy as jnp
from jax import lax
from jax.experimental import pallas as pl
from jax.experimental.pallas import tpu as pltpu
from jax.sharding import Mesh
from jax.sharding import PartitionSpec as P

EPSILON = 1e-06
POWER = 8.0
BF = jnp.bfloat16
F32 = jnp.float32
GROUP = ("dp", "core")
EVERY = ("dp", "z", "core")
GELU_A = 0.7978845608028654
GELU_B = 0.044715
HALO = 16
VMEM_BYTES = 48 * 1024 * 1024


def after(x, *others):
    return lax.optimization_barrier((x, *others))[0]


def gelu_pair(x):
    x2 = x * x
    th = jnp.tanh(GELU_A * (x + GELU_B * x2 * x))
    half = 0.5 * (1.0 + th)
    slope = half + 0.5 * x * (1.0 - th * th) * (GELU_A * (1.0 + 3.0 * GELU_B * x2))
    return x * half, slope


def gelu_only(x):
    return 0.5 * x * (1.0 + jnp.tanh(GELU_A * (x + GELU_B * x * x * x)))


def dot(a, b):
    return lax.dot_general(a, b, (((1,), (0,)), ((), ())), preferred_element_type=F32)


def dot_rows(a, b):
    return lax.dot_general(a, b, (((0,), (0,)), ((), ())), preferred_element_type=F32)


def dot_cols(a, b):
    return lax.dot_general(a, b, (((1,), (1,)), ((), ())), preferred_element_type=F32)


def minus_expm1(x):
    series = -x * (1.0 + x * (1 / 2) * (1.0 + x * (1 / 3) * (1.0 + x * (1 / 4) * (1.0 + x * (1 / 5) * (1.0 + x * (1 / 6))))))
    return jnp.where(x > -0.125, series, 1.0 - jnp.exp(x))


def conv_and_gates(inner_ref, prev, vec, gwf_ref, gws_ref, ext, block, own):
    rows = inner_ref.shape[0]
    ext[0:HALO, :] = prev.astype(F32)
    ext[HALO : HALO + rows, :] = inner_ref[...].astype(F32)
    conved = vec[4:5, :] + vec[0:1, :] * ext[HALO : HALO + rows, :]
    for tap in range(1, 4):
        conved = conved + vec[tap : tap + 1, :] * ext[HALO - tap : HALO - tap + rows, :]
    rounded = conved.astype(BF)
    gf = dot(rounded[:, :block], gwf_ref[...])
    gs = dot(rounded[:, block:], gws_ref[...])
    part = own - block
    rate_pre = jnp.concatenate([gf[:, :block], gs[:, :part]], axis=1) + vec[5:6, :own]
    open_pre = jnp.concatenate([gf[:, block:], gs[:, part:]], axis=1) + vec[6:7, :own]
    return conved, rounded, rate_pre, open_pre


def scan_groups(a_ref, b_ref, out_h, out_c, h, c, rows, width):
    place = lax.broadcasted_iota(jnp.int32, (8, width), 0)

    def one(g, carry):
        h, c = carry
        at = pl.ds(pl.multiple_of(g * 8, 8), 8)
        a, b = a_ref[at, :], b_ref[at, :]
        for shift in (1, 2, 4):
            keep = place >= shift
            pa = jnp.where(keep, pltpu.roll(a, shift, 0), 1.0)
            pb = jnp.where(keep, pltpu.roll(b, shift, 0), 0.0)
            b = a * pb + b
            a = a * pa
        b = b + a * h
        a = a * c
        out_h[at, :] = b
        out_c[at, :] = a
        return b[7:8, :], a[7:8, :]

    return lax.fori_loop(0, rows // 8, one, (h, c), unroll=4)


def forward_kernel(
    core_ref, inner_ref, prev_ref, halo_ref, keep_ref, vec_ref, gwf_ref, gws_ref,
    decay_ref, local_ref, cum_ref, last_ref, ext, b_ref, carry, *, block, own,
):
    c = pl.program_id(2)
    rows = inner_ref.shape[0]
    prev = jnp.where(c == 0, halo_ref[...].astype(F32), prev_ref[...].astype(F32))
    vec = vec_ref[...]
    conved, _, rate_pre, open_pre = conv_and_gates(inner_ref, prev, vec, gwf_ref, gws_ref, ext, block, own)
    keep = keep_ref[...]
    rate = jax.nn.sigmoid(rate_pre)
    opening = jax.nn.sigmoid(open_pre)
    log_decay = vec[7:8, :own] * rate
    scale = keep * jnp.sqrt(minus_expm1(2.0 * log_decay)) + (1.0 - keep)
    decay_ref[...] = jnp.exp(log_decay) * keep
    b_ref[...] = scale * opening * conved[:, :own]

    @pl.when(c == 0)
    def _():
        carry[0:1, :] = jnp.zeros((1, own), F32)
        carry[1:2, :] = jnp.ones((1, own), F32)

    h, p = scan_groups(decay_ref, b_ref, local_ref, cum_ref, carry[0:1, :], carry[1:2, :], rows, own)
    carry[0:1, :] = h
    carry[1:2, :] = p
    last_ref[...] = carry[...]


def reverse_kernel(core_ref, decay_ref, grad_ref, branch_ref, adj_ref, prod_ref, first_ref, carry, *, own):
    c = pl.program_id(2)
    rows = decay_ref.shape[0]
    place = lax.broadcasted_iota(jnp.int32, (8, own), 0)

    @pl.when(c == 0)
    def _():
        carry[0:1, :] = jnp.zeros((1, own), F32)
        carry[1:2, :] = jnp.ones((1, own), F32)

    def one(i, state):
        s, p = state
        at = pl.ds(pl.multiple_of((rows // 8 - 1 - i) * 8, 8), 8)
        a = decay_ref[at, :]
        hg = grad_ref[at, :] * gelu_only(branch_ref[at, :])
        b = a * hg
        for shift in (1, 2, 4):
            keep = place < 8 - shift
            na = jnp.where(keep, pltpu.roll(a, 8 - shift, 0), 1.0)
            nb = jnp.where(keep, pltpu.roll(b, 8 - shift, 0), 0.0)
            b = a * nb + b
            a = a * na
        b = b + a * s
        a = a * p
        last = place == 7
        adj_ref[at, :] = hg + jnp.where(last, s, pltpu.roll(b, 7, 0))
        prod_ref[at, :] = jnp.where(last, p, pltpu.roll(a, 7, 0))
        return b[0:1, :], a[0:1, :]

    s, p = lax.fori_loop(0, rows // 8, one, (carry[0:1, :], carry[1:2, :]), unroll=4)
    carry[0:1, :] = s
    carry[1:2, :] = p
    first_ref[...] = carry[...]


def backward_kernel(
    core_ref, inner_ref, prev_ref, halo_ref, keep_ref, vec_ref, gwf_ref, gws_ref, hidden_ref, before_ref, start_ref,
    adj_ref, prod_ref, suffix_ref,
    igrad_ref, tail_ref, head_ref, dgf_ref, dgs_ref, sums_ref, ext, hext, cext, *, block, own,
):
    c = pl.program_id(2)
    peers = pl.num_programs(2)
    first = (pl.program_id(0) == 0) & (pl.program_id(1) == 0) & (c == 0)
    at_start = c == peers - 1
    rows = inner_ref.shape[0]
    part = own - block
    window = vec_ref.shape[1]

    @pl.when(first)
    def _():
        dgf_ref[...] = jnp.zeros_like(dgf_ref)
        dgs_ref[...] = jnp.zeros_like(dgs_ref)
        sums_ref[...] = jnp.zeros_like(sums_ref)

    @pl.when(c == 0)
    def _():
        cext[rows : rows + 8, :] = jnp.zeros((8, window), F32)

    @pl.when(c > 0)
    def _():
        cext[rows : rows + 8, :] = cext[0:8, :]

    prev = jnp.where(at_start, halo_ref[...].astype(F32), prev_ref[...].astype(F32))
    vec = vec_ref[...]
    conved, rounded, rate_pre, open_pre = conv_and_gates(inner_ref, prev, vec, gwf_ref, gws_ref, ext, block, own)
    keep = keep_ref[...]
    conv = conved[:, :own]
    rate = jax.nn.sigmoid(rate_pre)
    opening = jax.nn.sigmoid(open_pre)
    factor = vec[7:8, :own]
    log_decay = factor * rate
    e = jnp.exp(log_decay)
    root = jnp.sqrt(minus_expm1(2.0 * log_decay))
    scale = keep * root + (1.0 - keep)

    adj = adj_ref[...] + prod_ref[...] * suffix_ref[0:1, :]
    hext[0:8, :] = jnp.where(at_start, jnp.broadcast_to(start_ref[0:1, :], (8, own)), before_ref[...])
    hext[8 : 8 + rows, :] = hidden_ref[...]
    before = hext[7 : 7 + rows, :]
    d_log = keep * (adj * before * e - adj * opening * conv * (e * e) / root)
    direct = adj * scale * opening
    g_rate = (d_log * factor * rate * (1.0 - rate)).astype(BF)
    g_open = (adj * scale * conv * opening * (1.0 - opening)).astype(BF)
    gf = jnp.concatenate([g_rate[:, :block], g_open[:, :block]], axis=1)
    gs = jnp.concatenate([g_rate[:, block:], g_open[:, block:]], axis=1)
    cgrad = jnp.concatenate([dot_cols(gf, gwf_ref[...]), dot_cols(gs, gws_ref[...])], axis=1)
    cgrad = cgrad + jnp.concatenate([direct, jnp.zeros((rows, window - own), F32)], axis=1)
    cext[0:rows, :] = cgrad
    dgf_ref[...] += dot_rows(rounded[:, :block], gf)
    dgs_ref[...] += dot_rows(rounded[:, block:], gs)

    igrad = vec[0:1, :] * cgrad
    for tap in range(1, 4):
        igrad = igrad + vec[tap : tap + 1, :] * cext[tap : tap + rows, :]
    igrad_ref[...] = igrad.astype(BF)

    @pl.when(c == 0)
    def _():
        tail_ref[...] = igrad[rows - HALO :, :]

    head_ref[...] = cgrad[0:8, :]

    def total(x):
        return jnp.sum(x, axis=0, keepdims=True)

    for tap in range(4):
        sums_ref[tap : tap + 1, :] += total(ext[HALO - tap : HALO - tap + rows, :] * cgrad)
    sums_ref[4:5, :] += total(cgrad)
    sums_ref[5:6, :own] += total(g_rate.astype(F32))
    sums_ref[6:7, :own] += total(g_open.astype(F32))
    sums_ref[7:8, :own] += total(d_log * rate)


def lane_blocks(n_dp, n_z):
    return [(d * n_z + z, z * n_dp + d) for d in range(n_dp) for z in range(n_z)]


def to_z(x, n_dp, n_z):
    w = x.shape[1] // (n_dp * n_z)
    pairs = sorted(lane_blocks(n_dp, n_z), key=lambda p: p[1])
    return jnp.concatenate([x[:, a * w : (a + 1) * w] for a, _ in pairs], axis=1)


def from_z(x, n_dp, n_z):
    w = x.shape[1] // (n_dp * n_z)
    return jnp.concatenate([x[:, b * w : (b + 1) * w] for _, b in lane_blocks(n_dp, n_z)], axis=1)


def total(pieces, i, steps):
    q, ax, a, bx, b = pieces
    low = i < steps // 2
    pick = lambda u, v: jnp.where(low, u[...].astype(F32), v[...].astype(F32))
    return q[...] + pick(ax, bx) + pick(a, b)


def inverse(x):
    return lax.rsqrt(jnp.mean(x * x, axis=1, keepdims=True) + EPSILON)


def norm_kernel(gain_ref, *refs, cuts):
    out_ref = refs[-1]
    for k, ref in enumerate(refs[:-1]):

        @pl.when(pl.program_id(0) == k)
        def _(ref=ref):
            x = ref[...].astype(F32)
            out_ref[...] = to_z(x * inverse(x) * gain_ref[...], *cuts).astype(BF)


def mid_kernel(q, ax, a, bx, b, tok_ref, gain_ref, mid_ref, normed_ref, *, cuts):
    i = pl.program_id(0)
    x = tok_ref[...].astype(F32) + from_z(total((q, ax, a, bx, b), i, pl.num_programs(0)), *cuts)
    mid_ref[...] = x
    normed_ref[...] = to_z(x * inverse(x) * gain_ref[...], *cuts).astype(BF)


def norm_back(grad, x, gain):
    inv = inverse(x)
    g = grad * gain
    return inv * g - x * (inv * inv * inv) * jnp.mean(x * g, axis=1, keepdims=True), grad * x * inv


def add_rows(ref, x):
    first = pl.program_id(0) == 0
    terms = jnp.sum(x.reshape(-1, 8, x.shape[1]), axis=0)

    @pl.when(first)
    def _():
        ref[...] = terms

    @pl.when(jnp.logical_not(first))
    def _():
        ref[...] += terms


def mid_back_kernel(q, ax, a, bx, b, mid_ref, cot_ref, gain_ref, grad_ref, low_ref, part_ref, *, cuts):
    i = pl.program_id(0)
    g = from_z(total((q, ax, a, bx, b), i, pl.num_programs(0)), *cuts)
    back, part = norm_back(g, mid_ref[...], gain_ref[...])
    grad = cot_ref[...].astype(F32) + back
    grad_ref[...] = grad
    low_ref[...] = to_z(grad, *cuts).astype(BF)
    add_rows(part_ref, part)


def tok_back_kernel(q, ax, a, bx, b, tok_ref, mid_grad_ref, gain_ref, grad_ref, part_ref, *, cuts):
    i = pl.program_id(0)
    g = from_z(total((q, ax, a, bx, b), i, pl.num_programs(0)), *cuts)
    back, part = norm_back(g, tok_ref[...].astype(F32), gain_ref[...])
    grad_ref[...] = mid_grad_ref[...] + back
    add_rows(part_ref, part)


def out_kernel(q, ax, a, bx, b, mid_ref, out_ref):
    out_ref[...] = mid_ref[...] + total((q, ax, a, bx, b), pl.program_id(0), pl.num_programs(0))


class OwnRows:
    def __init__(self, rows, width, steps=4):
        self.rows, self.width, self.steps = rows, width, steps

    def call(self, kernel, pieces, arrays, gain, outs):
        n, step = self.steps, self.rows // self.steps
        tile = pl.BlockSpec((step, self.width), lambda i: (i, 0))
        low = pl.BlockSpec((step, self.width), lambda i: (jnp.minimum(i, n // 2 - 1), 0))
        high = pl.BlockSpec((step, self.width), lambda i: (jnp.maximum(i - n // 2, 0), 0))
        line = pl.BlockSpec((1, self.width), lambda i: (0, 0))
        part = pl.BlockSpec((8, self.width), lambda i: (0, 0))
        shape = jax.ShapeDtypeStruct
        gains = [] if gain is None else [gain.reshape(1, self.width)]
        return pl.pallas_call(
            kernel,
            grid=(n,),
            in_specs=([tile, low, low, high, high] if pieces else []) + [tile] * len(arrays) + [line] * len(gains),
            out_specs=[part if t is None else tile for t in outs],
            out_shape=[
                shape((8, self.width), F32) if t is None else shape((self.rows, self.width), t) for t in outs
            ],
            compiler_params=pltpu.CompilerParams(vmem_limit_bytes=VMEM_BYTES),
        )(*pieces, *arrays, *gains)


def ff_pack_kernel(gate_ref, up_ref, out_ref, *, cuts):
    n_dp, n_z, n_core = cuts
    w = gate_ref.shape[1] // (n_dp * n_z * n_core)
    for d in range(n_dp):
        for c in range(n_core):
            for j, ref in enumerate((gate_ref, up_ref)):
                cols = [((d * n_z + z) * n_core + c) * w for z in range(n_z)]
                x = jnp.concatenate([ref[:, o : o + w].astype(F32) for o in cols], axis=1)
                out_ref[d * n_core + c, :, j * n_z * w : (j + 1) * n_z * w] = x.astype(BF)


def ff_unpack_kernel(x_ref, gate_ref, up_ref, *, cuts):
    n_dp, n_z, n_core = cuts
    w = gate_ref.shape[1] // (n_dp * n_z * n_core)
    for j, ref in enumerate((gate_ref, up_ref)):
        for d in range(n_dp):
            cols = []
            for z in range(n_z):
                for c in range(n_core):
                    o = (j * n_z + z) * w
                    cols.append(x_ref[d * n_core + c, :, o : o + w].astype(F32))
            span = n_z * n_core * w
            ref[:, d * span : (d + 1) * span] = jnp.concatenate(cols, axis=1)


class Blocks:
    def __init__(self, peers, lines, seqs, back):
        self.peers, self.lines, self.seqs, self.back = peers, lines, seqs, back

    def core(self, c):
        return self.peers - 1 - c if self.back else c

    def block(self, d, s, c, core):
        return (jnp.bitwise_xor(c, core[0]) * self.lines + d) * self.seqs + s

    def rows(self, count, width):
        return pl.BlockSpec((count, width), lambda d, s, c, core: (self.block(d, s, self.core(c), core), 0))

    def before(self, count, width, length):
        each = length // count

        def index(d, s, c, core):
            return (self.block(d, s, jnp.maximum(self.core(c) - 1, 0), core) * each + each - 1, 0)

        return pl.BlockSpec((count, width), index)

    def sequence(self, count, width):
        return pl.BlockSpec((count, width), lambda d, s, c, core: (d * self.seqs + s, 0))

    def whole(self, *shape):
        return pl.BlockSpec(shape, lambda d, s, c, core: (0,) * len(shape))

    def call(self, kernel, in_specs, out_specs, out_shape, scratch, *args):
        return pl.pallas_call(
            kernel,
            grid_spec=pltpu.PrefetchScalarGridSpec(
                num_scalar_prefetch=1,
                grid=(self.lines, self.seqs, self.peers),
                in_specs=in_specs,
                out_specs=out_specs,
                scratch_shapes=scratch,
            ),
            out_shape=out_shape,
            compiler_params=pltpu.CompilerParams(vmem_limit_bytes=VMEM_BYTES),
        )(*args)


class Plane:
    def __init__(self, n_dp, n_core):
        self.n_dp, self.n_core = n_dp, n_core
        self.core = lax.axis_index("core")
        self.dp = lax.axis_index("dp")

    def near(self, x, k):
        return lax.ppermute(x, "dp", [(i, i ^ k) for i in range(self.n_dp)])

    def twin(self, x):
        return lax.ppermute(x, "core", [(0, 1), (1, 0)])

    def pieces(self, x, late=()):
        half = x.shape[0] // 2
        x1, x2 = self.near(x, 1), self.near(x, 2)
        if late:
            x1, x2 = lax.optimization_barrier((x1, x2, *late))[:2]
        x3 = jnp.concatenate([self.near(x2[:half], 1), self.near(x1[half:], 2)], axis=0)
        mine = [x, x1, x2, x3]
        return mine + [self.twin(m) for m in mine]

    def gather(self, x, late=()):
        return jnp.concatenate(self.pieces(x, late), axis=0)

    def terms(self, product, rows):
        n = self.n_dp
        halves = ((n // 2, n), (0, n // 2))
        other = [self.twin(product((n + lo) * rows, (n + hi) * rows).astype(BF)) for lo, hi in halves]
        far, near = (product(lo * rows, hi * rows) + x.astype(F32) for (lo, hi), x in zip(halves, other))
        far = far.astype(BF)
        return [x[k * rows : (k + 1) * rows] for x in (near, far) for k in range(n // 2)]

    def send_first(self, q):
        half = q[0].shape[0] // 2
        low = lambda x: x.astype(BF)
        a3, b3 = self.near(q[3][:half], 1), self.near(q[3][half:], 2)
        a1, b2 = self.near(low(q[1][:half]), 1), self.near(q[2][half:], 2)
        return a3, b3, a1, b2

    def add_up(self, q, first=None, late=()):
        half = q[0].shape[0] // 2
        low = lambda x: x.astype(BF)
        a3, b3, a1, b2 = first or self.send_first(q)
        q2, q1 = (after(q[2], *late), after(q[1], *late)) if late else (q[2], q[1])
        self.second = (low(q2[:half].astype(F32) + a3.astype(F32)), low(q1[half:] + b3.astype(F32)))
        a, b = self.near(self.second[0], 2), self.near(self.second[1], 1)
        return q[0], a1, a, b2, b

    def scatter(self, product, rows):
        return self.add_up(self.terms(product, rows))

    def in_order(self, x):
        x = jnp.where(self.core == 1, x[::-1], x)
        for bit in (1, 2):
            y = x.reshape(2, self.n_dp // (2 * bit), 2, bit, *x.shape[2:])
            x = jnp.where((self.dp & bit) != 0, y[:, :, ::-1], y).reshape(x.shape)
        return jnp.swapaxes(x, 0, 1)


def body(
    tokens, doc_reset, cotangent, norm_gain, input_proj, branch_proj, conv_kernel, conv_bias, gate_weight, gate_bias,
    decay_param, output_proj, ffn_gain, ffn_gate, ffn_up, ffn_down,
):
    seqs, span, width = tokens.shape
    rows = seqs * span
    n_dp, n_z, n_core = (lax.axis_size(a) for a in EVERY)
    group = n_dp * n_core
    devices = group * n_z
    zi = lax.axis_index("z")
    me = lax.axis_index("dp") * n_core + lax.axis_index("core")
    rec = input_proj.shape[1]
    ff = ffn_gate.shape[1]
    block = gate_weight.shape[2]
    taps = conv_kernel.shape[0]
    drow = input_proj.shape[0]
    frow = ffn_down.shape[0]
    ff_own = ff // group
    blocks = rec // block
    shared = blocks - group
    sharers = group // shared
    part = block // sharers
    lanes = 128 * (-(-part // 128))
    own = block + lanes
    window = 2 * block
    total_rows = group * rows
    lines = n_dp * seqs

    plane = Plane(n_dp, n_core)
    core = plane.core
    core_id = core.astype(jnp.int32).reshape(1)

    def own_columns(w):
        lead = w.shape[0]
        full = w[:, : group * block].reshape(lead, group, block)
        rest = w[:, group * block :].reshape(lead, group, part)
        return jnp.concatenate([full, rest, jnp.zeros((lead, group, lanes - part), w.dtype)], axis=2)

    def window_columns(w):
        lead = w.shape[0]
        full = w[:, : group * block].reshape(lead, group, block)
        rest = w[:, group * block :].reshape(lead, shared, block)
        turned = jnp.stack([jnp.roll(rest, -part * q, axis=2) for q in range(sharers)], axis=2)
        return jnp.concatenate([full, turned.reshape(lead, group, block)], axis=2)

    def exchange(x):
        return lax.all_to_all(x, GROUP, split_axis=0, concat_axis=0, tiled=True)

    def to_members(x):
        y = jnp.swapaxes(x, 0, 1)
        return exchange(y.reshape(group * x.shape[0], x.shape[2]))

    def sum_z(x):
        return lax.psum_scatter(x, "z", scatter_dimension=0, tiled=True)

    def over_z(x):
        return lax.all_gather(x, "z", axis=0, tiled=True)

    cuts = (n_dp, n_z)
    cot = cotangent.reshape(rows, width)
    tok = tokens.reshape(rows, width)
    tok_pieces = plane.pieces(tok)
    rrow = rec // devices
    small = jnp.concatenate(
        [
            gate_weight.reshape(-1), norm_gain, ffn_gain, conv_kernel.reshape(-1), conv_bias, gate_bias.reshape(-1),
            decay_param,
        ]
    )
    small_len = small.shape[0]
    marks = (1 - doc_reset).astype(BF).reshape(-1, 256)
    small = jnp.pad(small, (0, -small_len % 256)).reshape(-1, 256)
    marks_at = small.shape[0]
    small = jnp.concatenate([small, marks])
    small = jnp.pad(small, ((0, -small.shape[0] % 32), (0, 0)))
    packed = small.shape[0]
    sent_in = to_members(window_columns(input_proj))
    small = over_z(after(small, sent_in))

    def pair(a, b):
        cut = block + part
        return jnp.concatenate([a[..., :block], b[..., :block], a[..., block:cut], b[..., block:cut]], axis=-1)

    def unpair(x, k):
        at = 2 * block + k * part
        return jnp.concatenate([x[..., k * block : (k + 1) * block], x[..., at : at + part]], axis=-1)

    both = pair(own_columns(branch_proj), own_columns(output_proj.T))
    sent_both = to_members(after(both, small, *tok_pieces[1:3]))
    ff_packed = pl.pallas_call(
        functools.partial(ff_pack_kernel, cuts=(n_dp, n_z, n_core)),
        out_shape=jax.ShapeDtypeStruct((group, drow, 2 * ff_own), BF),
        compiler_params=pltpu.CompilerParams(vmem_limit_bytes=VMEM_BYTES),
    )(ffn_gate, ffn_up)
    w_in = over_z(sent_in)
    w_both = over_z(sent_both)
    w_branch, w_out = (jnp.pad(unpair(w_both, k), ((0, 0), (0, lanes - part))) for k in range(2))
    small = plane.gather(small).reshape(n_core, n_dp, n_z, packed, 256)
    keep = lax.dynamic_index_in_dim(small, zi, 2, False)[:, :, marks_at : marks_at + rows // 256]
    keep = keep.astype(F32).reshape(total_rows, 1)
    ff_packed, small = lax.optimization_barrier((ff_packed, small))
    sent_ff = exchange(ff_packed.reshape(group * drow, 2 * ff_own))
    gates_len = 2 * rrow * block
    rest = small[:, :, :, gates_len // 256 : marks_at]
    rest = jnp.swapaxes(plane.in_order(rest), 1, 2).reshape(devices, -1)[:, : small_len - gates_len].astype(F32)
    gain = rest[:, :drow].reshape(width)
    fgain = rest[:, drow : 2 * drow].reshape(width)
    chan = rest[:, 2 * drow :].reshape(devices, taps + 4, rrow)
    chan = jnp.swapaxes(chan, 0, 1).reshape(taps + 4, rec)
    lam = chan[taps + 3 :]
    chan = jnp.concatenate([chan[: taps + 3], -POWER * jax.nn.softplus(-lam)], axis=0)

    quarter = me % sharers
    shared_at = (group + me // sharers) * block

    def my_window(x, axis):
        full = lax.dynamic_slice_in_dim(x, me * block, block, axis)
        other = lax.dynamic_slice_in_dim(x, shared_at, block, axis)
        turned = lax.dynamic_slice_in_dim(jnp.concatenate([other, other], axis), quarter * part, block, axis)
        return full, turned

    vec = jnp.concatenate(my_window(chan, 1), axis=1)
    mine = OwnRows(rows, width)
    normed = pl.pallas_call(
        functools.partial(norm_kernel, cuts=cuts),
        grid=(group,),
        in_specs=[pl.BlockSpec((1, width), lambda i: (0, 0))] + [pl.BlockSpec((rows, width), lambda i: (0, 0))] * group,
        out_specs=pl.BlockSpec((rows, width), lambda i: (i, 0)),
        out_shape=jax.ShapeDtypeStruct((total_rows, width), BF),
        compiler_params=pltpu.CompilerParams(vmem_limit_bytes=VMEM_BYTES),
    )(gain.reshape(1, width), *tok_pieces)

    normed, small = lax.optimization_barrier((normed, small))
    gates_all = small[:, :, :, : gates_len // 256].reshape(n_core, n_dp, n_z, 2, rrow * block // 256, 256)
    gates_all = jnp.transpose(plane.in_order(gates_all), (3, 0, 2, 1, 4, 5)).reshape(2, rec, block)
    gw_full, gw_shared = my_window(gates_all, 1)
    gw_shared = lax.dynamic_slice_in_dim(gw_shared, quarter * part, part, 2)
    gw_shared = jnp.pad(gw_shared, ((0, 0), (0, 0), (0, lanes - part)))
    gwf = jnp.concatenate([gw_full[0], gw_full[1]], axis=1)
    gws = jnp.concatenate([gw_shared[0], gw_shared[1]], axis=1)

    inner = dot(normed, w_in).astype(BF)
    cot_here, inner, sent_ff = lax.optimization_barrier((cot, inner, sent_ff))
    w_ff = over_z(sent_ff)
    w_down = over_z(after(ffn_down, sent_ff))
    branch = dot(normed, w_branch)
    ends = inner.reshape(n_core, n_dp, seqs, span, window)[:, :, :, span - HALO :]
    ends = jnp.where(core == 1, ends[0], ends[1]).reshape(lines * HALO, window)
    halo = lax.ppermute(ends, "z", [(i, i + 1) for i in range(n_z - 1)])

    at = Blocks(n_core, n_dp, seqs, False)
    seq_in = [
        lambda b: b.rows(span, window), lambda b: b.before(HALO, window, span), lambda b: b.sequence(HALO, window),
        lambda b: b.rows(span, 1), lambda b: b.whole(8, window), lambda b: b.whole(block, window),
        lambda b: b.whole(block, 2 * lanes),
    ]
    row_f32 = jax.ShapeDtypeStruct((total_rows, own), F32)
    decay, local, cum, last = at.call(
        functools.partial(forward_kernel, block=block, own=own),
        [f(at) for f in seq_in],
        [at.rows(span, own)] * 3 + [at.sequence(8, own)],
        [row_f32] * 3 + [jax.ShapeDtypeStruct((lines * 8, own), F32)],
        [pltpu.VMEM((span + HALO, window), F32), pltpu.VMEM((span, own), F32), pltpu.VMEM((8, own), F32)],
        core_id, inner, inner, halo, keep, vec, gwf, gws,
    )

    cot_pieces = plane.pieces(cot_here, [last])

    def carried(x, way, beside):
        x = x.reshape(lines, 8, own)[:, :2]
        state = jnp.zeros((lines, own), F32)
        for k in range(n_z - 1, 0, -1):
            hops = [(i, i + way * k) for i in range(n_z) if 0 <= i + way * k < n_z]
            come = after(lax.ppermute(x, "z", hops), *beside)
            state = come[:, 1] * state + come[:, 0]
        return state

    start = carried(last, 1, [branch])

    def by_line(x):
        return x.reshape(1, n_dp, seqs, 1, own)

    def spread(x):
        return x.reshape(n_core, n_dp, seqs, span, own)

    hidden = (spread(local) + spread(cum) * by_line(start)).reshape(total_rows, own)
    mixed_out = (hidden * gelu_only(branch)).astype(BF)
    mixed_out, *cot_pieces = lax.optimization_barrier((mixed_out, *cot_pieces))
    terms = plane.scatter(lambda lo, hi: dot_cols(mixed_out[lo:hi], w_out), rows)
    mid, fnormed = mine.call(functools.partial(mid_kernel, cuts=cuts), terms, [tok], fgain, [F32, BF])

    cot_pieces[0] = after(cot_pieces[0], fnormed)
    cot_all = jnp.concatenate(cot_pieces, axis=0)
    fnormed = plane.gather(fnormed, [cot_all])
    pre_lin = dot(fnormed, w_ff)
    act, slope = gelu_pair(pre_lin[:, :ff_own])
    lin = pre_lin[:, ff_own:]
    fhidden = (act * lin).astype(BF)
    down_terms = dot_rows(fhidden, cot_all).astype(BF)
    hid_grad = dot_cols(after(cot_all, down_terms), w_down)
    fgrad = jnp.concatenate([(hid_grad * lin * slope).astype(BF), (hid_grad * act).astype(BF)], axis=1)
    down_sum = sum_z(down_terms)
    down_out = down_sum.astype(F32)
    terms = plane.terms(lambda lo, hi: dot_cols(fgrad[lo:hi], w_ff), rows)
    ff_terms = dot_rows(fnormed, after(fgrad, down_sum, *terms)).astype(BF)
    terms = plane.add_up(terms)
    ff_sum = sum_z(after(ff_terms, down_sum))
    terms = (after(terms[0], down_sum, ff_terms), *terms[1:])
    mid_grad, mid_low, ffn_gain_part = mine.call(
        functools.partial(mid_back_kernel, cuts=cuts), terms, [mid, cot], fgain, [F32, BF, None]
    )
    later = after(fhidden, mid_grad)
    out_terms = plane.terms(lambda lo, hi: dot(later[lo:hi], w_down), rows)
    ffn_gain_part = jnp.sum(ffn_gain_part, axis=0)
    mid_low = plane.gather(mid_low, [*out_terms, ffn_gain_part, down_out])
    out_terms[3] = after(out_terms[3], mid_low)

    mixed_grad = dot(mid_low, w_out)
    act_r, slope_r = gelu_pair(branch)
    branch_grad = (mixed_grad * hidden * slope_r).astype(BF)
    back = Blocks(n_core, n_dp, seqs, True)
    out_first = plane.send_first(out_terms)
    adj, prod, front = back.call(
        functools.partial(reverse_kernel, own=own),
        [back.rows(span, own)] * 3,
        [back.rows(span, own)] * 2 + [back.sequence(8, own)],
        [row_f32] * 2 + [jax.ShapeDtypeStruct((lines * 8, own), F32)],
        [pltpu.VMEM((8, own), F32)],
        core_id, decay, mixed_grad, branch,
    )
    branch_late, mixed_late, *out_first = lax.optimization_barrier((branch_grad, mixed_out, *out_first, adj))[:6]
    both = pair(dot_rows(normed, branch_late).astype(BF), dot_rows(mid_low, mixed_late).astype(BF))
    both, ff_sum = lax.optimization_barrier((both, ff_sum))
    out_terms = plane.add_up(out_terms, out_first, [both])
    suffix, *out_terms = lax.optimization_barrier((carried(front, -1, [both]), *out_terms))

    def eight(x):
        return jnp.broadcast_to(x[:, None, :], (lines, 8, own)).reshape(lines * 8, own)

    igrad, tail, head, dgf, dgs, sums = back.call(
        functools.partial(backward_kernel, block=block, own=own),
        [f(back) for f in seq_in]
        + [
            back.rows(span, own), back.before(8, own, span), back.sequence(8, own), back.rows(span, own),
            back.rows(span, own), back.sequence(8, own),
        ],
        [
            back.rows(span, window), back.sequence(HALO, window), back.sequence(8, window), back.whole(block, window),
            back.whole(block, 2 * lanes), back.whole(8, window),
        ],
        [
            jax.ShapeDtypeStruct((total_rows, window), BF), jax.ShapeDtypeStruct((lines * HALO, window), F32),
            jax.ShapeDtypeStruct((lines * 8, window), F32), jax.ShapeDtypeStruct((block, window), F32),
            jax.ShapeDtypeStruct((block, 2 * lanes), F32), jax.ShapeDtypeStruct((8, window), F32),
        ],
        [
            pltpu.VMEM((span + HALO, window), F32), pltpu.VMEM((span + 8, own), F32), pltpu.VMEM((span + 8, window), F32),
        ],
        core_id, inner, inner, halo, keep, vec, gwf, gws, hidden, hidden, eight(start), adj, prod, eight(suffix),
    )

    coming = lax.ppermute(head.astype(BF), "z", [(i + 1, i) for i in range(n_z - 1)]).astype(F32).reshape(lines, 8, window)
    fix = jnp.zeros((lines, HALO, window), F32)
    for tap in range(1, taps):
        fix = fix.at[:, HALO - tap :, :].add(vec[tap] * coming[:, :tap])
    tail = (tail.reshape(lines, HALO, window) + fix).astype(BF).reshape(1, n_dp, seqs, HALO, window)
    igrad = lax.dynamic_update_slice(
        igrad.reshape(n_core, n_dp, seqs, span, window), tail, (1 - core, 0, 0, span - HALO, 0)
    ).reshape(total_rows, window)
    ff_part = exchange(ff_sum)
    both_sum = sum_z(after(both, ff_sum))
    igrad = after(igrad, both_sum)
    in_terms = dot_rows(normed, igrad).astype(BF)
    igrad, in_terms, ff_part = lax.optimization_barrier((igrad, in_terms, ff_part))
    terms = plane.terms(
        lambda lo, hi: dot_cols(igrad[lo:hi], w_in) + dot_cols(branch_grad[lo:hi], w_branch), rows
    )
    both_late, ff_part, mid_late = lax.optimization_barrier((both_sum, ff_part, mid, *terms))[:3]
    both_part = exchange(both_late)
    layer_out = mine.call(out_kernel, out_terms, [mid_late], None, [F32])[0]
    gate_out, up_out = pl.pallas_call(
        functools.partial(ff_unpack_kernel, cuts=(n_dp, n_z, n_core)),
        out_shape=[jax.ShapeDtypeStruct((drow, ff), F32)] * 2,
        compiler_params=pltpu.CompilerParams(vmem_limit_bytes=VMEM_BYTES),
    )(ff_part.reshape(group, drow, 2 * ff_own))
    terms = plane.add_up(terms)
    second = plane.second
    first_terms, layer_out, gate_out, up_out, both_part = lax.optimization_barrier(
        (terms[0], layer_out, gate_out, up_out, both_part)
    )
    terms = (first_terms, *terms[1:])
    both_part = both_part.reshape(group, drow, 2 * (block + part))

    def own_natural(x):
        full = jnp.swapaxes(x[:, :, :block], 0, 1).reshape(drow, group * block)
        rest = jnp.swapaxes(x[:, :, block : block + part], 0, 1).reshape(drow, group * part)
        return jnp.concatenate([full, rest], axis=1).astype(F32)

    branch_proj_grad = own_natural(unpair(both_part, 0))
    output_proj_grad = own_natural(unpair(both_part, 1)).T

    def place_window(x, axis_len):
        lead = x.shape[:-1]
        other = x[..., block:]
        turned = lax.dynamic_slice_in_dim(
            jnp.concatenate([other, other], -1), lax.rem(block - quarter * part, block), block, x.ndim - 1
        )
        y = jnp.zeros((*lead, axis_len), x.dtype)
        y = lax.dynamic_update_slice_in_dim(y, x[..., :block], me * block, x.ndim - 1)
        return lax.dynamic_update_slice_in_dim(y, turned, shared_at, x.ndim - 1)

    dg_full = jnp.stack([dgf[:, :block], dgf[:, block:]])
    dg_shared = jnp.stack([dgs[:, :part], dgs[:, lanes : lanes + part]])
    dg_shared = lax.dynamic_slice_in_dim(
        jnp.concatenate([dg_shared, dg_shared], 1), lax.rem(block - quarter * part, block), block, 1
    )
    lot = n_core * rrow
    lots = (block + 2 * lot - 2) // lot

    def by_z(x, row):
        y = jnp.swapaxes(x, 0, 1).reshape(block, -1).astype(BF)
        q = row // lot
        y = lax.dynamic_update_slice(jnp.zeros((n_z * lot, y.shape[1]), BF), y, (row - q * lot, 0))
        y = y.reshape(n_z, lot, -1)
        return lax.dynamic_slice_in_dim(jnp.concatenate([y, y]), lax.rem(n_z - lax.rem(q, n_z), n_z), n_z, 0)

    def to_lines(x, row):
        q = row // lot
        q = q + lax.rem(zi + n_z - lax.rem(q, n_z), n_z)
        y = jnp.zeros((n_dp, *x.shape), x.dtype)
        return lax.dynamic_update_slice(y, x[None], (jnp.minimum(q // n_z, n_dp - 1), 0, 0))

    assert lots <= n_z
    gates = jnp.concatenate([by_z(dg_full, me * block), by_z(dg_shared, shared_at)], axis=2)
    gates = gates.reshape(n_z, lot * 2 * (block + part) // window, window)
    joined = jnp.concatenate([in_terms.reshape(n_z, group * drow, window), gates], axis=1)
    joined = sum_z(after(joined.reshape(-1, window), both_sum))
    joined = after(joined, *second)
    input_grad, gain_part = mine.call(
        functools.partial(tok_back_kernel, cuts=cuts), terms, [tok, mid_grad], gain, [F32, None]
    )
    blocks_z = jnp.swapaxes(jnp.sum(gain_part, axis=0).reshape(n_dp, n_z, n_core * drow), 0, 1).reshape(n_z, group * drow)
    blocks_z = lax.dynamic_slice_in_dim(jnp.concatenate([blocks_z, blocks_z]), zi, n_z, 0)
    gain_sum = blocks_z[0]
    for k in range(1, n_z):
        gain_sum = gain_sum + lax.ppermute(blocks_z[k], "z", [(i, (i + k) % n_z) for i in range(n_z)])
    gain_high = gain_sum.astype(BF)
    gain_low = (gain_sum - gain_high.astype(F32)).astype(BF)
    gain_rows = jnp.concatenate([gain_high.reshape(group, drow), gain_low.reshape(group, drow)], axis=1)
    gain_rows = jnp.pad(gain_rows[:, None, :], ((0, 0), (0, 3), (0, window - 2 * drow)))
    in_part = joined[: group * drow].reshape(group, drow, window)
    gates = joined[group * drow :].reshape(lot, 2 * (block + part))
    gates = jnp.concatenate(
        [to_lines(gates[:, : 2 * block], me * block), to_lines(gates[:, 2 * block :], shared_at)], axis=2
    )
    gates = gates.reshape(group, rrow * 2 * (block + part) // window, window)
    gates_end = drow + gates.shape[1]
    joined = exchange(jnp.concatenate([in_part, gates, gain_rows], axis=1).reshape(-1, window))

    lane = jnp.arange(window)
    mine = lane < block + part
    sums = jnp.where(jnp.concatenate([jnp.ones((5, window), bool), jnp.broadcast_to(mine, (3, window))], axis=0), sums, 0.0)
    sums = place_window(sums, rec)
    sums = jnp.concatenate([sums[:7], sums[7:8] * (POWER * jax.nn.sigmoid(-lam))], axis=0)
    vectors = jnp.concatenate(
        [
            ffn_gain_part.reshape(devices, drow),
            jnp.swapaxes(sums.reshape(8, devices, rrow), 0, 1).reshape(devices, 8 * rrow),
        ],
        axis=1,
    )
    vec_len = vectors.shape[1]
    vectors = lax.all_to_all(vectors, EVERY, split_axis=0, concat_axis=0, tiled=True)
    joined = joined.reshape(group, -1, window)
    in_part = joined[:, :drow]
    gates = joined[:, drow:gates_end].reshape(group, rrow, 2 * (block + part)).astype(F32)
    gain_out = jnp.sum(joined[:, gates_end].astype(F32), axis=0)
    gain_out = gain_out[:drow] + gain_out[drow : 2 * drow]
    vectors = jnp.sum(vectors.reshape(devices, vec_len), axis=0)
    fgain_out = vectors[:drow]
    chan_out = vectors[drow:].reshape(8, rrow)

    gates_out = jnp.sum(gates[:, :, : 2 * block], axis=0).reshape(rrow, 2, block)
    rest = jnp.sum(gates[:, :, 2 * block :].reshape(shared, sharers, rrow, 2, part), axis=0)
    rest = jnp.transpose(rest, (1, 2, 0, 3)).reshape(rrow, 2, block)
    gates_out = jnp.swapaxes(gates_out + rest, 0, 1)

    full = jnp.swapaxes(in_part[:, :, :block], 0, 1).reshape(drow, group * block).astype(F32)
    turned = in_part[:, :, block:window].astype(F32).reshape(shared, sharers, drow, block)
    other = sum(jnp.roll(turned[:, q], part * q, axis=2) for q in range(sharers))
    input_proj_grad = jnp.concatenate([full, jnp.swapaxes(other, 0, 1).reshape(drow, shared * block)], axis=1)

    return (
        layer_out.reshape(seqs, span, width),
        input_grad.reshape(seqs, span, width),
        gain_out,
        input_proj_grad,
        branch_proj_grad,
        chan_out[:taps],
        chan_out[taps],
        gates_out,
        chan_out[taps + 1 : taps + 3],
        chan_out[taps + 3],
        output_proj_grad,
        fgain_out,
        gate_out,
        up_out,
        down_out,
    )


def solution(mesh):
    n_dp, n_seq = mesh.shape["dp"], mesh.shape["seq"]
    split = Mesh(mesh.devices.reshape(n_dp, n_seq // 2, 2), EVERY)
    seq = ("z", "core")
    line = P("dp", seq, None)
    first = P(EVERY)
    rows = P(EVERY, None)
    cols = P(None, EVERY)
    mids = P(None, EVERY, None)
    return jax.shard_map(
        body,
        mesh=split,
        in_specs=(
            line, P("dp", seq), line, first, rows, rows, cols, first, mids, cols, first, cols, first, rows, rows, rows,
        ),
        out_specs=(
            line, line, first, rows, rows, cols, first, mids, cols, first, cols, first, rows, rows, rows,
        ),
        check_vma=False,
    )
```

```python
import functools

import jax
import jax.numpy as jnp
from jax import lax
from jax.experimental import pallas as pl
from jax.experimental.pallas import tpu as pltpu
from jax.sharding import Mesh
from jax.sharding import PartitionSpec as P

EPSILON = 1e-06
POWER = 8.0
BF = jnp.bfloat16
F32 = jnp.float32
GROUP = ("dp", "core")
EVERY = ("dp", "z", "core")
GELU_A = 0.7978845608028654
GELU_B = 0.044715
HALO = 16
VMEM_BYTES = 48 * 1024 * 1024


def after(x, *others):
    return lax.optimization_barrier((x, *others))[0]


def gelu_pair(x):
    x2 = x * x
    th = jnp.tanh(GELU_A * (x + GELU_B * x2 * x))
    half = 0.5 * (1.0 + th)
    slope = half + 0.5 * x * (1.0 - th * th) * (GELU_A * (1.0 + 3.0 * GELU_B * x2))
    return x * half, slope


def gelu_only(x):
    return 0.5 * x * (1.0 + jnp.tanh(GELU_A * (x + GELU_B * x * x * x)))


def dot(a, b):
    return lax.dot_general(a, b, (((1,), (0,)), ((), ())), preferred_element_type=F32)


def dot_rows(a, b):
    return lax.dot_general(a, b, (((0,), (0,)), ((), ())), preferred_element_type=F32)


def dot_cols(a, b):
    return lax.dot_general(a, b, (((1,), (1,)), ((), ())), preferred_element_type=F32)


def minus_expm1(x):
    series = -x * (1.0 + x * (1 / 2) * (1.0 + x * (1 / 3) * (1.0 + x * (1 / 4) * (1.0 + x * (1 / 5) * (1.0 + x * (1 / 6))))))
    return jnp.where(x > -0.125, series, 1.0 - jnp.exp(x))


def conv_and_gates(inner_ref, prev, vec, gwf_ref, gws_ref, ext, block, own):
    rows = inner_ref.shape[0]
    ext[0:HALO, :] = prev.astype(F32)
    ext[HALO : HALO + rows, :] = inner_ref[...].astype(F32)
    conved = vec[4:5, :] + vec[0:1, :] * ext[HALO : HALO + rows, :]
    for tap in range(1, 4):
        conved = conved + vec[tap : tap + 1, :] * ext[HALO - tap : HALO - tap + rows, :]
    rounded = conved.astype(BF)
    gf = dot(rounded[:, :block], gwf_ref[...])
    gs = dot(rounded[:, block:], gws_ref[...])
    part = own - block
    rate_pre = jnp.concatenate([gf[:, :block], gs[:, :part]], axis=1) + vec[5:6, :own]
    open_pre = jnp.concatenate([gf[:, block:], gs[:, part:]], axis=1) + vec[6:7, :own]
    return conved, rounded, rate_pre, open_pre


def scan_groups(a_ref, b_ref, out_h, out_c, h, c, rows, width):
    place = lax.broadcasted_iota(jnp.int32, (8, width), 0)

    def one(g, carry):
        h, c = carry
        at = pl.ds(pl.multiple_of(g * 8, 8), 8)
        a, b = a_ref[at, :], b_ref[at, :]
        for shift in (1, 2, 4):
            keep = place >= shift
            pa = jnp.where(keep, pltpu.roll(a, shift, 0), 1.0)
            pb = jnp.where(keep, pltpu.roll(b, shift, 0), 0.0)
            b = a * pb + b
            a = a * pa
        b = b + a * h
        a = a * c
        out_h[at, :] = b
        out_c[at, :] = a
        return b[7:8, :], a[7:8, :]

    return lax.fori_loop(0, rows // 8, one, (h, c), unroll=4)


def forward_kernel(
    core_ref, inner_ref, prev_ref, halo_ref, keep_ref, vec_ref, gwf_ref, gws_ref,
    decay_ref, local_ref, cum_ref, last_ref, ext, b_ref, carry, *, block, own,
):
    c = pl.program_id(2)
    rows = inner_ref.shape[0]
    prev = jnp.where(c == 0, halo_ref[...].astype(F32), prev_ref[...].astype(F32))
    vec = vec_ref[...]
    conved, _, rate_pre, open_pre = conv_and_gates(inner_ref, prev, vec, gwf_ref, gws_ref, ext, block, own)
    keep = keep_ref[...]
    rate = jax.nn.sigmoid(rate_pre)
    opening = jax.nn.sigmoid(open_pre)
    log_decay = vec[7:8, :own] * rate
    scale = keep * jnp.sqrt(minus_expm1(2.0 * log_decay)) + (1.0 - keep)
    decay_ref[...] = jnp.exp(log_decay) * keep
    b_ref[...] = scale * opening * conved[:, :own]

    @pl.when(c == 0)
    def _():
        carry[0:1, :] = jnp.zeros((1, own), F32)
        carry[1:2, :] = jnp.ones((1, own), F32)

    h, p = scan_groups(decay_ref, b_ref, local_ref, cum_ref, carry[0:1, :], carry[1:2, :], rows, own)
    carry[0:1, :] = h
    carry[1:2, :] = p
    last_ref[...] = carry[...]


def reverse_kernel(core_ref, decay_ref, grad_ref, branch_ref, adj_ref, prod_ref, first_ref, carry, *, own):
    c = pl.program_id(2)
    rows = decay_ref.shape[0]
    place = lax.broadcasted_iota(jnp.int32, (8, own), 0)

    @pl.when(c == 0)
    def _():
        carry[0:1, :] = jnp.zeros((1, own), F32)
        carry[1:2, :] = jnp.ones((1, own), F32)

    def one(i, state):
        s, p = state
        at = pl.ds(pl.multiple_of((rows // 8 - 1 - i) * 8, 8), 8)
        a = decay_ref[at, :]
        hg = grad_ref[at, :] * gelu_only(branch_ref[at, :])
        b = a * hg
        for shift in (1, 2, 4):
            keep = place < 8 - shift
            na = jnp.where(keep, pltpu.roll(a, 8 - shift, 0), 1.0)
            nb = jnp.where(keep, pltpu.roll(b, 8 - shift, 0), 0.0)
            b = a * nb + b
            a = a * na
        b = b + a * s
        a = a * p
        last = place == 7
        adj_ref[at, :] = hg + jnp.where(last, s, pltpu.roll(b, 7, 0))
        prod_ref[at, :] = jnp.where(last, p, pltpu.roll(a, 7, 0))
        return b[0:1, :], a[0:1, :]

    s, p = lax.fori_loop(0, rows // 8, one, (carry[0:1, :], carry[1:2, :]), unroll=4)
    carry[0:1, :] = s
    carry[1:2, :] = p
    first_ref[...] = carry[...]


def backward_kernel(
    core_ref, inner_ref, prev_ref, halo_ref, keep_ref, vec_ref, gwf_ref, gws_ref, hidden_ref, before_ref, start_ref,
    adj_ref, prod_ref, suffix_ref,
    igrad_ref, tail_ref, head_ref, dgf_ref, dgs_ref, sums_ref, ext, hext, cext, *, block, own,
):
    c = pl.program_id(2)
    peers = pl.num_programs(2)
    first = (pl.program_id(0) == 0) & (pl.program_id(1) == 0) & (c == 0)
    at_start = c == peers - 1
    rows = inner_ref.shape[0]
    part = own - block
    window = vec_ref.shape[1]

    @pl.when(first)
    def _():
        dgf_ref[...] = jnp.zeros_like(dgf_ref)
        dgs_ref[...] = jnp.zeros_like(dgs_ref)
        sums_ref[...] = jnp.zeros_like(sums_ref)

    @pl.when(c == 0)
    def _():
        cext[rows : rows + 8, :] = jnp.zeros((8, window), F32)

    @pl.when(c > 0)
    def _():
        cext[rows : rows + 8, :] = cext[0:8, :]

    prev = jnp.where(at_start, halo_ref[...].astype(F32), prev_ref[...].astype(F32))
    vec = vec_ref[...]
    conved, rounded, rate_pre, open_pre = conv_and_gates(inner_ref, prev, vec, gwf_ref, gws_ref, ext, block, own)
    keep = keep_ref[...]
    conv = conved[:, :own]
    rate = jax.nn.sigmoid(rate_pre)
    opening = jax.nn.sigmoid(open_pre)
    factor = vec[7:8, :own]
    log_decay = factor * rate
    e = jnp.exp(log_decay)
    root = jnp.sqrt(minus_expm1(2.0 * log_decay))
    scale = keep * root + (1.0 - keep)

    adj = adj_ref[...] + prod_ref[...] * suffix_ref[0:1, :]
    hext[0:8, :] = jnp.where(at_start, jnp.broadcast_to(start_ref[0:1, :], (8, own)), before_ref[...])
    hext[8 : 8 + rows, :] = hidden_ref[...]
    before = hext[7 : 7 + rows, :]
    d_log = keep * (adj * before * e - adj * opening * conv * (e * e) / root)
    direct = adj * scale * opening
    g_rate = (d_log * factor * rate * (1.0 - rate)).astype(BF)
    g_open = (adj * scale * conv * opening * (1.0 - opening)).astype(BF)
    gf = jnp.concatenate([g_rate[:, :block], g_open[:, :block]], axis=1)
    gs = jnp.concatenate([g_rate[:, block:], g_open[:, block:]], axis=1)
    cgrad = jnp.concatenate([dot_cols(gf, gwf_ref[...]), dot_cols(gs, gws_ref[...])], axis=1)
    cgrad = cgrad + jnp.concatenate([direct, jnp.zeros((rows, window - own), F32)], axis=1)
    cext[0:rows, :] = cgrad
    dgf_ref[...] += dot_rows(rounded[:, :block], gf)
    dgs_ref[...] += dot_rows(rounded[:, block:], gs)

    igrad = vec[0:1, :] * cgrad
    for tap in range(1, 4):
        igrad = igrad + vec[tap : tap + 1, :] * cext[tap : tap + rows, :]
    igrad_ref[...] = igrad.astype(BF)

    @pl.when(c == 0)
    def _():
        tail_ref[...] = igrad[rows - HALO :, :]

    head_ref[...] = cgrad[0:8, :]

    def total(x):
        return jnp.sum(x, axis=0, keepdims=True)

    for tap in range(4):
        sums_ref[tap : tap + 1, :] += total(ext[HALO - tap : HALO - tap + rows, :] * cgrad)
    sums_ref[4:5, :] += total(cgrad)
    sums_ref[5:6, :own] += total(g_rate.astype(F32))
    sums_ref[6:7, :own] += total(g_open.astype(F32))
    sums_ref[7:8, :own] += total(d_log * rate)


def lane_blocks(n_dp, n_z):
    return [(d * n_z + z, z * n_dp + d) for d in range(n_dp) for z in range(n_z)]


def to_z(x, n_dp, n_z):
    w = x.shape[1] // (n_dp * n_z)
    pairs = sorted(lane_blocks(n_dp, n_z), key=lambda p: p[1])
    return jnp.concatenate([x[:, a * w : (a + 1) * w] for a, _ in pairs], axis=1)


def from_z(x, n_dp, n_z):
    w = x.shape[1] // (n_dp * n_z)
    return jnp.concatenate([x[:, b * w : (b + 1) * w] for _, b in lane_blocks(n_dp, n_z)], axis=1)


def total(pieces, i, steps):
    q, ax, a, bx, b = pieces
    low = i < steps // 2
    pick = lambda u, v: jnp.where(low, u[...].astype(F32), v[...].astype(F32))
    return q[...] + pick(ax, bx) + pick(a, b)


def inverse(x):
    return lax.rsqrt(jnp.mean(x * x, axis=1, keepdims=True) + EPSILON)


def norm_kernel(gain_ref, *refs, cuts):
    out_ref = refs[-1]
    for k, ref in enumerate(refs[:-1]):

        @pl.when(pl.program_id(0) == k)
        def _(ref=ref):
            x = ref[...].astype(F32)
            out_ref[...] = to_z(x * inverse(x) * gain_ref[...], *cuts).astype(BF)


def mid_kernel(q, ax, a, bx, b, tok_ref, gain_ref, mid_ref, normed_ref, *, cuts):
    i = pl.program_id(0)
    x = tok_ref[...].astype(F32) + from_z(total((q, ax, a, bx, b), i, pl.num_programs(0)), *cuts)
    mid_ref[...] = x
    normed_ref[...] = to_z(x * inverse(x) * gain_ref[...], *cuts).astype(BF)


def norm_back(grad, x, gain):
    inv = inverse(x)
    g = grad * gain
    return inv * g - x * (inv * inv * inv) * jnp.mean(x * g, axis=1, keepdims=True), grad * x * inv


def add_rows(ref, x):
    first = pl.program_id(0) == 0
    terms = jnp.sum(x.reshape(-1, 8, x.shape[1]), axis=0)

    @pl.when(first)
    def _():
        ref[...] = terms

    @pl.when(jnp.logical_not(first))
    def _():
        ref[...] += terms


def mid_back_kernel(q, ax, a, bx, b, mid_ref, cot_ref, gain_ref, grad_ref, low_ref, part_ref, *, cuts):
    i = pl.program_id(0)
    g = from_z(total((q, ax, a, bx, b), i, pl.num_programs(0)), *cuts)
    back, part = norm_back(g, mid_ref[...], gain_ref[...])
    grad = cot_ref[...].astype(F32) + back
    grad_ref[...] = grad
    low_ref[...] = to_z(grad, *cuts).astype(BF)
    add_rows(part_ref, part)


def tok_back_kernel(q, ax, a, bx, b, tok_ref, mid_grad_ref, gain_ref, grad_ref, part_ref, *, cuts):
    i = pl.program_id(0)
    g = from_z(total((q, ax, a, bx, b), i, pl.num_programs(0)), *cuts)
    back, part = norm_back(g, tok_ref[...].astype(F32), gain_ref[...])
    grad_ref[...] = mid_grad_ref[...] + back
    add_rows(part_ref, part)


def out_kernel(q, ax, a, bx, b, mid_ref, out_ref):
    out_ref[...] = mid_ref[...] + total((q, ax, a, bx, b), pl.program_id(0), pl.num_programs(0))


class OwnRows:
    def __init__(self, rows, width, steps=4):
        self.rows, self.width, self.steps = rows, width, steps

    def call(self, kernel, pieces, arrays, gain, outs):
        n, step = self.steps, self.rows // self.steps
        tile = pl.BlockSpec((step, self.width), lambda i: (i, 0))
        low = pl.BlockSpec((step, self.width), lambda i: (jnp.minimum(i, n // 2 - 1), 0))
        high = pl.BlockSpec((step, self.width), lambda i: (jnp.maximum(i - n // 2, 0), 0))
        line = pl.BlockSpec((1, self.width), lambda i: (0, 0))
        part = pl.BlockSpec((8, self.width), lambda i: (0, 0))
        shape = jax.ShapeDtypeStruct
        gains = [] if gain is None else [gain.reshape(1, self.width)]
        return pl.pallas_call(
            kernel,
            grid=(n,),
            in_specs=([tile, low, low, high, high] if pieces else []) + [tile] * len(arrays) + [line] * len(gains),
            out_specs=[part if t is None else tile for t in outs],
            out_shape=[
                shape((8, self.width), F32) if t is None else shape((self.rows, self.width), t) for t in outs
            ],
            compiler_params=pltpu.CompilerParams(vmem_limit_bytes=VMEM_BYTES),
        )(*pieces, *arrays, *gains)


def pair_pack_kernel(a_ref, b_ref, out_ref, *, block, part):
    group = out_ref.shape[0]
    for n in range(group):
        at = group * block + n * part
        out_ref[n, :, :block] = a_ref[:, n * block : (n + 1) * block]
        out_ref[n, :, block : 2 * block] = b_ref[:, n * block : (n + 1) * block]
        parts = [ref[:, at : at + part].astype(F32) for ref in (a_ref, b_ref)]
        out_ref[n, :, 2 * block :] = jnp.concatenate(parts, axis=1).astype(BF)


def ff_pack_kernel(gate_ref, up_ref, out_ref, *, cuts):
    n_dp, n_z, n_core = cuts
    w = gate_ref.shape[1] // (n_dp * n_z * n_core)
    for d in range(n_dp):
        for c in range(n_core):
            for j, ref in enumerate((gate_ref, up_ref)):
                cols = [((d * n_z + z) * n_core + c) * w for z in range(n_z)]
                x = jnp.concatenate([ref[:, o : o + w].astype(F32) for o in cols], axis=1)
                out_ref[d * n_core + c, :, j * n_z * w : (j + 1) * n_z * w] = x.astype(BF)


def ff_unpack_kernel(x_ref, gate_ref, up_ref, *, cuts):
    n_dp, n_z, n_core = cuts
    w = gate_ref.shape[1] // (n_dp * n_z * n_core)
    for j, ref in enumerate((gate_ref, up_ref)):
        for d in range(n_dp):
            cols = []
            for z in range(n_z):
                for c in range(n_core):
                    o = (j * n_z + z) * w
                    cols.append(x_ref[d * n_core + c, :, o : o + w].astype(F32))
            span = n_z * n_core * w
            ref[:, d * span : (d + 1) * span] = jnp.concatenate(cols, axis=1)


class Blocks:
    def __init__(self, peers, lines, seqs, back):
        self.peers, self.lines, self.seqs, self.back = peers, lines, seqs, back

    def core(self, c):
        return self.peers - 1 - c if self.back else c

    def block(self, d, s, c, core):
        return (jnp.bitwise_xor(c, core[0]) * self.lines + d) * self.seqs + s

    def rows(self, count, width):
        return pl.BlockSpec((count, width), lambda d, s, c, core: (self.block(d, s, self.core(c), core), 0))

    def before(self, count, width, length):
        each = length // count

        def index(d, s, c, core):
            return (self.block(d, s, jnp.maximum(self.core(c) - 1, 0), core) * each + each - 1, 0)

        return pl.BlockSpec((count, width), index)

    def sequence(self, count, width):
        return pl.BlockSpec((count, width), lambda d, s, c, core: (d * self.seqs + s, 0))

    def whole(self, *shape):
        return pl.BlockSpec(shape, lambda d, s, c, core: (0,) * len(shape))

    def call(self, kernel, in_specs, out_specs, out_shape, scratch, *args):
        return pl.pallas_call(
            kernel,
            grid_spec=pltpu.PrefetchScalarGridSpec(
                num_scalar_prefetch=1,
                grid=(self.lines, self.seqs, self.peers),
                in_specs=in_specs,
                out_specs=out_specs,
                scratch_shapes=scratch,
            ),
            out_shape=out_shape,
            compiler_params=pltpu.CompilerParams(vmem_limit_bytes=VMEM_BYTES),
        )(*args)


class Plane:
    def __init__(self, n_dp, n_core):
        self.n_dp, self.n_core = n_dp, n_core
        self.core = lax.axis_index("core")
        self.dp = lax.axis_index("dp")

    def near(self, x, k):
        return lax.ppermute(x, "dp", [(i, i ^ k) for i in range(self.n_dp)])

    def twin(self, x):
        return lax.ppermute(x, "core", [(0, 1), (1, 0)])

    def pieces(self, x, late=()):
        half = x.shape[0] // 2
        x1, x2 = self.near(x, 1), self.near(x, 2)
        if late:
            x1, x2 = lax.optimization_barrier((x1, x2, *late))[:2]
        x3 = jnp.concatenate([self.near(x2[:half], 1), self.near(x1[half:], 2)], axis=0)
        mine = [x, x1, x2, x3]
        return mine + [self.twin(m) for m in mine]

    def gather(self, x, late=()):
        return jnp.concatenate(self.pieces(x, late), axis=0)

    def terms(self, product, rows):
        n = self.n_dp
        halves = ((n // 2, n), (0, n // 2))
        other = [self.twin(product((n + lo) * rows, (n + hi) * rows).astype(BF)) for lo, hi in halves]
        far, near = (product(lo * rows, hi * rows) + x.astype(F32) for (lo, hi), x in zip(halves, other))
        far = far.astype(BF)
        return [x[k * rows : (k + 1) * rows] for x in (near, far) for k in range(n // 2)]

    def send_first(self, q):
        half = q[0].shape[0] // 2
        low = lambda x: x.astype(BF)
        a3, b3 = self.near(q[3][:half], 1), self.near(q[3][half:], 2)
        a1, b2 = self.near(low(q[1][:half]), 1), self.near(q[2][half:], 2)
        return a3, b3, a1, b2

    def add_up(self, q, first=None, late=()):
        half = q[0].shape[0] // 2
        low = lambda x: x.astype(BF)
        a3, b3, a1, b2 = first or self.send_first(q)
        q2, q1 = (after(q[2], *late), after(q[1], *late)) if late else (q[2], q[1])
        self.second = (low(q2[:half].astype(F32) + a3.astype(F32)), low(q1[half:] + b3.astype(F32)))
        a, b = self.near(self.second[0], 2), self.near(self.second[1], 1)
        return q[0], a1, a, b2, b

    def scatter(self, product, rows):
        return self.add_up(self.terms(product, rows))

    def in_order(self, x):
        x = jnp.where(self.core == 1, x[::-1], x)
        for bit in (1, 2):
            y = x.reshape(2, self.n_dp // (2 * bit), 2, bit, *x.shape[2:])
            x = jnp.where((self.dp & bit) != 0, y[:, :, ::-1], y).reshape(x.shape)
        return jnp.swapaxes(x, 0, 1)


def body(
    tokens, doc_reset, cotangent, norm_gain, input_proj, branch_proj, conv_kernel, conv_bias, gate_weight, gate_bias,
    decay_param, output_proj, ffn_gain, ffn_gate, ffn_up, ffn_down,
):
    seqs, span, width = tokens.shape
    rows = seqs * span
    n_dp, n_z, n_core = (lax.axis_size(a) for a in EVERY)
    group = n_dp * n_core
    devices = group * n_z
    zi = lax.axis_index("z")
    me = lax.axis_index("dp") * n_core + lax.axis_index("core")
    rec = input_proj.shape[1]
    ff = ffn_gate.shape[1]
    block = gate_weight.shape[2]
    taps = conv_kernel.shape[0]
    drow = input_proj.shape[0]
    frow = ffn_down.shape[0]
    ff_own = ff // group
    blocks = rec // block
    shared = blocks - group
    sharers = group // shared
    part = block // sharers
    lanes = 128 * (-(-part // 128))
    own = block + lanes
    window = 2 * block
    total_rows = group * rows
    lines = n_dp * seqs

    plane = Plane(n_dp, n_core)
    core = plane.core
    core_id = core.astype(jnp.int32).reshape(1)

    def window_columns(w):
        lead = w.shape[0]
        full = w[:, : group * block].reshape(lead, group, block)
        rest = w[:, group * block :].reshape(lead, shared, block)
        turned = jnp.stack([jnp.roll(rest, -part * q, axis=2) for q in range(sharers)], axis=2)
        return jnp.concatenate([full, turned.reshape(lead, group, block)], axis=2)

    def exchange(x):
        return lax.all_to_all(x, GROUP, split_axis=0, concat_axis=0, tiled=True)

    def to_members(x):
        y = jnp.swapaxes(x, 0, 1)
        return exchange(y.reshape(group * x.shape[0], x.shape[2]))

    def sum_z(x):
        return lax.psum_scatter(x, "z", scatter_dimension=0, tiled=True)

    def over_z(x):
        return lax.all_gather(x, "z", axis=0, tiled=True)

    cuts = (n_dp, n_z)
    cot = cotangent.reshape(rows, width)
    tok = tokens.reshape(rows, width)
    tok_pieces = plane.pieces(tok)
    rrow = rec // devices
    vectors = jnp.concatenate(
        [norm_gain, ffn_gain, conv_kernel.reshape(-1), conv_bias, gate_bias.reshape(-1), decay_param]
    )
    small_len = vectors.shape[0]
    vectors = jnp.pad(vectors, (0, -small_len % 256)).reshape(-1, 256)
    gates_rows = 2 * rrow * block // 256
    marks_at = gates_rows + vectors.shape[0]
    marks = (1 - doc_reset).astype(BF).reshape(-1, 256)
    small = jnp.concatenate([gate_weight.reshape(gates_rows, 256), vectors, marks], axis=0)
    small = jnp.pad(small, ((0, -small.shape[0] % 32), (0, 0)))
    packed = small.shape[0]
    sent_in = to_members(window_columns(input_proj))
    small = over_z(after(small, sent_in))

    def pair(a, b):
        cut = block + part
        return jnp.concatenate([a[..., :block], b[..., :block], a[..., block:cut], b[..., block:cut]], axis=-1)

    def unpair(x, k):
        at = 2 * block + k * part
        return jnp.concatenate([x[..., k * block : (k + 1) * block], x[..., at : at + part]], axis=-1)

    both = pl.pallas_call(
        functools.partial(pair_pack_kernel, block=block, part=part),
        out_shape=jax.ShapeDtypeStruct((group, drow, 2 * (block + part)), BF),
        compiler_params=pltpu.CompilerParams(vmem_limit_bytes=VMEM_BYTES),
    )(branch_proj, output_proj.T)
    sent_both = exchange(after(both, small).reshape(group * drow, 2 * (block + part)))
    ff_packed = pl.pallas_call(
        functools.partial(ff_pack_kernel, cuts=(n_dp, n_z, n_core)),
        out_shape=jax.ShapeDtypeStruct((group, drow, 2 * ff_own), BF),
        compiler_params=pltpu.CompilerParams(vmem_limit_bytes=VMEM_BYTES),
    )(ffn_gate, ffn_up)
    w_in = over_z(sent_in)
    w_both = over_z(sent_both)
    w_branch, w_out = (jnp.pad(unpair(w_both, k), ((0, 0), (0, lanes - part))) for k in range(2))
    small = plane.gather(small, [sent_both]).reshape(n_core, n_dp, n_z, packed, 256)
    keep = lax.dynamic_index_in_dim(small, zi, 2, False)[:, :, marks_at : marks_at + rows // 256]
    keep = keep.astype(F32).reshape(total_rows, 1)
    ff_packed, small = lax.optimization_barrier((ff_packed, small))
    sent_ff = exchange(ff_packed.reshape(group * drow, 2 * ff_own))
    rest = small[:, :, :, gates_rows:marks_at]
    rest = jnp.swapaxes(plane.in_order(rest), 1, 2).reshape(devices, -1)[:, :small_len].astype(F32)
    gain = rest[:, :drow].reshape(width)
    fgain = rest[:, drow : 2 * drow].reshape(width)
    chan = rest[:, 2 * drow :].reshape(devices, taps + 4, rrow)
    chan = jnp.swapaxes(chan, 0, 1).reshape(taps + 4, rec)
    lam = chan[taps + 3 :]
    chan = jnp.concatenate([chan[: taps + 3], -POWER * jax.nn.softplus(-lam)], axis=0)

    quarter = me % sharers
    shared_at = (group + me // sharers) * block

    def my_window(x, axis):
        full = lax.dynamic_slice_in_dim(x, me * block, block, axis)
        other = lax.dynamic_slice_in_dim(x, shared_at, block, axis)
        turned = lax.dynamic_slice_in_dim(jnp.concatenate([other, other], axis), quarter * part, block, axis)
        return full, turned

    vec = jnp.concatenate(my_window(chan, 1), axis=1)
    mine = OwnRows(rows, width)
    normed = pl.pallas_call(
        functools.partial(norm_kernel, cuts=cuts),
        grid=(group,),
        in_specs=[pl.BlockSpec((1, width), lambda i: (0, 0))] + [pl.BlockSpec((rows, width), lambda i: (0, 0))] * group,
        out_specs=pl.BlockSpec((rows, width), lambda i: (i, 0)),
        out_shape=jax.ShapeDtypeStruct((total_rows, width), BF),
        compiler_params=pltpu.CompilerParams(vmem_limit_bytes=VMEM_BYTES),
    )(gain.reshape(1, width), *tok_pieces)

    normed, small = lax.optimization_barrier((normed, small))
    gates_all = small[:, :, :, :gates_rows].reshape(n_core, n_dp, n_z, 2, rrow * block // 256, 256)
    gates_all = jnp.transpose(plane.in_order(gates_all), (3, 0, 2, 1, 4, 5)).reshape(2, rec, block)
    gw_full, gw_shared = my_window(gates_all, 1)
    gw_shared = lax.dynamic_slice_in_dim(gw_shared, quarter * part, part, 2)
    gw_shared = jnp.pad(gw_shared, ((0, 0), (0, 0), (0, lanes - part)))
    gwf = jnp.concatenate([gw_full[0], gw_full[1]], axis=1)
    gws = jnp.concatenate([gw_shared[0], gw_shared[1]], axis=1)

    inner = dot(normed, w_in).astype(BF)
    cot_here, inner, sent_ff = lax.optimization_barrier((cot, inner, sent_ff))
    w_ff = over_z(sent_ff)
    w_down = over_z(after(ffn_down, sent_ff))
    branch = dot(normed, w_branch)
    ends = inner.reshape(n_core, n_dp, seqs, span, window)[:, :, :, span - HALO :]
    ends = jnp.where(core == 1, ends[0], ends[1]).reshape(lines * HALO, window)
    halo = lax.ppermute(ends, "z", [(i, i + 1) for i in range(n_z - 1)])

    at = Blocks(n_core, n_dp, seqs, False)
    seq_in = [
        lambda b: b.rows(span, window), lambda b: b.before(HALO, window, span), lambda b: b.sequence(HALO, window),
        lambda b: b.rows(span, 1), lambda b: b.whole(8, window), lambda b: b.whole(block, window),
        lambda b: b.whole(block, 2 * lanes),
    ]
    row_f32 = jax.ShapeDtypeStruct((total_rows, own), F32)
    decay, local, cum, last = at.call(
        functools.partial(forward_kernel, block=block, own=own),
        [f(at) for f in seq_in],
        [at.rows(span, own)] * 3 + [at.sequence(8, own)],
        [row_f32] * 3 + [jax.ShapeDtypeStruct((lines * 8, own), F32)],
        [pltpu.VMEM((span + HALO, window), F32), pltpu.VMEM((span, own), F32), pltpu.VMEM((8, own), F32)],
        core_id, inner, inner, halo, keep, vec, gwf, gws,
    )

    cot_pieces = plane.pieces(cot_here, [last])

    def carried(x, way, beside):
        x = x.reshape(lines, 8, own)[:, :2]
        state = jnp.zeros((lines, own), F32)
        for k in range(n_z - 1, 0, -1):
            hops = [(i, i + way * k) for i in range(n_z) if 0 <= i + way * k < n_z]
            come = after(lax.ppermute(x, "z", hops), *beside)
            state = come[:, 1] * state + come[:, 0]
        return state

    start = carried(last, 1, [branch])

    def by_line(x):
        return x.reshape(1, n_dp, seqs, 1, own)

    def spread(x):
        return x.reshape(n_core, n_dp, seqs, span, own)

    hidden = (spread(local) + spread(cum) * by_line(start)).reshape(total_rows, own)
    mixed_out = (hidden * gelu_only(branch)).astype(BF)
    mixed_out, *cot_pieces = lax.optimization_barrier((mixed_out, *cot_pieces))
    terms = plane.scatter(lambda lo, hi: dot_cols(mixed_out[lo:hi], w_out), rows)
    mid, fnormed = mine.call(functools.partial(mid_kernel, cuts=cuts), terms, [tok], fgain, [F32, BF])

    cot_pieces[0] = after(cot_pieces[0], fnormed)
    cot_all = jnp.concatenate(cot_pieces, axis=0)
    fnormed = plane.gather(fnormed, [cot_all])
    pre_lin = dot(fnormed, w_ff)
    act, slope = gelu_pair(pre_lin[:, :ff_own])
    lin = pre_lin[:, ff_own:]
    fhidden = (act * lin).astype(BF)
    down_terms = dot_rows(fhidden, cot_all).astype(BF)
    hid_grad = dot_cols(after(cot_all, down_terms), w_down)
    fgrad = jnp.concatenate([(hid_grad * lin * slope).astype(BF), (hid_grad * act).astype(BF)], axis=1)
    down_sum = sum_z(down_terms)
    down_out = down_sum.astype(F32)
    terms = plane.terms(lambda lo, hi: dot_cols(fgrad[lo:hi], w_ff), rows)
    ff_terms = dot_rows(fnormed, after(fgrad, down_sum, *terms)).astype(BF)
    terms = plane.add_up(terms)
    ff_sum = sum_z(after(ff_terms, down_sum))
    terms = (after(terms[0], down_sum, ff_terms), *terms[1:])
    mid_grad, mid_low, ffn_gain_part = mine.call(
        functools.partial(mid_back_kernel, cuts=cuts), terms, [mid, cot], fgain, [F32, BF, None]
    )
    later = after(fhidden, mid_grad)
    out_terms = plane.terms(lambda lo, hi: dot(later[lo:hi], w_down), rows)
    ffn_gain_part = jnp.sum(ffn_gain_part, axis=0)
    mid_low = plane.gather(mid_low, [*out_terms, ffn_gain_part, down_out])
    out_terms[3] = after(out_terms[3], mid_low)

    mixed_grad = dot(mid_low, w_out)
    act_r, slope_r = gelu_pair(branch)
    branch_grad = (mixed_grad * hidden * slope_r).astype(BF)
    back = Blocks(n_core, n_dp, seqs, True)
    out_first = plane.send_first(out_terms)
    adj, prod, front = back.call(
        functools.partial(reverse_kernel, own=own),
        [back.rows(span, own)] * 3,
        [back.rows(span, own)] * 2 + [back.sequence(8, own)],
        [row_f32] * 2 + [jax.ShapeDtypeStruct((lines * 8, own), F32)],
        [pltpu.VMEM((8, own), F32)],
        core_id, decay, mixed_grad, branch,
    )
    branch_late, mixed_late, *out_first = lax.optimization_barrier((branch_grad, mixed_out, *out_first, adj))[:6]
    both = pair(dot_rows(normed, branch_late).astype(BF), dot_rows(mid_low, mixed_late).astype(BF))
    both, ff_sum = lax.optimization_barrier((both, ff_sum))
    out_terms = plane.add_up(out_terms, out_first, [both])
    suffix, *out_terms = lax.optimization_barrier((carried(front, -1, [both]), *out_terms))

    def eight(x):
        return jnp.broadcast_to(x[:, None, :], (lines, 8, own)).reshape(lines * 8, own)

    igrad, tail, head, dgf, dgs, sums = back.call(
        functools.partial(backward_kernel, block=block, own=own),
        [f(back) for f in seq_in]
        + [
            back.rows(span, own), back.before(8, own, span), back.sequence(8, own), back.rows(span, own),
            back.rows(span, own), back.sequence(8, own),
        ],
        [
            back.rows(span, window), back.sequence(HALO, window), back.sequence(8, window), back.whole(block, window),
            back.whole(block, 2 * lanes), back.whole(8, window),
        ],
        [
            jax.ShapeDtypeStruct((total_rows, window), BF), jax.ShapeDtypeStruct((lines * HALO, window), F32),
            jax.ShapeDtypeStruct((lines * 8, window), F32), jax.ShapeDtypeStruct((block, window), F32),
            jax.ShapeDtypeStruct((block, 2 * lanes), F32), jax.ShapeDtypeStruct((8, window), F32),
        ],
        [
            pltpu.VMEM((span + HALO, window), F32), pltpu.VMEM((span + 8, own), F32), pltpu.VMEM((span + 8, window), F32),
        ],
        core_id, inner, inner, halo, keep, vec, gwf, gws, hidden, hidden, eight(start), adj, prod, eight(suffix),
    )

    coming = lax.ppermute(head.astype(BF), "z", [(i + 1, i) for i in range(n_z - 1)]).astype(F32).reshape(lines, 8, window)
    fix = jnp.zeros((lines, HALO, window), F32)
    for tap in range(1, taps):
        fix = fix.at[:, HALO - tap :, :].add(vec[tap] * coming[:, :tap])
    tail = (tail.reshape(lines, HALO, window) + fix).astype(BF).reshape(1, n_dp, seqs, HALO, window)
    igrad = lax.dynamic_update_slice(
        igrad.reshape(n_core, n_dp, seqs, span, window), tail, (1 - core, 0, 0, span - HALO, 0)
    ).reshape(total_rows, window)
    ff_part = exchange(ff_sum)
    both_sum = sum_z(after(both, ff_sum))
    igrad = after(igrad, both_sum)
    in_terms = dot_rows(normed, igrad).astype(BF)
    igrad, in_terms, ff_part = lax.optimization_barrier((igrad, in_terms, ff_part))
    terms = plane.terms(
        lambda lo, hi: dot_cols(igrad[lo:hi], w_in) + dot_cols(branch_grad[lo:hi], w_branch), rows
    )
    both_late, ff_part, mid_late = lax.optimization_barrier((both_sum, ff_part, mid, *terms))[:3]
    both_part = exchange(both_late)
    layer_out = mine.call(out_kernel, out_terms, [mid_late], None, [F32])[0]
    gate_out, up_out = pl.pallas_call(
        functools.partial(ff_unpack_kernel, cuts=(n_dp, n_z, n_core)),
        out_shape=[jax.ShapeDtypeStruct((drow, ff), F32)] * 2,
        compiler_params=pltpu.CompilerParams(vmem_limit_bytes=VMEM_BYTES),
    )(ff_part.reshape(group, drow, 2 * ff_own))
    terms = plane.add_up(terms)
    second = plane.second
    first_terms, layer_out, gate_out, up_out, both_part = lax.optimization_barrier(
        (terms[0], layer_out, gate_out, up_out, both_part)
    )
    terms = (first_terms, *terms[1:])
    both_part = both_part.reshape(group, drow, 2 * (block + part))

    def own_natural(x):
        full = jnp.swapaxes(x[:, :, :block], 0, 1).reshape(drow, group * block)
        rest = jnp.swapaxes(x[:, :, block : block + part], 0, 1).reshape(drow, group * part)
        return jnp.concatenate([full, rest], axis=1).astype(F32)

    branch_proj_grad = own_natural(unpair(both_part, 0))
    output_proj_grad = own_natural(unpair(both_part, 1)).T

    def place_window(x, axis_len):
        lead = x.shape[:-1]
        other = x[..., block:]
        turned = lax.dynamic_slice_in_dim(
            jnp.concatenate([other, other], -1), lax.rem(block - quarter * part, block), block, x.ndim - 1
        )
        y = jnp.zeros((*lead, axis_len), x.dtype)
        y = lax.dynamic_update_slice_in_dim(y, x[..., :block], me * block, x.ndim - 1)
        return lax.dynamic_update_slice_in_dim(y, turned, shared_at, x.ndim - 1)

    dg_full = jnp.stack([dgf[:, :block], dgf[:, block:]])
    dg_shared = jnp.stack([dgs[:, :part], dgs[:, lanes : lanes + part]])
    dg_shared = lax.dynamic_slice_in_dim(
        jnp.concatenate([dg_shared, dg_shared], 1), lax.rem(block - quarter * part, block), block, 1
    )
    lot = n_core * rrow
    lots = (block + 2 * lot - 2) // lot

    def by_z(x, row):
        y = jnp.swapaxes(x, 0, 1).reshape(block, -1).astype(BF)
        q = row // lot
        y = lax.dynamic_update_slice(jnp.zeros((n_z * lot, y.shape[1]), BF), y, (row - q * lot, 0))
        y = y.reshape(n_z, lot, -1)
        return lax.dynamic_slice_in_dim(jnp.concatenate([y, y]), lax.rem(n_z - lax.rem(q, n_z), n_z), n_z, 0)

    def to_lines(x, row):
        q = row // lot
        q = q + lax.rem(zi + n_z - lax.rem(q, n_z), n_z)
        y = jnp.zeros((n_dp, *x.shape), x.dtype)
        return lax.dynamic_update_slice(y, x[None], (jnp.minimum(q // n_z, n_dp - 1), 0, 0))

    assert lots <= n_z
    gates = jnp.concatenate([by_z(dg_full, me * block), by_z(dg_shared, shared_at)], axis=2)
    gates = gates.reshape(n_z, lot * 2 * (block + part) // window, window)
    joined = jnp.concatenate([in_terms.reshape(n_z, group * drow, window), gates], axis=1)
    joined = sum_z(after(joined.reshape(-1, window), both_sum))
    joined = after(joined, *second)
    input_grad, gain_part = mine.call(
        functools.partial(tok_back_kernel, cuts=cuts), terms, [tok, mid_grad], gain, [F32, None]
    )
    blocks_z = jnp.swapaxes(jnp.sum(gain_part, axis=0).reshape(n_dp, n_z, n_core * drow), 0, 1).reshape(n_z, group * drow)
    blocks_z = lax.dynamic_slice_in_dim(jnp.concatenate([blocks_z, blocks_z]), zi, n_z, 0)
    gain_sum = blocks_z[0]
    for k in range(1, n_z):
        gain_sum = gain_sum + lax.ppermute(blocks_z[k], "z", [(i, (i + k) % n_z) for i in range(n_z)])
    gain_high = gain_sum.astype(BF)
    gain_low = (gain_sum - gain_high.astype(F32)).astype(BF)
    gain_rows = jnp.concatenate([gain_high.reshape(group, drow), gain_low.reshape(group, drow)], axis=1)
    gain_rows = jnp.pad(gain_rows[:, None, :], ((0, 0), (0, 3), (0, window - 2 * drow)))
    in_part = joined[: group * drow].reshape(group, drow, window)
    gates = joined[group * drow :].reshape(lot, 2 * (block + part))
    gates = jnp.concatenate(
        [to_lines(gates[:, : 2 * block], me * block), to_lines(gates[:, 2 * block :], shared_at)], axis=2
    )
    gates = gates.reshape(group, rrow * 2 * (block + part) // window, window)
    gates_end = drow + gates.shape[1]
    joined = exchange(jnp.concatenate([in_part, gates, gain_rows], axis=1).reshape(-1, window))

    lane = jnp.arange(window)
    mine = lane < block + part
    sums = jnp.where(jnp.concatenate([jnp.ones((5, window), bool), jnp.broadcast_to(mine, (3, window))], axis=0), sums, 0.0)
    sums = place_window(sums, rec)
    sums = jnp.concatenate([sums[:7], sums[7:8] * (POWER * jax.nn.sigmoid(-lam))], axis=0)
    vectors = jnp.concatenate(
        [
            ffn_gain_part.reshape(devices, drow),
            jnp.swapaxes(sums.reshape(8, devices, rrow), 0, 1).reshape(devices, 8 * rrow),
        ],
        axis=1,
    )
    vec_len = vectors.shape[1]
    vectors = lax.all_to_all(vectors, EVERY, split_axis=0, concat_axis=0, tiled=True)
    joined = joined.reshape(group, -1, window)
    in_part = joined[:, :drow]
    gates = joined[:, drow:gates_end].reshape(group, rrow, 2 * (block + part)).astype(F32)
    gain_out = jnp.sum(joined[:, gates_end].astype(F32), axis=0)
    gain_out = gain_out[:drow] + gain_out[drow : 2 * drow]
    vectors = jnp.sum(vectors.reshape(devices, vec_len), axis=0)
    fgain_out = vectors[:drow]
    chan_out = vectors[drow:].reshape(8, rrow)

    gates_out = jnp.sum(gates[:, :, : 2 * block], axis=0).reshape(rrow, 2, block)
    rest = jnp.sum(gates[:, :, 2 * block :].reshape(shared, sharers, rrow, 2, part), axis=0)
    rest = jnp.transpose(rest, (1, 2, 0, 3)).reshape(rrow, 2, block)
    gates_out = jnp.swapaxes(gates_out + rest, 0, 1)

    full = jnp.swapaxes(in_part[:, :, :block], 0, 1).reshape(drow, group * block).astype(F32)
    turned = in_part[:, :, block:window].astype(F32).reshape(shared, sharers, drow, block)
    other = sum(jnp.roll(turned[:, q], part * q, axis=2) for q in range(sharers))
    input_proj_grad = jnp.concatenate([full, jnp.swapaxes(other, 0, 1).reshape(drow, shared * block)], axis=1)

    return (
        layer_out.reshape(seqs, span, width),
        input_grad.reshape(seqs, span, width),
        gain_out,
        input_proj_grad,
        branch_proj_grad,
        chan_out[:taps],
        chan_out[taps],
        gates_out,
        chan_out[taps + 1 : taps + 3],
        chan_out[taps + 3],
        output_proj_grad,
        fgain_out,
        gate_out,
        up_out,
        down_out,
    )


def solution(mesh):
    n_dp, n_seq = mesh.shape["dp"], mesh.shape["seq"]
    split = Mesh(mesh.devices.reshape(n_dp, n_seq // 2, 2), EVERY)
    seq = ("z", "core")
    line = P("dp", seq, None)
    first = P(EVERY)
    rows = P(EVERY, None)
    cols = P(None, EVERY)
    mids = P(None, EVERY, None)
    return jax.shard_map(
        body,
        mesh=split,
        in_specs=(
            line, P("dp", seq), line, first, rows, rows, cols, first, mids, cols, first, cols, first, rows, rows, rows,
        ),
        out_specs=(
            line, line, first, rows, rows, cols, first, mids, cols, first, cols, first, rows, rows, rows,
        ),
        check_vma=False,
    )
```

```python
import functools

import jax
import jax.numpy as jnp
from jax import lax
from jax.experimental import pallas as pl
from jax.experimental.pallas import tpu as pltpu
from jax.sharding import Mesh
from jax.sharding import PartitionSpec as P

EPSILON = 1e-06
POWER = 8.0
BF = jnp.bfloat16
F32 = jnp.float32
GROUP = ("dp", "core")
EVERY = ("dp", "z", "core")
GELU_A = 0.7978845608028654
GELU_B = 0.044715
HALO = 16
VMEM_BYTES = 48 * 1024 * 1024


def after(x, *others):
    return lax.optimization_barrier((x, *others))[0]


def gelu_pair(x):
    x2 = x * x
    th = jnp.tanh(GELU_A * (x + GELU_B * x2 * x))
    half = 0.5 * (1.0 + th)
    slope = half + 0.5 * x * (1.0 - th * th) * (GELU_A * (1.0 + 3.0 * GELU_B * x2))
    return x * half, slope


def gelu_only(x):
    return 0.5 * x * (1.0 + jnp.tanh(GELU_A * (x + GELU_B * x * x * x)))


def dot(a, b):
    return lax.dot_general(a, b, (((1,), (0,)), ((), ())), preferred_element_type=F32)


def dot_rows(a, b):
    return lax.dot_general(a, b, (((0,), (0,)), ((), ())), preferred_element_type=F32)


def dot_cols(a, b):
    return lax.dot_general(a, b, (((1,), (1,)), ((), ())), preferred_element_type=F32)


def minus_expm1(x):
    series = -x * (1.0 + x * (1 / 2) * (1.0 + x * (1 / 3) * (1.0 + x * (1 / 4) * (1.0 + x * (1 / 5) * (1.0 + x * (1 / 6))))))
    return jnp.where(x > -0.125, series, 1.0 - jnp.exp(x))


def conv_and_gates(inner_ref, prev, vec, gwf_ref, gws_ref, ext, block, own):
    rows = inner_ref.shape[0]
    ext[0:HALO, :] = prev.astype(F32)
    ext[HALO : HALO + rows, :] = inner_ref[...].astype(F32)
    conved = vec[4:5, :] + vec[0:1, :] * ext[HALO : HALO + rows, :]
    for tap in range(1, 4):
        conved = conved + vec[tap : tap + 1, :] * ext[HALO - tap : HALO - tap + rows, :]
    rounded = conved.astype(BF)
    gf = dot(rounded[:, :block], gwf_ref[...])
    gs = dot(rounded[:, block:], gws_ref[...])
    part = own - block
    rate_pre = jnp.concatenate([gf[:, :block], gs[:, :part]], axis=1) + vec[5:6, :own]
    open_pre = jnp.concatenate([gf[:, block:], gs[:, part:]], axis=1) + vec[6:7, :own]
    return conved, rounded, rate_pre, open_pre


def scan_groups(a_ref, b_ref, out_h, out_c, h, c, rows, width):
    place = lax.broadcasted_iota(jnp.int32, (8, width), 0)

    def one(g, carry):
        h, c = carry
        at = pl.ds(pl.multiple_of(g * 8, 8), 8)
        a, b = a_ref[at, :], b_ref[at, :]
        for shift in (1, 2, 4):
            keep = place >= shift
            pa = jnp.where(keep, pltpu.roll(a, shift, 0), 1.0)
            pb = jnp.where(keep, pltpu.roll(b, shift, 0), 0.0)
            b = a * pb + b
            a = a * pa
        b = b + a * h
        a = a * c
        out_h[at, :] = b
        out_c[at, :] = a
        return b[7:8, :], a[7:8, :]

    return lax.fori_loop(0, rows // 8, one, (h, c), unroll=4)


def forward_kernel(
    core_ref, inner_ref, prev_ref, halo_ref, keep_ref, vec_ref, gwf_ref, gws_ref,
    decay_ref, local_ref, cum_ref, last_ref, ext, b_ref, carry, *, block, own,
):
    c = pl.program_id(2)
    rows = inner_ref.shape[0]
    prev = jnp.where(c == 0, halo_ref[...].astype(F32), prev_ref[...].astype(F32))
    vec = vec_ref[...]
    conved, _, rate_pre, open_pre = conv_and_gates(inner_ref, prev, vec, gwf_ref, gws_ref, ext, block, own)
    keep = keep_ref[...]
    rate = jax.nn.sigmoid(rate_pre)
    opening = jax.nn.sigmoid(open_pre)
    log_decay = vec[7:8, :own] * rate
    scale = keep * jnp.sqrt(minus_expm1(2.0 * log_decay)) + (1.0 - keep)
    decay_ref[...] = jnp.exp(log_decay) * keep
    b_ref[...] = scale * opening * conved[:, :own]

    @pl.when(c == 0)
    def _():
        carry[0:1, :] = jnp.zeros((1, own), F32)
        carry[1:2, :] = jnp.ones((1, own), F32)

    h, p = scan_groups(decay_ref, b_ref, local_ref, cum_ref, carry[0:1, :], carry[1:2, :], rows, own)
    carry[0:1, :] = h
    carry[1:2, :] = p
    last_ref[...] = carry[...]


def reverse_kernel(core_ref, decay_ref, grad_ref, branch_ref, adj_ref, prod_ref, first_ref, carry, *, own):
    c = pl.program_id(2)
    rows = decay_ref.shape[0]
    place = lax.broadcasted_iota(jnp.int32, (8, own), 0)

    @pl.when(c == 0)
    def _():
        carry[0:1, :] = jnp.zeros((1, own), F32)
        carry[1:2, :] = jnp.ones((1, own), F32)

    def one(i, state):
        s, p = state
        at = pl.ds(pl.multiple_of((rows // 8 - 1 - i) * 8, 8), 8)
        a = decay_ref[at, :]
        hg = grad_ref[at, :] * gelu_only(branch_ref[at, :])
        b = a * hg
        for shift in (1, 2, 4):
            keep = place < 8 - shift
            na = jnp.where(keep, pltpu.roll(a, 8 - shift, 0), 1.0)
            nb = jnp.where(keep, pltpu.roll(b, 8 - shift, 0), 0.0)
            b = a * nb + b
            a = a * na
        b = b + a * s
        a = a * p
        last = place == 7
        adj_ref[at, :] = hg + jnp.where(last, s, pltpu.roll(b, 7, 0))
        prod_ref[at, :] = jnp.where(last, p, pltpu.roll(a, 7, 0))
        return b[0:1, :], a[0:1, :]

    s, p = lax.fori_loop(0, rows // 8, one, (carry[0:1, :], carry[1:2, :]), unroll=4)
    carry[0:1, :] = s
    carry[1:2, :] = p
    first_ref[...] = carry[...]


def backward_kernel(
    core_ref, inner_ref, prev_ref, halo_ref, keep_ref, vec_ref, gwf_ref, gws_ref, hidden_ref, before_ref, start_ref,
    adj_ref, prod_ref, suffix_ref,
    igrad_ref, tail_ref, head_ref, dgf_ref, dgs_ref, sums_ref, ext, hext, cext, *, block, own,
):
    c = pl.program_id(2)
    peers = pl.num_programs(2)
    first = (pl.program_id(0) == 0) & (pl.program_id(1) == 0) & (c == 0)
    at_start = c == peers - 1
    rows = inner_ref.shape[0]
    part = own - block
    window = vec_ref.shape[1]

    @pl.when(first)
    def _():
        dgf_ref[...] = jnp.zeros_like(dgf_ref)
        dgs_ref[...] = jnp.zeros_like(dgs_ref)
        sums_ref[...] = jnp.zeros_like(sums_ref)

    @pl.when(c == 0)
    def _():
        cext[rows : rows + 8, :] = jnp.zeros((8, window), F32)

    @pl.when(c > 0)
    def _():
        cext[rows : rows + 8, :] = cext[0:8, :]

    prev = jnp.where(at_start, halo_ref[...].astype(F32), prev_ref[...].astype(F32))
    vec = vec_ref[...]
    conved, rounded, rate_pre, open_pre = conv_and_gates(inner_ref, prev, vec, gwf_ref, gws_ref, ext, block, own)
    keep = keep_ref[...]
    conv = conved[:, :own]
    rate = jax.nn.sigmoid(rate_pre)
    opening = jax.nn.sigmoid(open_pre)
    factor = vec[7:8, :own]
    log_decay = factor * rate
    e = jnp.exp(log_decay)
    root = jnp.sqrt(minus_expm1(2.0 * log_decay))
    scale = keep * root + (1.0 - keep)

    adj = adj_ref[...] + prod_ref[...] * suffix_ref[0:1, :]
    hext[0:8, :] = jnp.where(at_start, jnp.broadcast_to(start_ref[0:1, :], (8, own)), before_ref[...])
    hext[8 : 8 + rows, :] = hidden_ref[...]
    before = hext[7 : 7 + rows, :]
    d_log = keep * (adj * before * e - adj * opening * conv * (e * e) / root)
    direct = adj * scale * opening
    g_rate = (d_log * factor * rate * (1.0 - rate)).astype(BF)
    g_open = (adj * scale * conv * opening * (1.0 - opening)).astype(BF)
    gf = jnp.concatenate([g_rate[:, :block], g_open[:, :block]], axis=1)
    gs = jnp.concatenate([g_rate[:, block:], g_open[:, block:]], axis=1)
    cgrad = jnp.concatenate([dot_cols(gf, gwf_ref[...]), dot_cols(gs, gws_ref[...])], axis=1)
    cgrad = cgrad + jnp.concatenate([direct, jnp.zeros((rows, window - own), F32)], axis=1)
    cext[0:rows, :] = cgrad
    dgf_ref[...] += dot_rows(rounded[:, :block], gf)
    dgs_ref[...] += dot_rows(rounded[:, block:], gs)

    igrad = vec[0:1, :] * cgrad
    for tap in range(1, 4):
        igrad = igrad + vec[tap : tap + 1, :] * cext[tap : tap + rows, :]
    igrad_ref[...] = igrad.astype(BF)

    @pl.when(c == 0)
    def _():
        tail_ref[...] = igrad[rows - HALO :, :]

    head_ref[...] = cgrad[0:8, :]

    def total(x):
        return jnp.sum(x, axis=0, keepdims=True)

    for tap in range(4):
        sums_ref[tap : tap + 1, :] += total(ext[HALO - tap : HALO - tap + rows, :] * cgrad)
    sums_ref[4:5, :] += total(cgrad)
    sums_ref[5:6, :own] += total(g_rate.astype(F32))
    sums_ref[6:7, :own] += total(g_open.astype(F32))
    sums_ref[7:8, :own] += total(d_log * rate)


def lane_blocks(n_dp, n_z):
    return [(d * n_z + z, z * n_dp + d) for d in range(n_dp) for z in range(n_z)]


def to_z(x, n_dp, n_z):
    w = x.shape[1] // (n_dp * n_z)
    pairs = sorted(lane_blocks(n_dp, n_z), key=lambda p: p[1])
    return jnp.concatenate([x[:, a * w : (a + 1) * w] for a, _ in pairs], axis=1)


def from_z(x, n_dp, n_z):
    w = x.shape[1] // (n_dp * n_z)
    return jnp.concatenate([x[:, b * w : (b + 1) * w] for _, b in lane_blocks(n_dp, n_z)], axis=1)


def total(pieces, i, steps):
    q, ax, a, bx, b = pieces
    low = i < steps // 2
    pick = lambda u, v: jnp.where(low, u[...].astype(F32), v[...].astype(F32))
    return q[...] + pick(ax, bx) + pick(a, b)


def inverse(x):
    return lax.rsqrt(jnp.mean(x * x, axis=1, keepdims=True) + EPSILON)


def norm_kernel(gain_ref, *refs, cuts):
    out_ref = refs[-1]
    for k, ref in enumerate(refs[:-1]):

        @pl.when(pl.program_id(0) == k)
        def _(ref=ref):
            x = ref[...].astype(F32)
            out_ref[...] = to_z(x * inverse(x) * gain_ref[...], *cuts).astype(BF)


def mid_kernel(q, ax, a, bx, b, tok_ref, gain_ref, mid_ref, normed_ref, *, cuts):
    i = pl.program_id(0)
    x = tok_ref[...].astype(F32) + from_z(total((q, ax, a, bx, b), i, pl.num_programs(0)), *cuts)
    mid_ref[...] = x
    normed_ref[...] = to_z(x * inverse(x) * gain_ref[...], *cuts).astype(BF)


def norm_back(grad, x, gain):
    inv = inverse(x)
    g = grad * gain
    return inv * g - x * (inv * inv * inv) * jnp.mean(x * g, axis=1, keepdims=True), grad * x * inv


def add_rows(ref, x):
    first = pl.program_id(0) == 0
    terms = jnp.sum(x.reshape(-1, 8, x.shape[1]), axis=0)

    @pl.when(first)
    def _():
        ref[...] = terms

    @pl.when(jnp.logical_not(first))
    def _():
        ref[...] += terms


def mid_back_kernel(q, ax, a, bx, b, mid_ref, cot_ref, gain_ref, grad_ref, low_ref, part_ref, *, cuts):
    i = pl.program_id(0)
    g = from_z(total((q, ax, a, bx, b), i, pl.num_programs(0)), *cuts)
    back, part = norm_back(g, mid_ref[...], gain_ref[...])
    grad = cot_ref[...].astype(F32) + back
    grad_ref[...] = grad
    low_ref[...] = to_z(grad, *cuts).astype(BF)
    add_rows(part_ref, part)


def tok_back_kernel(q, ax, a, bx, b, tok_ref, mid_grad_ref, gain_ref, grad_ref, part_ref, *, cuts):
    i = pl.program_id(0)
    g = from_z(total((q, ax, a, bx, b), i, pl.num_programs(0)), *cuts)
    back, part = norm_back(g, tok_ref[...].astype(F32), gain_ref[...])
    grad_ref[...] = mid_grad_ref[...] + back
    add_rows(part_ref, part)


def out_kernel(q, ax, a, bx, b, mid_ref, out_ref):
    out_ref[...] = mid_ref[...] + total((q, ax, a, bx, b), pl.program_id(0), pl.num_programs(0))


class OwnRows:
    def __init__(self, rows, width, steps=4):
        self.rows, self.width, self.steps = rows, width, steps

    def call(self, kernel, pieces, arrays, gain, outs):
        n, step = self.steps, self.rows // self.steps
        tile = pl.BlockSpec((step, self.width), lambda i: (i, 0))
        low = pl.BlockSpec((step, self.width), lambda i: (jnp.minimum(i, n // 2 - 1), 0))
        high = pl.BlockSpec((step, self.width), lambda i: (jnp.maximum(i - n // 2, 0), 0))
        line = pl.BlockSpec((1, self.width), lambda i: (0, 0))
        part = pl.BlockSpec((8, self.width), lambda i: (0, 0))
        shape = jax.ShapeDtypeStruct
        gains = [] if gain is None else [gain.reshape(1, self.width)]
        return pl.pallas_call(
            kernel,
            grid=(n,),
            in_specs=([tile, low, low, high, high] if pieces else []) + [tile] * len(arrays) + [line] * len(gains),
            out_specs=[part if t is None else tile for t in outs],
            out_shape=[
                shape((8, self.width), F32) if t is None else shape((self.rows, self.width), t) for t in outs
            ],
            compiler_params=pltpu.CompilerParams(vmem_limit_bytes=VMEM_BYTES),
        )(*pieces, *arrays, *gains)


def pair_pack_kernel(a_ref, b_ref, out_ref, *, block, part):
    group = out_ref.shape[0]
    for n in range(group):
        at = group * block + n * part
        out_ref[n, :, :block] = a_ref[:, n * block : (n + 1) * block]
        out_ref[n, :, block : 2 * block] = b_ref[:, n * block : (n + 1) * block]
        parts = [ref[:, at : at + part].astype(F32) for ref in (a_ref, b_ref)]
        out_ref[n, :, 2 * block :] = jnp.concatenate(parts, axis=1).astype(BF)


def ff_pack_kernel(gate_ref, up_ref, out_ref, *, cuts):
    n_dp, n_z, n_core = cuts
    w = gate_ref.shape[1] // (n_dp * n_z * n_core)
    for d in range(n_dp):
        for c in range(n_core):
            for j, ref in enumerate((gate_ref, up_ref)):
                cols = [((d * n_z + z) * n_core + c) * w for z in range(n_z)]
                x = jnp.concatenate([ref[:, o : o + w].astype(F32) for o in cols], axis=1)
                out_ref[d * n_core + c, :, j * n_z * w : (j + 1) * n_z * w] = x.astype(BF)


def ff_unpack_kernel(x_ref, gate_ref, up_ref, *, cuts):
    n_dp, n_z, n_core = cuts
    w = gate_ref.shape[1] // (n_dp * n_z * n_core)
    for j, ref in enumerate((gate_ref, up_ref)):
        for d in range(n_dp):
            cols = []
            for z in range(n_z):
                for c in range(n_core):
                    o = (j * n_z + z) * w
                    cols.append(x_ref[d * n_core + c, :, o : o + w].astype(F32))
            span = n_z * n_core * w
            ref[:, d * span : (d + 1) * span] = jnp.concatenate(cols, axis=1)


class Blocks:
    def __init__(self, peers, lines, seqs, back):
        self.peers, self.lines, self.seqs, self.back = peers, lines, seqs, back

    def core(self, c):
        return self.peers - 1 - c if self.back else c

    def block(self, d, s, c, core):
        return (jnp.bitwise_xor(c, core[0]) * self.lines + d) * self.seqs + s

    def rows(self, count, width):
        return pl.BlockSpec((count, width), lambda d, s, c, core: (self.block(d, s, self.core(c), core), 0))

    def before(self, count, width, length):
        each = length // count

        def index(d, s, c, core):
            return (self.block(d, s, jnp.maximum(self.core(c) - 1, 0), core) * each + each - 1, 0)

        return pl.BlockSpec((count, width), index)

    def sequence(self, count, width):
        return pl.BlockSpec((count, width), lambda d, s, c, core: (d * self.seqs + s, 0))

    def whole(self, *shape):
        return pl.BlockSpec(shape, lambda d, s, c, core: (0,) * len(shape))

    def call(self, kernel, in_specs, out_specs, out_shape, scratch, *args):
        return pl.pallas_call(
            kernel,
            grid_spec=pltpu.PrefetchScalarGridSpec(
                num_scalar_prefetch=1,
                grid=(self.lines, self.seqs, self.peers),
                in_specs=in_specs,
                out_specs=out_specs,
                scratch_shapes=scratch,
            ),
            out_shape=out_shape,
            compiler_params=pltpu.CompilerParams(vmem_limit_bytes=VMEM_BYTES),
        )(*args)


class Plane:
    def __init__(self, n_dp, n_core):
        self.n_dp, self.n_core = n_dp, n_core
        self.core = lax.axis_index("core")
        self.dp = lax.axis_index("dp")

    def near(self, x, k):
        return lax.ppermute(x, "dp", [(i, i ^ k) for i in range(self.n_dp)])

    def twin(self, x):
        return lax.ppermute(x, "core", [(0, 1), (1, 0)])

    def pieces(self, x, late=()):
        half = x.shape[0] // 2
        x1, x2 = self.near(x, 1), self.near(x, 2)
        if late:
            x1, x2 = lax.optimization_barrier((x1, x2, *late))[:2]
        x3 = jnp.concatenate([self.near(x2[:half], 1), self.near(x1[half:], 2)], axis=0)
        mine = [x, x1, x2, x3]
        return mine + [self.twin(m) for m in mine]

    def gather(self, x, late=()):
        return jnp.concatenate(self.pieces(x, late), axis=0)

    def terms(self, product, rows):
        n = self.n_dp
        halves = ((n // 2, n), (0, n // 2))
        other = [self.twin(product((n + lo) * rows, (n + hi) * rows).astype(BF)) for lo, hi in halves]
        far, near = (product(lo * rows, hi * rows) + x.astype(F32) for (lo, hi), x in zip(halves, other))
        far = far.astype(BF)
        return [x[k * rows : (k + 1) * rows] for x in (near, far) for k in range(n // 2)]

    def send_first(self, q):
        half = q[0].shape[0] // 2
        low = lambda x: x.astype(BF)
        a3, b3 = self.near(q[3][:half], 1), self.near(q[3][half:], 2)
        a1, b2 = self.near(low(q[1][:half]), 1), self.near(q[2][half:], 2)
        return a3, b3, a1, b2

    def add_up(self, q, first=None, late=()):
        half = q[0].shape[0] // 2
        low = lambda x: x.astype(BF)
        a3, b3, a1, b2 = first or self.send_first(q)
        q2, q1 = (after(q[2], *late), after(q[1], *late)) if late else (q[2], q[1])
        self.second = (low(q2[:half].astype(F32) + a3.astype(F32)), low(q1[half:] + b3.astype(F32)))
        a, b = self.near(self.second[0], 2), self.near(self.second[1], 1)
        return q[0], a1, a, b2, b

    def scatter(self, product, rows):
        return self.add_up(self.terms(product, rows))

    def in_order(self, x):
        x = jnp.where(self.core == 1, x[::-1], x)
        for bit in (1, 2):
            y = x.reshape(2, self.n_dp // (2 * bit), 2, bit, *x.shape[2:])
            x = jnp.where((self.dp & bit) != 0, y[:, :, ::-1], y).reshape(x.shape)
        return jnp.swapaxes(x, 0, 1)


def body(
    tokens, doc_reset, cotangent, norm_gain, input_proj, branch_proj, conv_kernel, conv_bias, gate_weight, gate_bias,
    decay_param, output_proj, ffn_gain, ffn_gate, ffn_up, ffn_down,
):
    seqs, span, width = tokens.shape
    rows = seqs * span
    n_dp, n_z, n_core = (lax.axis_size(a) for a in EVERY)
    group = n_dp * n_core
    devices = group * n_z
    zi = lax.axis_index("z")
    me = lax.axis_index("dp") * n_core + lax.axis_index("core")
    rec = input_proj.shape[1]
    ff = ffn_gate.shape[1]
    block = gate_weight.shape[2]
    taps = conv_kernel.shape[0]
    drow = input_proj.shape[0]
    frow = ffn_down.shape[0]
    ff_own = ff // group
    blocks = rec // block
    shared = blocks - group
    sharers = group // shared
    part = block // sharers
    lanes = 128 * (-(-part // 128))
    own = block + lanes
    window = 2 * block
    total_rows = group * rows
    lines = n_dp * seqs

    plane = Plane(n_dp, n_core)
    core = plane.core
    core_id = core.astype(jnp.int32).reshape(1)

    def window_columns(w):
        lead = w.shape[0]
        full = w[:, : group * block].reshape(lead, group, block)
        rest = w[:, group * block :].reshape(lead, shared, block)
        turned = jnp.stack([jnp.roll(rest, -part * q, axis=2) for q in range(sharers)], axis=2)
        return jnp.concatenate([full, turned.reshape(lead, group, block)], axis=2)

    def exchange(x):
        return lax.all_to_all(x, GROUP, split_axis=0, concat_axis=0, tiled=True)

    def to_members(x):
        y = jnp.swapaxes(x, 0, 1)
        return exchange(y.reshape(group * x.shape[0], x.shape[2]))

    def sum_z(x):
        return lax.psum_scatter(x, "z", scatter_dimension=0, tiled=True)

    def over_z(x):
        return lax.all_gather(x, "z", axis=0, tiled=True)

    cuts = (n_dp, n_z)
    cot = cotangent.reshape(rows, width)
    tok = tokens.reshape(rows, width)
    tok_pieces = plane.pieces(tok)
    rrow = rec // devices
    vectors = jnp.concatenate(
        [norm_gain, ffn_gain, conv_kernel.reshape(-1), conv_bias, gate_bias.reshape(-1), decay_param]
    )
    small_len = vectors.shape[0]
    vectors = jnp.pad(vectors, (0, -small_len % 256)).reshape(-1, 256)
    gates_rows = 2 * rrow * block // 256
    marks_at = gates_rows + vectors.shape[0]
    marks = (1 - doc_reset).astype(BF).reshape(-1, 256)
    small = jnp.concatenate([gate_weight.reshape(gates_rows, 256), vectors, marks], axis=0)
    small = jnp.pad(small, ((0, -small.shape[0] % 32), (0, 0)))
    packed = small.shape[0]
    sent_in = to_members(window_columns(input_proj))
    small = over_z(after(small, sent_in))

    def pair(a, b):
        cut = block + part
        return jnp.concatenate([a[..., :block], b[..., :block], a[..., block:cut], b[..., block:cut]], axis=-1)

    def unpair(x, k):
        at = 2 * block + k * part
        return jnp.concatenate([x[..., k * block : (k + 1) * block], x[..., at : at + part]], axis=-1)

    both = pl.pallas_call(
        functools.partial(pair_pack_kernel, block=block, part=part),
        out_shape=jax.ShapeDtypeStruct((group, drow, 2 * (block + part)), BF),
        compiler_params=pltpu.CompilerParams(vmem_limit_bytes=VMEM_BYTES),
    )(branch_proj, output_proj.T)
    sent_both = exchange(after(both, small).reshape(group * drow, 2 * (block + part)))
    ff_packed = pl.pallas_call(
        functools.partial(ff_pack_kernel, cuts=(n_dp, n_z, n_core)),
        out_shape=jax.ShapeDtypeStruct((group, drow, 2 * ff_own), BF),
        compiler_params=pltpu.CompilerParams(vmem_limit_bytes=VMEM_BYTES),
    )(ffn_gate, ffn_up)
    w_in = over_z(sent_in)
    w_both = over_z(sent_both)
    w_branch, w_out = (jnp.pad(unpair(w_both, k), ((0, 0), (0, lanes - part))) for k in range(2))
    small = plane.gather(small, [sent_both]).reshape(n_core, n_dp, n_z, packed, 256)
    keep = lax.dynamic_index_in_dim(small, zi, 2, False)[:, :, marks_at : marks_at + rows // 256]
    keep = keep.astype(F32).reshape(total_rows, 1)
    ff_packed, small = lax.optimization_barrier((ff_packed, small))
    sent_ff = exchange(ff_packed.reshape(group * drow, 2 * ff_own))
    rest = small[:, :, :, gates_rows:marks_at]
    rest = jnp.swapaxes(plane.in_order(rest), 1, 2).reshape(devices, -1)[:, :small_len].astype(F32)
    gain = rest[:, :drow].reshape(width)
    fgain = rest[:, drow : 2 * drow].reshape(width)
    chan = rest[:, 2 * drow :].reshape(devices, taps + 4, rrow)
    chan = jnp.swapaxes(chan, 0, 1).reshape(taps + 4, rec)
    lam = chan[taps + 3 :]
    chan = jnp.concatenate([chan[: taps + 3], -POWER * jax.nn.softplus(-lam)], axis=0)

    quarter = me % sharers
    shared_at = (group + me // sharers) * block

    def my_window(x, axis):
        full = lax.dynamic_slice_in_dim(x, me * block, block, axis)
        other = lax.dynamic_slice_in_dim(x, shared_at, block, axis)
        turned = lax.dynamic_slice_in_dim(jnp.concatenate([other, other], axis), quarter * part, block, axis)
        return full, turned

    vec = jnp.concatenate(my_window(chan, 1), axis=1)
    mine = OwnRows(rows, width)
    normed = pl.pallas_call(
        functools.partial(norm_kernel, cuts=cuts),
        grid=(group,),
        in_specs=[pl.BlockSpec((1, width), lambda i: (0, 0))] + [pl.BlockSpec((rows, width), lambda i: (0, 0))] * group,
        out_specs=pl.BlockSpec((rows, width), lambda i: (i, 0)),
        out_shape=jax.ShapeDtypeStruct((total_rows, width), BF),
        compiler_params=pltpu.CompilerParams(vmem_limit_bytes=VMEM_BYTES),
    )(gain.reshape(1, width), *tok_pieces)

    normed, small = lax.optimization_barrier((normed, small))
    gates_all = small[:, :, :, :gates_rows].reshape(n_core, n_dp, n_z, 2, rrow * block // 256, 256)
    gates_all = jnp.transpose(plane.in_order(gates_all), (3, 0, 2, 1, 4, 5)).reshape(2, rec, block)
    gw_full, gw_shared = my_window(gates_all, 1)
    gw_shared = lax.dynamic_slice_in_dim(gw_shared, quarter * part, part, 2)
    gw_shared = jnp.pad(gw_shared, ((0, 0), (0, 0), (0, lanes - part)))
    gwf = jnp.concatenate([gw_full[0], gw_full[1]], axis=1)
    gws = jnp.concatenate([gw_shared[0], gw_shared[1]], axis=1)

    inner = dot(normed, w_in).astype(BF)
    cot_here, inner, sent_ff = lax.optimization_barrier((cot, inner, sent_ff))
    w_ff = over_z(sent_ff)
    w_down = over_z(after(ffn_down, sent_ff))
    branch = dot(normed, w_branch)
    ends = inner.reshape(n_core, n_dp, seqs, span, window)[:, :, :, span - HALO :]
    ends = jnp.where(core == 1, ends[0], ends[1]).reshape(lines * HALO, window)
    halo = lax.ppermute(ends, "z", [(i, i + 1) for i in range(n_z - 1)])

    at = Blocks(n_core, n_dp, seqs, False)
    seq_in = [
        lambda b: b.rows(span, window), lambda b: b.before(HALO, window, span), lambda b: b.sequence(HALO, window),
        lambda b: b.rows(span, 1), lambda b: b.whole(8, window), lambda b: b.whole(block, window),
        lambda b: b.whole(block, 2 * lanes),
    ]
    row_f32 = jax.ShapeDtypeStruct((total_rows, own), F32)
    decay, local, cum, last = at.call(
        functools.partial(forward_kernel, block=block, own=own),
        [f(at) for f in seq_in],
        [at.rows(span, own)] * 3 + [at.sequence(8, own)],
        [row_f32] * 3 + [jax.ShapeDtypeStruct((lines * 8, own), F32)],
        [pltpu.VMEM((span + HALO, window), F32), pltpu.VMEM((span, own), F32), pltpu.VMEM((8, own), F32)],
        core_id, inner, inner, halo, keep, vec, gwf, gws,
    )

    cot_pieces = plane.pieces(cot_here, [last])

    def carried(x, way, beside):
        x = x.reshape(lines, 8, own)[:, :2]
        state = jnp.zeros((lines, own), F32)
        for k in range(n_z - 1, 0, -1):
            hops = [(i, i + way * k) for i in range(n_z) if 0 <= i + way * k < n_z]
            come = after(lax.ppermute(x, "z", hops), *beside)
            state = come[:, 1] * state + come[:, 0]
        return state

    start = carried(last, 1, [branch])

    def by_line(x):
        return x.reshape(1, n_dp, seqs, 1, own)

    def spread(x):
        return x.reshape(n_core, n_dp, seqs, span, own)

    hidden = (spread(local) + spread(cum) * by_line(start)).reshape(total_rows, own)
    mixed_out = (hidden * gelu_only(branch)).astype(BF)
    mixed_out, *cot_pieces = lax.optimization_barrier((mixed_out, *cot_pieces))
    terms = plane.scatter(lambda lo, hi: dot_cols(mixed_out[lo:hi], w_out), rows)
    mid, fnormed = mine.call(functools.partial(mid_kernel, cuts=cuts), terms, [tok], fgain, [F32, BF])

    cot_pieces[0] = after(cot_pieces[0], fnormed)
    cot_all = jnp.concatenate(cot_pieces, axis=0)
    fnormed = plane.gather(fnormed, [cot_all])
    pre_lin = dot(fnormed, w_ff)
    act, slope = gelu_pair(pre_lin[:, :ff_own])
    lin = pre_lin[:, ff_own:]
    fhidden = (act * lin).astype(BF)
    down_terms = dot_rows(fhidden, cot_all).astype(BF)
    hid_grad = dot_cols(after(cot_all, down_terms), w_down)
    fgrad = jnp.concatenate([(hid_grad * lin * slope).astype(BF), (hid_grad * act).astype(BF)], axis=1)
    down_sum = sum_z(down_terms)
    down_out = down_sum.astype(F32)
    terms = plane.terms(lambda lo, hi: dot_cols(fgrad[lo:hi], w_ff), rows)
    ff_terms = dot_rows(fnormed, after(fgrad, *terms)).astype(BF)
    terms = plane.add_up(terms)
    ff_sum = sum_z(after(ff_terms, down_sum))
    terms = (after(terms[0], down_sum, ff_terms), *terms[1:])
    mid_grad, mid_low, ffn_gain_part = mine.call(
        functools.partial(mid_back_kernel, cuts=cuts), terms, [mid, cot], fgain, [F32, BF, None]
    )
    later = after(fhidden, mid_grad)
    out_terms = plane.terms(lambda lo, hi: dot(later[lo:hi], w_down), rows)
    ffn_gain_part = jnp.sum(ffn_gain_part, axis=0)
    mid_low = plane.gather(mid_low, [*out_terms, ffn_gain_part, down_out])
    out_terms[3] = after(out_terms[3], mid_low)

    mixed_grad = dot(mid_low, w_out)
    act_r, slope_r = gelu_pair(branch)
    branch_grad = (mixed_grad * hidden * slope_r).astype(BF)
    back = Blocks(n_core, n_dp, seqs, True)
    out_first = plane.send_first(out_terms)
    adj, prod, front = back.call(
        functools.partial(reverse_kernel, own=own),
        [back.rows(span, own)] * 3,
        [back.rows(span, own)] * 2 + [back.sequence(8, own)],
        [row_f32] * 2 + [jax.ShapeDtypeStruct((lines * 8, own), F32)],
        [pltpu.VMEM((8, own), F32)],
        core_id, decay, mixed_grad, branch,
    )
    branch_late, mixed_late, *out_first = lax.optimization_barrier((branch_grad, mixed_out, *out_first, adj))[:6]
    both = pair(dot_rows(normed, branch_late).astype(BF), dot_rows(mid_low, mixed_late).astype(BF))
    both, ff_sum = lax.optimization_barrier((both, ff_sum))
    out_terms = plane.add_up(out_terms, out_first, [both])
    suffix, *out_terms = lax.optimization_barrier((carried(front, -1, [both]), *out_terms))

    def eight(x):
        return jnp.broadcast_to(x[:, None, :], (lines, 8, own)).reshape(lines * 8, own)

    igrad, tail, head, dgf, dgs, sums = back.call(
        functools.partial(backward_kernel, block=block, own=own),
        [f(back) for f in seq_in]
        + [
            back.rows(span, own), back.before(8, own, span), back.sequence(8, own), back.rows(span, own),
            back.rows(span, own), back.sequence(8, own),
        ],
        [
            back.rows(span, window), back.sequence(HALO, window), back.sequence(8, window), back.whole(block, window),
            back.whole(block, 2 * lanes), back.whole(8, window),
        ],
        [
            jax.ShapeDtypeStruct((total_rows, window), BF), jax.ShapeDtypeStruct((lines * HALO, window), F32),
            jax.ShapeDtypeStruct((lines * 8, window), F32), jax.ShapeDtypeStruct((block, window), F32),
            jax.ShapeDtypeStruct((block, 2 * lanes), F32), jax.ShapeDtypeStruct((8, window), F32),
        ],
        [
            pltpu.VMEM((span + HALO, window), F32), pltpu.VMEM((span + 8, own), F32), pltpu.VMEM((span + 8, window), F32),
        ],
        core_id, inner, inner, halo, keep, vec, gwf, gws, hidden, hidden, eight(start), adj, prod, eight(suffix),
    )

    coming = lax.ppermute(head.astype(BF), "z", [(i + 1, i) for i in range(n_z - 1)]).astype(F32).reshape(lines, 8, window)
    fix = jnp.zeros((lines, HALO, window), F32)
    for tap in range(1, taps):
        fix = fix.at[:, HALO - tap :, :].add(vec[tap] * coming[:, :tap])
    tail = (tail.reshape(lines, HALO, window) + fix).astype(BF).reshape(1, n_dp, seqs, HALO, window)
    igrad = lax.dynamic_update_slice(
        igrad.reshape(n_core, n_dp, seqs, span, window), tail, (1 - core, 0, 0, span - HALO, 0)
    ).reshape(total_rows, window)
    ff_part = exchange(ff_sum)
    both_sum = sum_z(after(both, ff_sum))
    igrad = after(igrad, both_sum)
    in_terms = dot_rows(normed, igrad).astype(BF)
    igrad, in_terms, ff_part = lax.optimization_barrier((igrad, in_terms, ff_part))
    terms = plane.terms(
        lambda lo, hi: dot_cols(igrad[lo:hi], w_in) + dot_cols(branch_grad[lo:hi], w_branch), rows
    )
    both_late, ff_part, mid_late = lax.optimization_barrier((both_sum, ff_part, mid, *terms))[:3]
    both_part = exchange(both_late)
    layer_out = mine.call(out_kernel, out_terms, [mid_late], None, [F32])[0]
    gate_out, up_out = pl.pallas_call(
        functools.partial(ff_unpack_kernel, cuts=(n_dp, n_z, n_core)),
        out_shape=[jax.ShapeDtypeStruct((drow, ff), F32)] * 2,
        compiler_params=pltpu.CompilerParams(vmem_limit_bytes=VMEM_BYTES),
    )(ff_part.reshape(group, drow, 2 * ff_own))
    terms = plane.add_up(terms)
    second = plane.second
    first_terms, layer_out, gate_out, up_out, both_part = lax.optimization_barrier(
        (terms[0], layer_out, gate_out, up_out, both_part)
    )
    terms = (first_terms, *terms[1:])
    both_part = both_part.reshape(group, drow, 2 * (block + part))

    def own_natural(x):
        full = jnp.swapaxes(x[:, :, :block], 0, 1).reshape(drow, group * block)
        rest = jnp.swapaxes(x[:, :, block : block + part], 0, 1).reshape(drow, group * part)
        return jnp.concatenate([full, rest], axis=1).astype(F32)

    branch_proj_grad = own_natural(unpair(both_part, 0))
    output_proj_grad = own_natural(unpair(both_part, 1)).T

    def place_window(x, axis_len):
        lead = x.shape[:-1]
        other = x[..., block:]
        turned = lax.dynamic_slice_in_dim(
            jnp.concatenate([other, other], -1), lax.rem(block - quarter * part, block), block, x.ndim - 1
        )
        y = jnp.zeros((*lead, axis_len), x.dtype)
        y = lax.dynamic_update_slice_in_dim(y, x[..., :block], me * block, x.ndim - 1)
        return lax.dynamic_update_slice_in_dim(y, turned, shared_at, x.ndim - 1)

    dg_full = jnp.stack([dgf[:, :block], dgf[:, block:]])
    dg_shared = jnp.stack([dgs[:, :part], dgs[:, lanes : lanes + part]])
    dg_shared = lax.dynamic_slice_in_dim(
        jnp.concatenate([dg_shared, dg_shared], 1), lax.rem(block - quarter * part, block), block, 1
    )
    lot = n_core * rrow
    lots = (block + 2 * lot - 2) // lot

    def by_z(x, row):
        y = jnp.swapaxes(x, 0, 1).reshape(block, -1).astype(BF)
        q = row // lot
        y = lax.dynamic_update_slice(jnp.zeros((n_z * lot, y.shape[1]), BF), y, (row - q * lot, 0))
        y = y.reshape(n_z, lot, -1)
        return lax.dynamic_slice_in_dim(jnp.concatenate([y, y]), lax.rem(n_z - lax.rem(q, n_z), n_z), n_z, 0)

    def to_lines(x, row):
        q = row // lot
        q = q + lax.rem(zi + n_z - lax.rem(q, n_z), n_z)
        y = jnp.zeros((n_dp, *x.shape), x.dtype)
        return lax.dynamic_update_slice(y, x[None], (jnp.minimum(q // n_z, n_dp - 1), 0, 0))

    assert lots <= n_z
    gates = jnp.concatenate([by_z(dg_full, me * block), by_z(dg_shared, shared_at)], axis=2)
    gates = gates.reshape(n_z, lot * 2 * (block + part) // window, window)
    joined = jnp.concatenate([in_terms.reshape(n_z, group * drow, window), gates], axis=1)
    joined = sum_z(after(joined.reshape(-1, window), both_sum))
    joined = after(joined, *second)
    input_grad, gain_part = mine.call(
        functools.partial(tok_back_kernel, cuts=cuts), terms, [tok, mid_grad], gain, [F32, None]
    )
    blocks_z = jnp.swapaxes(jnp.sum(gain_part, axis=0).reshape(n_dp, n_z, n_core * drow), 0, 1).reshape(n_z, group * drow)
    blocks_z = lax.dynamic_slice_in_dim(jnp.concatenate([blocks_z, blocks_z]), zi, n_z, 0)
    gain_sum = blocks_z[0]
    for k in range(1, n_z):
        gain_sum = gain_sum + lax.ppermute(blocks_z[k], "z", [(i, (i + k) % n_z) for i in range(n_z)])
    gain_high = gain_sum.astype(BF)
    gain_low = (gain_sum - gain_high.astype(F32)).astype(BF)
    gain_rows = jnp.concatenate([gain_high.reshape(group, drow), gain_low.reshape(group, drow)], axis=1)
    gain_rows = jnp.pad(gain_rows[:, None, :], ((0, 0), (0, 3), (0, window - 2 * drow)))
    in_part = joined[: group * drow].reshape(group, drow, window)
    gates = joined[group * drow :].reshape(lot, 2 * (block + part))
    gates = jnp.concatenate(
        [to_lines(gates[:, : 2 * block], me * block), to_lines(gates[:, 2 * block :], shared_at)], axis=2
    )
    gates = gates.reshape(group, rrow * 2 * (block + part) // window, window)
    gates_end = drow + gates.shape[1]
    joined = exchange(jnp.concatenate([in_part, gates, gain_rows], axis=1).reshape(-1, window))

    lane = jnp.arange(window)
    mine = lane < block + part
    sums = jnp.where(jnp.concatenate([jnp.ones((5, window), bool), jnp.broadcast_to(mine, (3, window))], axis=0), sums, 0.0)
    sums = place_window(sums, rec)
    sums = jnp.concatenate([sums[:7], sums[7:8] * (POWER * jax.nn.sigmoid(-lam))], axis=0)
    vectors = jnp.concatenate(
        [
            ffn_gain_part.reshape(devices, drow),
            jnp.swapaxes(sums.reshape(8, devices, rrow), 0, 1).reshape(devices, 8 * rrow),
        ],
        axis=1,
    )
    vec_len = vectors.shape[1]
    vectors = lax.all_to_all(vectors, EVERY, split_axis=0, concat_axis=0, tiled=True)
    joined = joined.reshape(group, -1, window)
    in_part = joined[:, :drow]
    gates = joined[:, drow:gates_end].reshape(group, rrow, 2 * (block + part)).astype(F32)
    gain_out = jnp.sum(joined[:, gates_end].astype(F32), axis=0)
    gain_out = gain_out[:drow] + gain_out[drow : 2 * drow]
    vectors = jnp.sum(vectors.reshape(devices, vec_len), axis=0)
    fgain_out = vectors[:drow]
    chan_out = vectors[drow:].reshape(8, rrow)

    gates_out = jnp.sum(gates[:, :, : 2 * block], axis=0).reshape(rrow, 2, block)
    rest = jnp.sum(gates[:, :, 2 * block :].reshape(shared, sharers, rrow, 2, part), axis=0)
    rest = jnp.transpose(rest, (1, 2, 0, 3)).reshape(rrow, 2, block)
    gates_out = jnp.swapaxes(gates_out + rest, 0, 1)

    full = jnp.swapaxes(in_part[:, :, :block], 0, 1).reshape(drow, group * block).astype(F32)
    turned = in_part[:, :, block:window].astype(F32).reshape(shared, sharers, drow, block)
    other = sum(jnp.roll(turned[:, q], part * q, axis=2) for q in range(sharers))
    input_proj_grad = jnp.concatenate([full, jnp.swapaxes(other, 0, 1).reshape(drow, shared * block)], axis=1)

    return (
        layer_out.reshape(seqs, span, width),
        input_grad.reshape(seqs, span, width),
        gain_out,
        input_proj_grad,
        branch_proj_grad,
        chan_out[:taps],
        chan_out[taps],
        gates_out,
        chan_out[taps + 1 : taps + 3],
        chan_out[taps + 3],
        output_proj_grad,
        fgain_out,
        gate_out,
        up_out,
        down_out,
    )


def solution(mesh):
    n_dp, n_seq = mesh.shape["dp"], mesh.shape["seq"]
    split = Mesh(mesh.devices.reshape(n_dp, n_seq // 2, 2), EVERY)
    seq = ("z", "core")
    line = P("dp", seq, None)
    first = P(EVERY)
    rows = P(EVERY, None)
    cols = P(None, EVERY)
    mids = P(None, EVERY, None)
    return jax.shard_map(
        body,
        mesh=split,
        in_specs=(
            line, P("dp", seq), line, first, rows, rows, cols, first, mids, cols, first, cols, first, rows, rows, rows,
        ),
        out_specs=(
            line, line, first, rows, rows, cols, first, mids, cols, first, cols, first, rows, rows, rows,
        ),
        check_vma=False,
    )
```

```python
import functools

import jax
import jax.numpy as jnp
from jax import lax
from jax.experimental import pallas as pl
from jax.experimental.pallas import tpu as pltpu
from jax.sharding import Mesh
from jax.sharding import PartitionSpec as P

EPSILON = 1e-06
POWER = 8.0
BF = jnp.bfloat16
F32 = jnp.float32
GROUP = ("dp", "core")
EVERY = ("dp", "z", "core")
GELU_A = 0.7978845608028654
GELU_B = 0.044715
HALO = 16
VMEM_BYTES = 48 * 1024 * 1024


def after(x, *others):
    return lax.optimization_barrier((x, *others))[0]


def gelu_pair(x):
    x2 = x * x
    th = jnp.tanh(GELU_A * (x + GELU_B * x2 * x))
    half = 0.5 * (1.0 + th)
    slope = half + 0.5 * x * (1.0 - th * th) * (GELU_A * (1.0 + 3.0 * GELU_B * x2))
    return x * half, slope


def gelu_only(x):
    return 0.5 * x * (1.0 + jnp.tanh(GELU_A * (x + GELU_B * x * x * x)))


def dot(a, b):
    return lax.dot_general(a, b, (((1,), (0,)), ((), ())), preferred_element_type=F32)


def dot_rows(a, b):
    return lax.dot_general(a, b, (((0,), (0,)), ((), ())), preferred_element_type=F32)


def dot_cols(a, b):
    return lax.dot_general(a, b, (((1,), (1,)), ((), ())), preferred_element_type=F32)


def minus_expm1(x):
    series = -x * (1.0 + x * (1 / 2) * (1.0 + x * (1 / 3) * (1.0 + x * (1 / 4) * (1.0 + x * (1 / 5) * (1.0 + x * (1 / 6))))))
    return jnp.where(x > -0.125, series, 1.0 - jnp.exp(x))


def conv_and_gates(inner_ref, prev, vec, gwf_ref, gws_ref, ext, block, own):
    rows = inner_ref.shape[0]
    ext[0:HALO, :] = prev.astype(F32)
    ext[HALO : HALO + rows, :] = inner_ref[...].astype(F32)
    conved = vec[4:5, :] + vec[0:1, :] * ext[HALO : HALO + rows, :]
    for tap in range(1, 4):
        conved = conved + vec[tap : tap + 1, :] * ext[HALO - tap : HALO - tap + rows, :]
    rounded = conved.astype(BF)
    gf = dot(rounded[:, :block], gwf_ref[...])
    gs = dot(rounded[:, block:], gws_ref[...])
    part = own - block
    rate_pre = jnp.concatenate([gf[:, :block], gs[:, :part]], axis=1) + vec[5:6, :own]
    open_pre = jnp.concatenate([gf[:, block:], gs[:, part:]], axis=1) + vec[6:7, :own]
    return conved, rounded, rate_pre, open_pre


def scan_groups(a_ref, b_ref, out_h, out_c, h, c, rows, width):
    place = lax.broadcasted_iota(jnp.int32, (8, width), 0)

    def one(g, carry):
        h, c = carry
        at = pl.ds(pl.multiple_of(g * 8, 8), 8)
        a, b = a_ref[at, :], b_ref[at, :]
        for shift in (1, 2, 4):
            keep = place >= shift
            pa = jnp.where(keep, pltpu.roll(a, shift, 0), 1.0)
            pb = jnp.where(keep, pltpu.roll(b, shift, 0), 0.0)
            b = a * pb + b
            a = a * pa
        b = b + a * h
        a = a * c
        out_h[at, :] = b
        out_c[at, :] = a
        return b[7:8, :], a[7:8, :]

    return lax.fori_loop(0, rows // 8, one, (h, c), unroll=8)


def forward_kernel(
    core_ref, inner_ref, prev_ref, halo_ref, keep_ref, vec_ref, gwf_ref, gws_ref,
    decay_ref, local_ref, cum_ref, last_ref, ext, b_ref, carry, *, block, own,
):
    c = pl.program_id(2)
    rows = inner_ref.shape[0]
    prev = jnp.where(c == 0, halo_ref[...].astype(F32), prev_ref[...].astype(F32))
    vec = vec_ref[...]
    conved, _, rate_pre, open_pre = conv_and_gates(inner_ref, prev, vec, gwf_ref, gws_ref, ext, block, own)
    keep = keep_ref[...]
    rate = jax.nn.sigmoid(rate_pre)
    opening = jax.nn.sigmoid(open_pre)
    log_decay = vec[7:8, :own] * rate
    scale = keep * jnp.sqrt(minus_expm1(2.0 * log_decay)) + (1.0 - keep)
    decay_ref[...] = jnp.exp(log_decay) * keep
    b_ref[...] = scale * opening * conved[:, :own]

    @pl.when(c == 0)
    def _():
        carry[0:1, :] = jnp.zeros((1, own), F32)
        carry[1:2, :] = jnp.ones((1, own), F32)

    h, p = scan_groups(decay_ref, b_ref, local_ref, cum_ref, carry[0:1, :], carry[1:2, :], rows, own)
    carry[0:1, :] = h
    carry[1:2, :] = p
    last_ref[...] = carry[...]


def reverse_kernel(core_ref, decay_ref, grad_ref, branch_ref, adj_ref, prod_ref, first_ref, carry, *, own):
    c = pl.program_id(2)
    rows = decay_ref.shape[0]
    place = lax.broadcasted_iota(jnp.int32, (8, own), 0)

    @pl.when(c == 0)
    def _():
        carry[0:1, :] = jnp.zeros((1, own), F32)
        carry[1:2, :] = jnp.ones((1, own), F32)

    def one(i, state):
        s, p = state
        at = pl.ds(pl.multiple_of((rows // 8 - 1 - i) * 8, 8), 8)
        a = decay_ref[at, :]
        hg = grad_ref[at, :] * gelu_only(branch_ref[at, :])
        b = a * hg
        for shift in (1, 2, 4):
            keep = place < 8 - shift
            na = jnp.where(keep, pltpu.roll(a, 8 - shift, 0), 1.0)
            nb = jnp.where(keep, pltpu.roll(b, 8 - shift, 0), 0.0)
            b = a * nb + b
            a = a * na
        b = b + a * s
        a = a * p
        last = place == 7
        adj_ref[at, :] = hg + jnp.where(last, s, pltpu.roll(b, 7, 0))
        prod_ref[at, :] = jnp.where(last, p, pltpu.roll(a, 7, 0))
        return b[0:1, :], a[0:1, :]

    s, p = lax.fori_loop(0, rows // 8, one, (carry[0:1, :], carry[1:2, :]), unroll=8)
    carry[0:1, :] = s
    carry[1:2, :] = p
    first_ref[...] = carry[...]


def backward_kernel(
    core_ref, inner_ref, prev_ref, halo_ref, keep_ref, vec_ref, gwf_ref, gws_ref, hidden_ref, before_ref, start_ref,
    adj_ref, prod_ref, suffix_ref,
    igrad_ref, tail_ref, head_ref, dgf_ref, dgs_ref, sums_ref, ext, hext, cext, *, block, own,
):
    c = pl.program_id(2)
    peers = pl.num_programs(2)
    first = (pl.program_id(0) == 0) & (pl.program_id(1) == 0) & (c == 0)
    at_start = c == peers - 1
    rows = inner_ref.shape[0]
    part = own - block
    window = vec_ref.shape[1]

    @pl.when(first)
    def _():
        dgf_ref[...] = jnp.zeros_like(dgf_ref)
        dgs_ref[...] = jnp.zeros_like(dgs_ref)
        sums_ref[...] = jnp.zeros_like(sums_ref)

    @pl.when(c == 0)
    def _():
        cext[rows : rows + 8, :] = jnp.zeros((8, window), F32)

    @pl.when(c > 0)
    def _():
        cext[rows : rows + 8, :] = cext[0:8, :]

    prev = jnp.where(at_start, halo_ref[...].astype(F32), prev_ref[...].astype(F32))
    vec = vec_ref[...]
    conved, rounded, rate_pre, open_pre = conv_and_gates(inner_ref, prev, vec, gwf_ref, gws_ref, ext, block, own)
    keep = keep_ref[...]
    conv = conved[:, :own]
    rate = jax.nn.sigmoid(rate_pre)
    opening = jax.nn.sigmoid(open_pre)
    factor = vec[7:8, :own]
    log_decay = factor * rate
    e = jnp.exp(log_decay)
    left = minus_expm1(2.0 * log_decay)
    scale = keep * jnp.sqrt(left) + (1.0 - keep)

    adj = adj_ref[...] + prod_ref[...] * suffix_ref[0:1, :]
    hext[0:8, :] = jnp.where(at_start, jnp.broadcast_to(start_ref[0:1, :], (8, own)), before_ref[...])
    hext[8 : 8 + rows, :] = hidden_ref[...]
    before = hext[7 : 7 + rows, :]
    d_log = keep * (adj * before * e - adj * opening * conv * (e * e) * lax.rsqrt(left))
    direct = adj * scale * opening
    g_rate = (d_log * factor * rate * (1.0 - rate)).astype(BF)
    g_open = (adj * scale * conv * opening * (1.0 - opening)).astype(BF)
    gf = jnp.concatenate([g_rate[:, :block], g_open[:, :block]], axis=1)
    gs = jnp.concatenate([g_rate[:, block:], g_open[:, block:]], axis=1)
    cgrad = jnp.concatenate([dot_cols(gf, gwf_ref[...]), dot_cols(gs, gws_ref[...])], axis=1)
    cgrad = cgrad + jnp.concatenate([direct, jnp.zeros((rows, window - own), F32)], axis=1)
    cext[0:rows, :] = cgrad
    dgf_ref[...] += dot_rows(rounded[:, :block], gf)
    dgs_ref[...] += dot_rows(rounded[:, block:], gs)

    igrad = vec[0:1, :] * cgrad
    for tap in range(1, 4):
        igrad = igrad + vec[tap : tap + 1, :] * cext[tap : tap + rows, :]
    igrad_ref[...] = igrad.astype(BF)

    @pl.when(c == 0)
    def _():
        tail_ref[...] = igrad[rows - HALO :, :]

    head_ref[...] = cgrad[0:8, :]

    def total(x):
        return jnp.sum(x, axis=0, keepdims=True)

    for tap in range(4):
        sums_ref[tap : tap + 1, :] += total(ext[HALO - tap : HALO - tap + rows, :] * cgrad)
    sums_ref[4:5, :] += total(cgrad)
    sums_ref[5:6, :own] += total(g_rate.astype(F32))
    sums_ref[6:7, :own] += total(g_open.astype(F32))
    sums_ref[7:8, :own] += total(d_log * rate)


def lane_blocks(n_dp, n_z):
    return [(d * n_z + z, z * n_dp + d) for d in range(n_dp) for z in range(n_z)]


def to_z(x, n_dp, n_z):
    w = x.shape[1] // (n_dp * n_z)
    pairs = sorted(lane_blocks(n_dp, n_z), key=lambda p: p[1])
    return jnp.concatenate([x[:, a * w : (a + 1) * w] for a, _ in pairs], axis=1)


def from_z(x, n_dp, n_z):
    w = x.shape[1] // (n_dp * n_z)
    return jnp.concatenate([x[:, b * w : (b + 1) * w] for _, b in lane_blocks(n_dp, n_z)], axis=1)


def total(pieces, i, steps):
    q, ax, a, bx, b = pieces
    low = i < steps // 2
    pick = lambda u, v: jnp.where(low, u[...].astype(F32), v[...].astype(F32))
    return q[...] + pick(ax, bx) + pick(a, b)


def inverse(x):
    return lax.rsqrt(jnp.mean(x * x, axis=1, keepdims=True) + EPSILON)


def norm_kernel(gain_ref, *refs, cuts):
    out_ref = refs[-1]
    for k, ref in enumerate(refs[:-1]):

        @pl.when(pl.program_id(0) == k)
        def _(ref=ref):
            x = ref[...].astype(F32)
            out_ref[...] = to_z(x * inverse(x) * gain_ref[...], *cuts).astype(BF)


def mid_kernel(q, ax, a, bx, b, tok_ref, gain_ref, mid_ref, normed_ref, *, cuts):
    i = pl.program_id(0)
    x = tok_ref[...].astype(F32) + from_z(total((q, ax, a, bx, b), i, pl.num_programs(0)), *cuts)
    mid_ref[...] = x
    normed_ref[...] = to_z(x * inverse(x) * gain_ref[...], *cuts).astype(BF)


def norm_back(grad, x, gain):
    inv = inverse(x)
    g = grad * gain
    return inv * g - x * (inv * inv * inv) * jnp.mean(x * g, axis=1, keepdims=True), grad * x * inv


def add_rows(ref, x):
    first = pl.program_id(0) == 0
    terms = jnp.sum(x.reshape(-1, 8, x.shape[1]), axis=0)

    @pl.when(first)
    def _():
        ref[...] = terms

    @pl.when(jnp.logical_not(first))
    def _():
        ref[...] += terms


def mid_back_kernel(q, ax, a, bx, b, mid_ref, cot_ref, gain_ref, grad_ref, low_ref, part_ref, *, cuts):
    i = pl.program_id(0)
    g = from_z(total((q, ax, a, bx, b), i, pl.num_programs(0)), *cuts)
    back, part = norm_back(g, mid_ref[...], gain_ref[...])
    grad = cot_ref[...].astype(F32) + back
    grad_ref[...] = grad
    low_ref[...] = to_z(grad, *cuts).astype(BF)
    add_rows(part_ref, part)


def tok_back_kernel(q, ax, a, bx, b, tok_ref, mid_grad_ref, gain_ref, grad_ref, part_ref, *, cuts):
    i = pl.program_id(0)
    g = from_z(total((q, ax, a, bx, b), i, pl.num_programs(0)), *cuts)
    back, part = norm_back(g, tok_ref[...].astype(F32), gain_ref[...])
    grad_ref[...] = mid_grad_ref[...] + back
    add_rows(part_ref, part)


def out_kernel(q, ax, a, bx, b, mid_ref, out_ref):
    out_ref[...] = mid_ref[...] + total((q, ax, a, bx, b), pl.program_id(0), pl.num_programs(0))


class OwnRows:
    def __init__(self, rows, width, steps=4):
        self.rows, self.width, self.steps = rows, width, steps

    def call(self, kernel, pieces, arrays, gain, outs):
        n, step = self.steps, self.rows // self.steps
        tile = pl.BlockSpec((step, self.width), lambda i: (i, 0))
        low = pl.BlockSpec((step, self.width), lambda i: (jnp.minimum(i, n // 2 - 1), 0))
        high = pl.BlockSpec((step, self.width), lambda i: (jnp.maximum(i - n // 2, 0), 0))
        line = pl.BlockSpec((1, self.width), lambda i: (0, 0))
        part = pl.BlockSpec((8, self.width), lambda i: (0, 0))
        shape = jax.ShapeDtypeStruct
        gains = [] if gain is None else [gain.reshape(1, self.width)]
        return pl.pallas_call(
            kernel,
            grid=(n,),
            in_specs=([tile, low, low, high, high] if pieces else []) + [tile] * len(arrays) + [line] * len(gains),
            out_specs=[part if t is None else tile for t in outs],
            out_shape=[
                shape((8, self.width), F32) if t is None else shape((self.rows, self.width), t) for t in outs
            ],
            compiler_params=pltpu.CompilerParams(vmem_limit_bytes=VMEM_BYTES),
        )(*pieces, *arrays, *gains)


def pair_pack_kernel(a_ref, b_ref, out_ref, *, block, part):
    group = out_ref.shape[0]
    for n in range(group):
        at = group * block + n * part
        out_ref[n, :, :block] = a_ref[:, n * block : (n + 1) * block]
        out_ref[n, :, block : 2 * block] = b_ref[:, n * block : (n + 1) * block]
        parts = [ref[:, at : at + part].astype(F32) for ref in (a_ref, b_ref)]
        out_ref[n, :, 2 * block :] = jnp.concatenate(parts, axis=1).astype(BF)


def ff_pack_kernel(gate_ref, up_ref, out_ref, *, cuts):
    n_dp, n_z, n_core = cuts
    w = gate_ref.shape[1] // (n_dp * n_z * n_core)
    for d in range(n_dp):
        for c in range(n_core):
            for j, ref in enumerate((gate_ref, up_ref)):
                cols = [((d * n_z + z) * n_core + c) * w for z in range(n_z)]
                x = jnp.concatenate([ref[:, o : o + w].astype(F32) for o in cols], axis=1)
                out_ref[d * n_core + c, :, j * n_z * w : (j + 1) * n_z * w] = x.astype(BF)


def ff_unpack_kernel(x_ref, gate_ref, up_ref, *, cuts):
    n_dp, n_z, n_core = cuts
    w = gate_ref.shape[1] // (n_dp * n_z * n_core)
    for j, ref in enumerate((gate_ref, up_ref)):
        for d in range(n_dp):
            cols = []
            for z in range(n_z):
                for c in range(n_core):
                    o = (j * n_z + z) * w
                    cols.append(x_ref[d * n_core + c, :, o : o + w].astype(F32))
            span = n_z * n_core * w
            ref[:, d * span : (d + 1) * span] = jnp.concatenate(cols, axis=1)


class Blocks:
    def __init__(self, peers, lines, seqs, back):
        self.peers, self.lines, self.seqs, self.back = peers, lines, seqs, back

    def core(self, c):
        return self.peers - 1 - c if self.back else c

    def block(self, d, s, c, core):
        return (jnp.bitwise_xor(c, core[0]) * self.lines + d) * self.seqs + s

    def rows(self, count, width):
        return pl.BlockSpec((count, width), lambda d, s, c, core: (self.block(d, s, self.core(c), core), 0))

    def before(self, count, width, length):
        each = length // count

        def index(d, s, c, core):
            return (self.block(d, s, jnp.maximum(self.core(c) - 1, 0), core) * each + each - 1, 0)

        return pl.BlockSpec((count, width), index)

    def sequence(self, count, width):
        return pl.BlockSpec((count, width), lambda d, s, c, core: (d * self.seqs + s, 0))

    def whole(self, *shape):
        return pl.BlockSpec(shape, lambda d, s, c, core: (0,) * len(shape))

    def call(self, kernel, in_specs, out_specs, out_shape, scratch, *args):
        return pl.pallas_call(
            kernel,
            grid_spec=pltpu.PrefetchScalarGridSpec(
                num_scalar_prefetch=1,
                grid=(self.lines, self.seqs, self.peers),
                in_specs=in_specs,
                out_specs=out_specs,
                scratch_shapes=scratch,
            ),
            out_shape=out_shape,
            compiler_params=pltpu.CompilerParams(vmem_limit_bytes=VMEM_BYTES),
        )(*args)


class Plane:
    def __init__(self, n_dp, n_core):
        self.n_dp, self.n_core = n_dp, n_core
        self.core = lax.axis_index("core")
        self.dp = lax.axis_index("dp")

    def near(self, x, k):
        return lax.ppermute(x, "dp", [(i, i ^ k) for i in range(self.n_dp)])

    def twin(self, x):
        return lax.ppermute(x, "core", [(0, 1), (1, 0)])

    def pieces(self, x, late=()):
        half = x.shape[0] // 2
        x1, x2 = self.near(x, 1), self.near(x, 2)
        if late:
            x1, x2 = lax.optimization_barrier((x1, x2, *late))[:2]
        x3 = jnp.concatenate([self.near(x2[:half], 1), self.near(x1[half:], 2)], axis=0)
        mine = [x, x1, x2, x3]
        return mine + [self.twin(m) for m in mine]

    def gather(self, x, late=()):
        return jnp.concatenate(self.pieces(x, late), axis=0)

    def terms(self, product, rows):
        n = self.n_dp
        halves = ((n // 2, n), (0, n // 2))
        other = [self.twin(product((n + lo) * rows, (n + hi) * rows).astype(BF)) for lo, hi in halves]
        far, near = (product(lo * rows, hi * rows) + x.astype(F32) for (lo, hi), x in zip(halves, other))
        far = far.astype(BF)
        return [x[k * rows : (k + 1) * rows] for x in (near, far) for k in range(n // 2)]

    def send_first(self, q):
        half = q[0].shape[0] // 2
        low = lambda x: x.astype(BF)
        a3, b3 = self.near(q[3][:half], 1), self.near(q[3][half:], 2)
        a1, b2 = self.near(low(q[1][:half]), 1), self.near(q[2][half:], 2)
        return a3, b3, a1, b2

    def add_up(self, q, first=None, late=()):
        half = q[0].shape[0] // 2
        low = lambda x: x.astype(BF)
        a3, b3, a1, b2 = first or self.send_first(q)
        q2, q1 = (after(q[2], *late), after(q[1], *late)) if late else (q[2], q[1])
        self.second = (low(q2[:half].astype(F32) + a3.astype(F32)), low(q1[half:] + b3.astype(F32)))
        a, b = self.near(self.second[0], 2), self.near(self.second[1], 1)
        return q[0], a1, a, b2, b

    def scatter(self, product, rows):
        return self.add_up(self.terms(product, rows))

    def in_order(self, x):
        x = jnp.where(self.core == 1, x[::-1], x)
        for bit in (1, 2):
            y = x.reshape(2, self.n_dp // (2 * bit), 2, bit, *x.shape[2:])
            x = jnp.where((self.dp & bit) != 0, y[:, :, ::-1], y).reshape(x.shape)
        return jnp.swapaxes(x, 0, 1)


def body(
    tokens, doc_reset, cotangent, norm_gain, input_proj, branch_proj, conv_kernel, conv_bias, gate_weight, gate_bias,
    decay_param, output_proj, ffn_gain, ffn_gate, ffn_up, ffn_down,
):
    seqs, span, width = tokens.shape
    rows = seqs * span
    n_dp, n_z, n_core = (lax.axis_size(a) for a in EVERY)
    group = n_dp * n_core
    devices = group * n_z
    zi = lax.axis_index("z")
    me = lax.axis_index("dp") * n_core + lax.axis_index("core")
    rec = input_proj.shape[1]
    ff = ffn_gate.shape[1]
    block = gate_weight.shape[2]
    taps = conv_kernel.shape[0]
    drow = input_proj.shape[0]
    frow = ffn_down.shape[0]
    ff_own = ff // group
    blocks = rec // block
    shared = blocks - group
    sharers = group // shared
    part = block // sharers
    lanes = 128 * (-(-part // 128))
    own = block + lanes
    window = 2 * block
    total_rows = group * rows
    lines = n_dp * seqs

    plane = Plane(n_dp, n_core)
    core = plane.core
    core_id = core.astype(jnp.int32).reshape(1)

    def window_columns(w):
        lead = w.shape[0]
        full = w[:, : group * block].reshape(lead, group, block)
        rest = w[:, group * block :].reshape(lead, shared, block)
        turned = jnp.stack([jnp.roll(rest, -part * q, axis=2) for q in range(sharers)], axis=2)
        return jnp.concatenate([full, turned.reshape(lead, group, block)], axis=2)

    def exchange(x):
        return lax.all_to_all(x, GROUP, split_axis=0, concat_axis=0, tiled=True)

    def to_members(x):
        y = jnp.swapaxes(x, 0, 1)
        return exchange(y.reshape(group * x.shape[0], x.shape[2]))

    def sum_z(x):
        return lax.psum_scatter(x, "z", scatter_dimension=0, tiled=True)

    def over_z(x):
        return lax.all_gather(x, "z", axis=0, tiled=True)

    cuts = (n_dp, n_z)
    cot = cotangent.reshape(rows, width)
    tok = tokens.reshape(rows, width)
    tok_pieces = plane.pieces(tok)
    rrow = rec // devices
    vectors = jnp.concatenate(
        [norm_gain, ffn_gain, conv_kernel.reshape(-1), conv_bias, gate_bias.reshape(-1), decay_param]
    )
    small_len = vectors.shape[0]
    vectors = jnp.pad(vectors, (0, -small_len % 256)).reshape(-1, 256)
    gates_rows = 2 * rrow * block // 256
    marks_at = gates_rows + vectors.shape[0]
    marks = (1 - doc_reset).astype(BF).reshape(-1, 256)
    small = jnp.concatenate([gate_weight.reshape(gates_rows, 256), vectors, marks], axis=0)
    small = jnp.pad(small, ((0, -small.shape[0] % 32), (0, 0)))
    packed = small.shape[0]
    sent_in = to_members(window_columns(input_proj))
    small = over_z(after(small, sent_in))

    def pair(a, b):
        cut = block + part
        return jnp.concatenate([a[..., :block], b[..., :block], a[..., block:cut], b[..., block:cut]], axis=-1)

    def unpair(x, k):
        at = 2 * block + k * part
        return jnp.concatenate([x[..., k * block : (k + 1) * block], x[..., at : at + part]], axis=-1)

    both = pl.pallas_call(
        functools.partial(pair_pack_kernel, block=block, part=part),
        out_shape=jax.ShapeDtypeStruct((group, drow, 2 * (block + part)), BF),
        compiler_params=pltpu.CompilerParams(vmem_limit_bytes=VMEM_BYTES),
    )(branch_proj, output_proj.T)
    sent_both = exchange(after(both, small).reshape(group * drow, 2 * (block + part)))
    ff_packed = pl.pallas_call(
        functools.partial(ff_pack_kernel, cuts=(n_dp, n_z, n_core)),
        out_shape=jax.ShapeDtypeStruct((group, drow, 2 * ff_own), BF),
        compiler_params=pltpu.CompilerParams(vmem_limit_bytes=VMEM_BYTES),
    )(ffn_gate, ffn_up)
    w_in = over_z(sent_in)
    w_both = over_z(sent_both)
    w_branch, w_out = (jnp.pad(unpair(w_both, k), ((0, 0), (0, lanes - part))) for k in range(2))
    small = plane.gather(small, [sent_both]).reshape(n_core, n_dp, n_z, packed, 256)
    keep = lax.dynamic_index_in_dim(small, zi, 2, False)[:, :, marks_at : marks_at + rows // 256]
    keep = keep.astype(F32).reshape(total_rows, 1)
    ff_packed, small = lax.optimization_barrier((ff_packed, small))
    sent_ff = exchange(ff_packed.reshape(group * drow, 2 * ff_own))
    rest = small[:, :, :, gates_rows:marks_at]
    rest = jnp.swapaxes(plane.in_order(rest), 1, 2).reshape(devices, -1)[:, :small_len].astype(F32)
    gain = rest[:, :drow].reshape(width)
    fgain = rest[:, drow : 2 * drow].reshape(width)
    chan = rest[:, 2 * drow :].reshape(devices, taps + 4, rrow)
    chan = jnp.swapaxes(chan, 0, 1).reshape(taps + 4, rec)
    lam = chan[taps + 3 :]
    chan = jnp.concatenate([chan[: taps + 3], -POWER * jax.nn.softplus(-lam)], axis=0)

    quarter = me % sharers
    shared_at = (group + me // sharers) * block

    def my_window(x, axis):
        full = lax.dynamic_slice_in_dim(x, me * block, block, axis)
        other = lax.dynamic_slice_in_dim(x, shared_at, block, axis)
        turned = lax.dynamic_slice_in_dim(jnp.concatenate([other, other], axis), quarter * part, block, axis)
        return full, turned

    vec = jnp.concatenate(my_window(chan, 1), axis=1)
    mine = OwnRows(rows, width)
    normed = pl.pallas_call(
        functools.partial(norm_kernel, cuts=cuts),
        grid=(group,),
        in_specs=[pl.BlockSpec((1, width), lambda i: (0, 0))] + [pl.BlockSpec((rows, width), lambda i: (0, 0))] * group,
        out_specs=pl.BlockSpec((rows, width), lambda i: (i, 0)),
        out_shape=jax.ShapeDtypeStruct((total_rows, width), BF),
        compiler_params=pltpu.CompilerParams(vmem_limit_bytes=VMEM_BYTES),
    )(gain.reshape(1, width), *tok_pieces)

    normed, small = lax.optimization_barrier((normed, small))
    gates_all = small[:, :, :, :gates_rows].reshape(n_core, n_dp, n_z, 2, rrow * block // 256, 256)
    gates_all = jnp.transpose(plane.in_order(gates_all), (3, 0, 2, 1, 4, 5)).reshape(2, rec, block)
    gw_full, gw_shared = my_window(gates_all, 1)
    gw_shared = lax.dynamic_slice_in_dim(gw_shared, quarter * part, part, 2)
    gw_shared = jnp.pad(gw_shared, ((0, 0), (0, 0), (0, lanes - part)))
    gwf = jnp.concatenate([gw_full[0], gw_full[1]], axis=1)
    gws = jnp.concatenate([gw_shared[0], gw_shared[1]], axis=1)

    inner = dot(normed, w_in).astype(BF)
    cot_here, inner, sent_ff = lax.optimization_barrier((cot, inner, sent_ff))
    w_ff = over_z(sent_ff)
    w_down = over_z(after(ffn_down, sent_ff))
    branch = dot(normed, w_branch)
    ends = inner.reshape(n_core, n_dp, seqs, span, window)[:, :, :, span - HALO :]
    ends = jnp.where(core == 1, ends[0], ends[1]).reshape(lines * HALO, window)
    halo = lax.ppermute(ends, "z", [(i, i + 1) for i in range(n_z - 1)])

    at = Blocks(n_core, n_dp, seqs, False)
    seq_in = [
        lambda b: b.rows(span, window), lambda b: b.before(HALO, window, span), lambda b: b.sequence(HALO, window),
        lambda b: b.rows(span, 1), lambda b: b.whole(8, window), lambda b: b.whole(block, window),
        lambda b: b.whole(block, 2 * lanes),
    ]
    row_f32 = jax.ShapeDtypeStruct((total_rows, own), F32)
    decay, local, cum, last = at.call(
        functools.partial(forward_kernel, block=block, own=own),
        [f(at) for f in seq_in],
        [at.rows(span, own)] * 3 + [at.sequence(8, own)],
        [row_f32] * 3 + [jax.ShapeDtypeStruct((lines * 8, own), F32)],
        [pltpu.VMEM((span + HALO, window), F32), pltpu.VMEM((span, own), F32), pltpu.VMEM((8, own), F32)],
        core_id, inner, inner, halo, keep, vec, gwf, gws,
    )

    cot_pieces = plane.pieces(cot_here, [last])

    def carried(x, way, beside):
        x = x.reshape(lines, 8, own)[:, :2]
        state = jnp.zeros((lines, own), F32)
        for k in range(n_z - 1, 0, -1):
            hops = [(i, i + way * k) for i in range(n_z) if 0 <= i + way * k < n_z]
            come = after(lax.ppermute(x, "z", hops), *beside)
            state = come[:, 1] * state + come[:, 0]
        return state

    start = carried(last, 1, [branch])

    def by_line(x):
        return x.reshape(1, n_dp, seqs, 1, own)

    def spread(x):
        return x.reshape(n_core, n_dp, seqs, span, own)

    hidden = (spread(local) + spread(cum) * by_line(start)).reshape(total_rows, own)
    mixed_out = (hidden * gelu_only(branch)).astype(BF)
    mixed_out, *cot_pieces = lax.optimization_barrier((mixed_out, *cot_pieces))
    terms = plane.scatter(lambda lo, hi: dot_cols(mixed_out[lo:hi], w_out), rows)
    mid, fnormed = mine.call(functools.partial(mid_kernel, cuts=cuts), terms, [tok], fgain, [F32, BF])

    cot_pieces[0] = after(cot_pieces[0], fnormed)
    cot_all = jnp.concatenate(cot_pieces, axis=0)
    fnormed = plane.gather(fnormed, [cot_all])
    pre_lin = dot(fnormed, w_ff)
    act, slope = gelu_pair(pre_lin[:, :ff_own])
    lin = pre_lin[:, ff_own:]
    fhidden = (act * lin).astype(BF)
    down_terms = dot_rows(fhidden, cot_all).astype(BF)
    hid_grad = dot_cols(after(cot_all, down_terms), w_down)
    fgrad = jnp.concatenate([(hid_grad * lin * slope).astype(BF), (hid_grad * act).astype(BF)], axis=1)
    down_sum = sum_z(down_terms)
    down_out = down_sum.astype(F32)
    terms = plane.terms(lambda lo, hi: dot_cols(fgrad[lo:hi], w_ff), rows)
    ff_terms = dot_rows(fnormed, after(fgrad, down_sum, *terms)).astype(BF)
    terms = plane.add_up(terms)
    ff_sum = sum_z(after(ff_terms, down_sum))
    terms = (after(terms[0], down_sum, ff_terms), *terms[1:])
    mid_grad, mid_low, ffn_gain_part = mine.call(
        functools.partial(mid_back_kernel, cuts=cuts), terms, [mid, cot], fgain, [F32, BF, None]
    )
    later = after(fhidden, mid_grad)
    out_terms = plane.terms(lambda lo, hi: dot(later[lo:hi], w_down), rows)
    ffn_gain_part = jnp.sum(ffn_gain_part, axis=0)
    mid_low = plane.gather(mid_low, [*out_terms, ffn_gain_part, down_out])
    out_terms[3] = after(out_terms[3], mid_low)

    mixed_grad = dot(mid_low, w_out)
    act_r, slope_r = gelu_pair(branch)
    branch_grad = (mixed_grad * hidden * slope_r).astype(BF)
    back = Blocks(n_core, n_dp, seqs, True)
    out_first = plane.send_first(out_terms)
    adj, prod, front = back.call(
        functools.partial(reverse_kernel, own=own),
        [back.rows(span, own)] * 3,
        [back.rows(span, own)] * 2 + [back.sequence(8, own)],
        [row_f32] * 2 + [jax.ShapeDtypeStruct((lines * 8, own), F32)],
        [pltpu.VMEM((8, own), F32)],
        core_id, decay, mixed_grad, branch,
    )
    branch_late, mixed_late, *out_first = lax.optimization_barrier((branch_grad, mixed_out, *out_first, adj))[:6]
    both = pair(dot_rows(normed, branch_late).astype(BF), dot_rows(mid_low, mixed_late).astype(BF))
    both, ff_sum = lax.optimization_barrier((both, ff_sum))
    out_terms = plane.add_up(out_terms, out_first, [both])
    suffix, *out_terms = lax.optimization_barrier((carried(front, -1, [both]), *out_terms))

    def eight(x):
        return jnp.broadcast_to(x[:, None, :], (lines, 8, own)).reshape(lines * 8, own)

    igrad, tail, head, dgf, dgs, sums = back.call(
        functools.partial(backward_kernel, block=block, own=own),
        [f(back) for f in seq_in]
        + [
            back.rows(span, own), back.before(8, own, span), back.sequence(8, own), back.rows(span, own),
            back.rows(span, own), back.sequence(8, own),
        ],
        [
            back.rows(span, window), back.sequence(HALO, window), back.sequence(8, window), back.whole(block, window),
            back.whole(block, 2 * lanes), back.whole(8, window),
        ],
        [
            jax.ShapeDtypeStruct((total_rows, window), BF), jax.ShapeDtypeStruct((lines * HALO, window), F32),
            jax.ShapeDtypeStruct((lines * 8, window), F32), jax.ShapeDtypeStruct((block, window), F32),
            jax.ShapeDtypeStruct((block, 2 * lanes), F32), jax.ShapeDtypeStruct((8, window), F32),
        ],
        [
            pltpu.VMEM((span + HALO, window), F32), pltpu.VMEM((span + 8, own), F32), pltpu.VMEM((span + 8, window), F32),
        ],
        core_id, inner, inner, halo, keep, vec, gwf, gws, hidden, hidden, eight(start), adj, prod, eight(suffix),
    )

    coming = lax.ppermute(head.astype(BF), "z", [(i + 1, i) for i in range(n_z - 1)]).astype(F32).reshape(lines, 8, window)
    fix = jnp.zeros((lines, HALO, window), F32)
    for tap in range(1, taps):
        fix = fix.at[:, HALO - tap :, :].add(vec[tap] * coming[:, :tap])
    tail = (tail.reshape(lines, HALO, window) + fix).astype(BF).reshape(1, n_dp, seqs, HALO, window)
    igrad = lax.dynamic_update_slice(
        igrad.reshape(n_core, n_dp, seqs, span, window), tail, (1 - core, 0, 0, span - HALO, 0)
    ).reshape(total_rows, window)
    ff_part = exchange(ff_sum)
    both_sum = sum_z(after(both, ff_sum))
    igrad = after(igrad, both_sum)
    in_terms = dot_rows(normed, igrad).astype(BF)
    igrad, in_terms, ff_part = lax.optimization_barrier((igrad, in_terms, ff_part))
    terms = plane.terms(
        lambda lo, hi: dot_cols(igrad[lo:hi], w_in) + dot_cols(branch_grad[lo:hi], w_branch), rows
    )
    both_late, ff_part, mid_late = lax.optimization_barrier((both_sum, ff_part, mid, *terms))[:3]
    both_part = exchange(both_late)
    layer_out = mine.call(out_kernel, out_terms, [mid_late], None, [F32])[0]
    gate_out, up_out = pl.pallas_call(
        functools.partial(ff_unpack_kernel, cuts=(n_dp, n_z, n_core)),
        out_shape=[jax.ShapeDtypeStruct((drow, ff), F32)] * 2,
        compiler_params=pltpu.CompilerParams(vmem_limit_bytes=VMEM_BYTES),
    )(ff_part.reshape(group, drow, 2 * ff_own))
    terms = plane.add_up(terms)
    second = plane.second
    first_terms, layer_out, gate_out, up_out, both_part = lax.optimization_barrier(
        (terms[0], layer_out, gate_out, up_out, both_part)
    )
    terms = (first_terms, *terms[1:])
    both_part = both_part.reshape(group, drow, 2 * (block + part))

    def own_natural(x):
        full = jnp.swapaxes(x[:, :, :block], 0, 1).reshape(drow, group * block)
        rest = jnp.swapaxes(x[:, :, block : block + part], 0, 1).reshape(drow, group * part)
        return jnp.concatenate([full, rest], axis=1).astype(F32)

    branch_proj_grad = own_natural(unpair(both_part, 0))
    output_proj_grad = own_natural(unpair(both_part, 1)).T

    def place_window(x, axis_len):
        lead = x.shape[:-1]
        other = x[..., block:]
        turned = lax.dynamic_slice_in_dim(
            jnp.concatenate([other, other], -1), lax.rem(block - quarter * part, block), block, x.ndim - 1
        )
        y = jnp.zeros((*lead, axis_len), x.dtype)
        y = lax.dynamic_update_slice_in_dim(y, x[..., :block], me * block, x.ndim - 1)
        return lax.dynamic_update_slice_in_dim(y, turned, shared_at, x.ndim - 1)

    dg_full = jnp.stack([dgf[:, :block], dgf[:, block:]])
    dg_shared = jnp.stack([dgs[:, :part], dgs[:, lanes : lanes + part]])
    dg_shared = lax.dynamic_slice_in_dim(
        jnp.concatenate([dg_shared, dg_shared], 1), lax.rem(block - quarter * part, block), block, 1
    )
    lot = n_core * rrow
    lots = (block + 2 * lot - 2) // lot

    def by_z(x, row):
        y = jnp.swapaxes(x, 0, 1).reshape(block, -1).astype(BF)
        q = row // lot
        y = lax.dynamic_update_slice(jnp.zeros((n_z * lot, y.shape[1]), BF), y, (row - q * lot, 0))
        y = y.reshape(n_z, lot, -1)
        return lax.dynamic_slice_in_dim(jnp.concatenate([y, y]), lax.rem(n_z - lax.rem(q, n_z), n_z), n_z, 0)

    def to_lines(x, row):
        q = row // lot
        q = q + lax.rem(zi + n_z - lax.rem(q, n_z), n_z)
        y = jnp.zeros((n_dp, *x.shape), x.dtype)
        return lax.dynamic_update_slice(y, x[None], (jnp.minimum(q // n_z, n_dp - 1), 0, 0))

    assert lots <= n_z
    gates = jnp.concatenate([by_z(dg_full, me * block), by_z(dg_shared, shared_at)], axis=2)
    gates = gates.reshape(n_z, lot * 2 * (block + part) // window, window)
    joined = jnp.concatenate([in_terms.reshape(n_z, group * drow, window), gates], axis=1)
    joined = sum_z(after(joined.reshape(-1, window), both_sum))
    joined = after(joined, *second)
    input_grad, gain_part = mine.call(
        functools.partial(tok_back_kernel, cuts=cuts), terms, [tok, mid_grad], gain, [F32, None]
    )
    blocks_z = jnp.swapaxes(jnp.sum(gain_part, axis=0).reshape(n_dp, n_z, n_core * drow), 0, 1).reshape(n_z, group * drow)
    blocks_z = lax.dynamic_slice_in_dim(jnp.concatenate([blocks_z, blocks_z]), zi, n_z, 0)
    gain_sum = blocks_z[0]
    for k in range(1, n_z):
        gain_sum = gain_sum + lax.ppermute(blocks_z[k], "z", [(i, (i + k) % n_z) for i in range(n_z)])
    gain_high = gain_sum.astype(BF)
    gain_low = (gain_sum - gain_high.astype(F32)).astype(BF)
    gain_rows = jnp.concatenate([gain_high.reshape(group, drow), gain_low.reshape(group, drow)], axis=1)
    gain_rows = jnp.pad(gain_rows[:, None, :], ((0, 0), (0, 3), (0, window - 2 * drow)))
    in_part = joined[: group * drow].reshape(group, drow, window)
    gates = joined[group * drow :].reshape(lot, 2 * (block + part))
    gates = jnp.concatenate(
        [to_lines(gates[:, : 2 * block], me * block), to_lines(gates[:, 2 * block :], shared_at)], axis=2
    )
    gates = gates.reshape(group, rrow * 2 * (block + part) // window, window)
    gates_end = drow + gates.shape[1]
    joined = exchange(jnp.concatenate([in_part, gates, gain_rows], axis=1).reshape(-1, window))

    lane = jnp.arange(window)
    mine = lane < block + part
    sums = jnp.where(jnp.concatenate([jnp.ones((5, window), bool), jnp.broadcast_to(mine, (3, window))], axis=0), sums, 0.0)
    sums = place_window(sums, rec)
    sums = jnp.concatenate([sums[:7], sums[7:8] * (POWER * jax.nn.sigmoid(-lam))], axis=0)
    vectors = jnp.concatenate(
        [
            ffn_gain_part.reshape(devices, drow),
            jnp.swapaxes(sums.reshape(8, devices, rrow), 0, 1).reshape(devices, 8 * rrow),
        ],
        axis=1,
    )
    vec_len = vectors.shape[1]
    vectors = lax.all_to_all(vectors, EVERY, split_axis=0, concat_axis=0, tiled=True)
    joined = joined.reshape(group, -1, window)
    in_part = joined[:, :drow]
    gates = joined[:, drow:gates_end].reshape(group, rrow, 2 * (block + part)).astype(F32)
    gain_out = jnp.sum(joined[:, gates_end].astype(F32), axis=0)
    gain_out = gain_out[:drow] + gain_out[drow : 2 * drow]
    vectors = jnp.sum(vectors.reshape(devices, vec_len), axis=0)
    fgain_out = vectors[:drow]
    chan_out = vectors[drow:].reshape(8, rrow)

    gates_out = jnp.sum(gates[:, :, : 2 * block], axis=0).reshape(rrow, 2, block)
    rest = jnp.sum(gates[:, :, 2 * block :].reshape(shared, sharers, rrow, 2, part), axis=0)
    rest = jnp.transpose(rest, (1, 2, 0, 3)).reshape(rrow, 2, block)
    gates_out = jnp.swapaxes(gates_out + rest, 0, 1)

    full = jnp.swapaxes(in_part[:, :, :block], 0, 1).reshape(drow, group * block).astype(F32)
    turned = in_part[:, :, block:window].astype(F32).reshape(shared, sharers, drow, block)
    other = sum(jnp.roll(turned[:, q], part * q, axis=2) for q in range(sharers))
    input_proj_grad = jnp.concatenate([full, jnp.swapaxes(other, 0, 1).reshape(drow, shared * block)], axis=1)

    return (
        layer_out.reshape(seqs, span, width),
        input_grad.reshape(seqs, span, width),
        gain_out,
        input_proj_grad,
        branch_proj_grad,
        chan_out[:taps],
        chan_out[taps],
        gates_out,
        chan_out[taps + 1 : taps + 3],
        chan_out[taps + 3],
        output_proj_grad,
        fgain_out,
        gate_out,
        up_out,
        down_out,
    )


def solution(mesh):
    n_dp, n_seq = mesh.shape["dp"], mesh.shape["seq"]
    split = Mesh(mesh.devices.reshape(n_dp, n_seq // 2, 2), EVERY)
    seq = ("z", "core")
    line = P("dp", seq, None)
    first = P(EVERY)
    rows = P(EVERY, None)
    cols = P(None, EVERY)
    mids = P(None, EVERY, None)
    return jax.shard_map(
        body,
        mesh=split,
        in_specs=(
            line, P("dp", seq), line, first, rows, rows, cols, first, mids, cols, first, cols, first, rows, rows, rows,
        ),
        out_specs=(
            line, line, first, rows, rows, cols, first, mids, cols, first, cols, first, rows, rows, rows,
        ),
        check_vma=False,
    )
```
